256 devices in a mesh: grp: 4 (over z_lo, core), slab: 64 (over z_hi, x, y).
Axes of the slice: x: 4, y: 4, z: 8 (z_hi: 4, z_lo: 2; z = z_hi * 2 + z_lo), core: 2. Of those that a mesh axis runs over, the one named last changes fastest.
Arguments:
- tangent: bfloat16 [4, 2, 2048, 8192], P('grp', None, 'slab'), may hold values from -6 to 6
- base: bfloat16 [2, 2048, 8192], P(None, 'slab', 'grp'), may hold values from -6 to 6
- theta: bfloat16 [2048, 8192], P('slab'), may hold values from -3.140625 to 3.140625
- eof_table: float32 [112, 2048], P(None, 'slab'), may hold values from -4 to 4
- mode_of_field: int32 [4], P('grp'), may hold values from 0 to 111
- block_factors: bfloat16 [16, 2, 128, 128], P(None, None, 'slab'), may hold values from -2 to 2, as said below
Outputs:
- tangent_next: bfloat16 [4, 2, 2048, 8192], P('grp', None, None, 'slab')
- base_next: bfloat16 [2, 2048, 8192], P(None, None, 'slab')
The draws below stay inside these ranges and needn't reach their ends.
Inputs may be any that keep to these rules, and one draw needn't show every extreme that they name: `mode_of_field`: each field names one of the 112 modes of the table; several fields may name the same mode. `block_factors`: in every block the complex entries G_k[127, 0] and G_k[0, 127] have magnitude between 1.94 and 2.21.
All inputs are finite; a program needn't handle non-finite values.
Results may differ from the reference program's by a relative error of at most 0.0093.
Values may be sent and summed in bfloat16 or wider, within the bound.
A program may use at most 64 MiB of HBM per device.

```python
import math
import jax
import jax.numpy as jnp
from jax import lax

NZ = 2048
NY = 8192
EOFS = 112
R2 = 128
R1 = 64
BLK = 128
NBLK = 16
MODES = 4


def draw_block_factors(key, part):
    key = jax.random.fold_in(key, 7)
    noise_key, diagonal_key, twist_key, radius_key, wobble_key, quadrant_key = jax.random.split(key, 6)
    noise = jax.random.truncated_normal(noise_key, -4.0, 4.0, (NBLK, 2, BLK, BLK), jnp.float32) * (0.5 / math.sqrt(BLK))
    diagonal = jax.random.uniform(diagonal_key, (NBLK, BLK), jnp.float32, 0.7, 1.3)
    twisted = jax.random.uniform(twist_key, (NBLK, BLK), jnp.float32, -0.4, 0.4)
    radius = jax.random.uniform(radius_key, (2, NBLK), jnp.float32, 1.95, 2.2)
    wobble = jax.random.uniform(wobble_key, (2, NBLK), jnp.float32, -0.3, 0.3)
    quadrant = jax.random.randint(quadrant_key, (2, NBLK), 0, 4).astype(jnp.float32)
    phase = 0.25 * math.pi + 0.5 * math.pi * quadrant + wobble
    corner_real = radius * jnp.cos(phase)
    corner_imag = radius * jnp.sin(phase)
    index = jnp.arange(BLK, dtype=jnp.int32)
    low_mask = ((index[:, None] == BLK - 1) & (index[None, :] == 0)).astype(jnp.float32)
    high_mask = ((index[:, None] == 0) & (index[None, :] == BLK - 1)).astype(jnp.float32)
    keep = 1.0 - low_mask - high_mask
    identity = jnp.eye(BLK, dtype=jnp.float32)
    real_part = (noise[:, 0] + diagonal[:, :, None] * identity[None]) * keep[None]
    real_part = real_part + corner_real[0][:, None, None] * low_mask[None] + corner_real[1][:, None, None] * high_mask[None]
    imag_part = (noise[:, 1] + twisted[:, :, None] * identity[None]) * keep[None]
    imag_part = imag_part + corner_imag[0][:, None, None] * low_mask[None] + corner_imag[1][:, None, None] * high_mask[None]
    return jnp.stack([real_part, imag_part], axis=1).astype(jnp.bfloat16)


def set_ends(drawn, stream_key, smallest, largest):
    longest = drawn.shape.index(max(drawn.shape))
    spots = []
    for shift in (0, 1):
        where = [jax.random.randint(jax.random.fold_in(stream_key, axis), (), 0, length) for axis, length in enumerate(drawn.shape)]
        where[longest] = (where[longest] + shift) % drawn.shape[longest]
        spots.append(tuple(where))
    return drawn.at[spots[0]].set(smallest).at[spots[1]].set(largest)


def block_levels(rng, shape, cuts, smallest, top_value):
    loudness = 1.0
    for dim, shards_of in cuts:
        heights = jax.random.uniform(jax.random.fold_in(jax.random.fold_in(rng, 6), dim), (shards_of,), jnp.float32, smallest / len(cuts), top_value / len(cuts))
        loudness = loudness * jnp.repeat(jnp.exp(heights), shape[dim] // shards_of).reshape((-1,) + (1,) * (len(shape) - 1 - dim))
    return loudness


def centred(rng, dims, deviation, most, cuts=(), kind=jnp.bfloat16):
    values = deviation * jax.random.normal(rng, dims, jnp.float32)
    if cuts:
        values = values * block_levels(rng, dims, cuts, -0.22, 0.18)
    return jnp.clip(values, -most, most).astype(kind)


def setup_inputs(seed: int = 0) -> dict:
    keys = jax.random.split(jax.random.key(seed), 7)
    tangent = centred(keys[0], (MODES, 2, NZ, NY), 1.0, 6.0, ((0, 4), (2, 64)))
    base = centred(keys[1], (2, NZ, NY), 1.0, 6.0, ((1, 64), (2, 4)))
    theta = jnp.clip(jax.random.uniform(keys[2], (NZ, NY), jnp.float32, -3.140625, 3.140625), -3.140625, 3.140625).astype(jnp.bfloat16)
    eof_table = centred(keys[3], (EOFS, NZ), 1.0, 4.0, ((1, 64),), jnp.float32)
    mode_of_field = set_ends(jax.random.randint(keys[4], (MODES,), 0, EOFS), jax.random.fold_in(keys[4], 1), 0, EOFS - 1).astype(jnp.int32)
    block_factors = draw_block_factors(jax.random.fold_in(keys[6], 71), 0)
    return {"tangent": tangent, "base": base, "theta": theta, "eof_table": eof_table, "mode_of_field": mode_of_field, "block_factors": block_factors}


ALPHA_REAL = 0.15
ALPHA_IMAG = 0.1
COUPLE_REAL = 0.35
COUPLE_IMAG = -0.25


def fourier_table(length, orient):
    counter = jnp.arange(length, dtype=jnp.int32)
    residue = (counter[:, None] * counter[None, :]) % length
    angles = (2.0 * math.pi / length) * residue.astype(jnp.float32)
    cosine = jnp.cos(angles).astype(jnp.bfloat16)
    sine_part = (-orient * jnp.sin(angles)).astype(jnp.bfloat16)
    upper_half = jnp.stack([cosine, sine_part], axis=1)
    lower_half = jnp.stack([-sine_part, cosine], axis=1)
    return jnp.stack([upper_half, lower_half], axis=0)


def phase_tables(first_size, second_size, total_size):
    first_index = jnp.arange(first_size, dtype=jnp.int32)
    second_index = jnp.arange(second_size, dtype=jnp.int32)
    twist_turns = (first_index[:, None] * second_index[None, :]) % total_size
    twist_angle = (-2.0 * math.pi / total_size) * twist_turns.astype(jnp.float32)
    wavenumber = first_index[:, None] + first_size * second_index[None, :]
    signed_wave = jnp.where(wavenumber < total_size // 2, wavenumber, wavenumber - total_size)
    kernel_turns = (signed_wave * signed_wave) % (2 * total_size)
    kernel_angle = (-math.pi / total_size) * kernel_turns.astype(jnp.float32)
    return jnp.cos(twist_angle), jnp.sin(twist_angle), jnp.cos(kernel_angle), jnp.sin(kernel_angle)


def rotate(values, cos_part, sin_part):
    real_part = values[:, 0]
    imag_part = values[:, 1]
    return jnp.stack([real_part * cos_part - imag_part * sin_part, real_part * sin_part + imag_part * cos_part], axis=1)


def cross_range(fields):
    field_count = fields.shape[0]
    depth_rows = fields.shape[2]
    forward_one = fourier_table(R1, 1.0).astype(jnp.float32)
    forward_two = fourier_table(R2, 1.0).astype(jnp.float32)
    backward_two = fourier_table(R2, -1.0).astype(jnp.float32)
    backward_one = fourier_table(R1, -1.0).astype(jnp.float32)
    twist_cos, twist_sin, kernel_cos, kernel_sin = phase_tables(R1, R2, NY)
    shaped = fields.astype(jnp.float32).reshape(field_count, 2, depth_rows, R1, R2)
    first_pass = jnp.einsum("fprab,paqk->fqrkb", shaped, forward_one)
    first_pass = rotate(first_pass, twist_cos, twist_sin).astype(jnp.bfloat16)
    second_pass = jnp.einsum("fprkb,pbqm->fqrkm", first_pass.astype(jnp.float32), forward_two)
    second_pass = rotate(second_pass, kernel_cos, kernel_sin).astype(jnp.bfloat16)
    third_pass = jnp.einsum("fprkm,pmqb->fqrkb", second_pass.astype(jnp.float32), backward_two)
    third_pass = rotate(third_pass, twist_cos, -twist_sin).astype(jnp.bfloat16)
    spread = jnp.einsum("fprkb,pkqa->fqrab", third_pass.astype(jnp.float32), backward_one) * (1.0 / NY)
    return spread.astype(jnp.bfloat16).reshape(field_count, 2, depth_rows, NY)


def corner_gain(factors, row_index, col_index):
    corner = factors[:, :, row_index, col_index].astype(jnp.float32)
    return COUPLE_REAL * corner[:, 0] - COUPLE_IMAG * corner[:, 1], COUPLE_REAL * corner[:, 1] + COUPLE_IMAG * corner[:, 0]


def complex_product(left_real, left_imag, right_real, right_imag):
    best = lax.Precision.HIGHEST
    real_part = jnp.dot(left_real, right_real, precision=best) - jnp.dot(left_imag, right_imag, precision=best)
    imag_part = jnp.dot(left_real, right_imag, precision=best) + jnp.dot(left_imag, right_real, precision=best)
    return real_part, imag_part


def chain_matrix(gain_real, gain_imag, offset):
    count = gain_real.shape[0]
    rows = jnp.arange(count, dtype=jnp.int32)[:, None]
    cols = jnp.arange(count, dtype=jnp.int32)[None, :]
    neighbour = (cols == rows - offset).astype(jnp.float32)
    identity = (cols == rows).astype(jnp.float32)
    power_real = -gain_real[:, None] * neighbour
    power_imag = -gain_imag[:, None] * neighbour
    total_real = identity + power_real
    total_imag = power_imag
    reach = 2
    while reach < count:
        power_real, power_imag = complex_product(power_real, power_imag, power_real, power_imag)
        total_real, total_imag = complex_product(total_real, total_imag, identity + power_real, power_imag)
        reach = reach * 2
    shift_real = jnp.dot(neighbour, total_real, precision=lax.Precision.HIGHEST)
    shift_imag = jnp.dot(neighbour, total_imag, precision=lax.Precision.HIGHEST)
    return jnp.stack([jnp.stack([shift_real, -shift_imag], axis=1), jnp.stack([shift_imag, shift_real], axis=1)], axis=0)


def apply_chain(operator, edge_rows):
    return jnp.einsum("qkpj,fpjc->fqkc", operator, edge_rows, precision=lax.Precision.HIGHEST)


def coupling_term(carried, column):
    carry_real = carried[:, 0]
    carry_imag = carried[:, 1]
    scaled_real = (COUPLE_REAL * carry_real - COUPLE_IMAG * carry_imag)[:, :, None, :]
    scaled_imag = (COUPLE_REAL * carry_imag + COUPLE_IMAG * carry_real)[:, :, None, :]
    column_real = column[:, 0][None, :, :, None]
    column_imag = column[:, 1][None, :, :, None]
    term_real = scaled_real * column_real - scaled_imag * column_imag
    term_imag = scaled_real * column_imag + scaled_imag * column_real
    return jnp.stack([term_real, term_imag], axis=1)


def depth_solve(fields, factors):
    field_count = fields.shape[0]
    columns = fields.shape[3]
    block_size = factors.shape[2]
    last_row = block_size - 1
    values = fields.astype(jnp.float32)
    padded = jnp.pad(values, ((0, 0), (0, 0), (1, 1), (0, 0)))
    second = padded[:, :, 2:] - 2.0 * values + padded[:, :, :-2]
    rhs_field = (values + rotate(second, ALPHA_REAL, ALPHA_IMAG)).astype(jnp.bfloat16)
    blocks = rhs_field.reshape(field_count, 2, factors.shape[0], block_size, columns)
    factor_real = factors[:, 0]
    factor_imag = factors[:, 1]
    stacked = jnp.stack([jnp.stack([factor_real, -factor_imag], axis=2), jnp.stack([factor_imag, factor_real], axis=2)], axis=1)
    products = jnp.einsum("kqipj,fpkjc->fqkic", stacked.astype(jnp.float32), blocks.astype(jnp.float32))
    gain_real, gain_imag = corner_gain(factors, last_row, 0)
    earlier = apply_chain(chain_matrix(gain_real, gain_imag, 1), products[:, :, :, last_row])
    solved = products - coupling_term(earlier, factors[:, :, :, 0].astype(jnp.float32))
    back_real, back_imag = corner_gain(factors, 0, last_row)
    later = apply_chain(chain_matrix(back_real, back_imag, -1), solved[:, :, :, 0])
    result = solved - coupling_term(later, factors[:, :, :, last_row].astype(jnp.float32))
    return result.astype(jnp.bfloat16).reshape(field_count, 2, fields.shape[2], columns)


def propagate(fields, factors):
    return depth_solve(cross_range(fields), factors)


def reference(tangent, base, theta, eof_table, mode_of_field, block_factors):
    angles = theta.astype(jnp.float32)
    cosine = jnp.cos(angles)
    sine_part = jnp.sin(angles)
    base_values = base.astype(jnp.float32)
    screened = rotate(base_values[None], cosine, sine_part).astype(jnp.bfloat16)
    profiles = eof_table[mode_of_field]

    def tangent_step(inputs):
        single, profile = inputs
        values = single.astype(jnp.float32)
        lifted = jnp.stack([values[0] - profile[:, None] * base_values[1], values[1] + profile[:, None] * base_values[0]])
        source = rotate(lifted[None], cosine, sine_part).astype(jnp.bfloat16)
        return propagate(source, block_factors)[0]

    tangent_next = lax.map(tangent_step, (tangent, profiles))
    base_next = propagate(screened, block_factors)[0]
    return tangent_next, base_next
```

```python
import functools
import math

import jax
import jax.numpy as jnp
import ml_dtypes
import numpy as np
from jax import lax
from jax.experimental import pallas as pl
from jax.experimental.pallas import tpu as pltpu
from jax.sharding import PartitionSpec as P

MESH = pl.DeviceIdType.MESH
NZ = 2048
NY = 8192
R1 = 64
R2 = 128
NBLK = 16
BLK = 128
SLAB = 64
GRP = 4
ROWS = 32
CH = 16
ALPHA_REAL = 0.15
ALPHA_IMAG = 0.1
COUPLE_REAL = 0.35
COUPLE_IMAG = -0.25
VMEM = pltpu.VMEM
ANY = pl.ANY
F32 = jnp.float32
BF16 = jnp.bfloat16


def trig_coefficients():
    nodes = np.cos(np.pi * (np.arange(64) + 0.5) / 64)
    square = (nodes + 1.0) * 0.5 * math.pi**2
    root = np.sqrt(square)
    cheb = np.polynomial.chebyshev
    sine = cheb.cheb2poly(cheb.chebfit(nodes, np.sin(root) / root, 7))
    cosine = cheb.cheb2poly(cheb.chebfit(nodes, np.cos(root), 8))

    def in_square(coefs):
        total = np.zeros(1)
        shift = np.array([-1.0, 2.0 / math.pi**2])
        power = np.ones(1)
        for coef in coefs:
            total = np.polynomial.polynomial.polyadd(total, coef * power)
            power = np.polynomial.polynomial.polymul(power, shift)
        return [float(v) for v in total]

    return in_square(sine), in_square(cosine)


SIN_COEFS, COS_COEFS = trig_coefficients()


def tables():
    k1 = np.arange(R1)
    b = np.arange(R2)
    angle = -2.0 * np.pi * ((k1[:, None] * b[None, :]) % NY) / NY
    wave = k1[:, None] + R1 * b[None, :]
    signed = np.where(wave < NY // 2, wave, wave - NY)
    kernel_angle = -np.pi * ((signed * signed) % (2 * NY)) / NY
    phases = np.stack([np.cos(angle), np.sin(angle), np.cos(kernel_angle), np.sin(kernel_angle)])
    phases = phases.astype(np.float32).reshape(4, R1, 1, R2)
    turn = 2.0 * np.pi * ((b[:, None] * b[None, :]) % R2) / R2
    c = np.cos(turn).astype(ml_dtypes.bfloat16).astype(np.float32)
    s = np.sin(turn).astype(ml_dtypes.bfloat16).astype(np.float32)
    forward = np.block([[c, -s], [s, c]])
    backward = np.block([[c, s], [-s, c]])
    fourier = np.stack([forward, backward]).astype(ml_dtypes.bfloat16)
    eight = np.arange(8)
    inner = -2.0 * np.pi * (eight[:, None] * eight[None, :]) / 64.0
    inner = np.concatenate([np.cos(inner), np.sin(inner)], axis=1).astype(np.float32)
    return phases, fourier, inner


def add(p, q):
    return (p[0] + q[0], p[1] + q[1])


def sub(p, q):
    return (p[0] - q[0], p[1] - q[1])


def mul(p, q):
    return (p[0] * q[0] - p[1] * q[1], p[0] * q[1] + p[1] * q[0])


def quarter(p, sign):
    return (-p[1], p[0]) if sign > 0 else (p[1], -p[0])


def dft8(x, sign):
    half = math.sqrt(0.5)

    def four(a, b, c, d):
        e0, e1 = add(a, c), sub(a, c)
        o0, o1 = add(b, d), quarter(sub(b, d), sign)
        return add(e0, o0), add(e1, o1), sub(e0, o0), sub(e1, o1)

    e = four(x[0], x[2], x[4], x[6])
    o = four(x[1], x[3], x[5], x[7])
    u1 = quarter(o[1], sign)
    u3 = quarter(o[3], sign)
    o1 = ((o[1][0] + u1[0]) * half, (o[1][1] + u1[1]) * half)
    o2 = quarter(o[2], sign)
    o3 = ((u3[0] - o[3][0]) * half, (u3[1] - o[3][1]) * half)
    o = (o[0], o1, o2, o3)
    return [add(e[i], o[i]) for i in range(4)] + [sub(e[i], o[i]) for i in range(4)]


def cos_sin(theta):
    u = theta * theta
    s = SIN_COEFS[-1]
    for coef in SIN_COEFS[-2::-1]:
        s = s * u + coef
    c = COS_COEFS[-1]
    for coef in COS_COEFS[-2::-1]:
        c = c * u + coef
    return c, s * theta


def cross_range(rows, load, store, inner_ref, phase_ref, fourier_ref, work, mid):
    def twist(index, sign):
        return [None] + [(inner_ref[index, k], sign * inner_ref[index, 8 + k]) for k in range(1, 8)]

    def forward_one(a2, carry):
        out = dft8([load(a1, a2) for a1 in range(8)], -1)
        factors = twist(a2, 1.0)
        for k in range(8):
            value = out[k] if k == 0 else mul(out[k], factors[k])
            for p in range(2):
                work[a2 * 8 + k, p, pl.ds(0, rows), :] = value[p]
        return carry

    lax.fori_loop(0, 8, forward_one, 0)

    def forward_two(k, carry):
        values = [tuple(work[a2 * 8 + k, p, pl.ds(0, rows), :] for p in range(2)) for a2 in range(8)]
        out = dft8(values, -1)
        for kk in range(8):
            k1 = k + 8 * kk
            value = mul(out[kk], (phase_ref[0, k1], phase_ref[1, k1]))
            for p in range(2):
                mid[k1, pl.ds(0, rows), pl.ds(128 * p, 128)] = value[p]
        return carry

    lax.fori_loop(0, 8, forward_two, 0)

    def inner(i, carry):
        part = pl.ds(i * 16, 16)
        y = mid[part, pl.ds(0, rows), :].reshape(16 * rows, 256).astype(BF16)
        y = jnp.dot(y, fourier_ref[0], preferred_element_type=F32).reshape(16, rows, 256)
        y = mul((y[:, :, :128], y[:, :, 128:]), (phase_ref[2, part], phase_ref[3, part]))
        y = jnp.concatenate(y, axis=2).reshape(16 * rows, 256).astype(BF16)
        y = jnp.dot(y, fourier_ref[1], preferred_element_type=F32).reshape(16, rows, 256)
        y = mul((y[:, :, :128], y[:, :, 128:]), (phase_ref[0, part], -phase_ref[1, part]))
        for p in range(2):
            work[part, p, pl.ds(0, rows), :] = y[p]
        return carry

    lax.fori_loop(0, 4, inner, 0)

    def backward_one(k2, carry):
        values = [tuple(work[8 * q + k2, p, pl.ds(0, rows), :] for p in range(2)) for q in range(8)]
        out = dft8(values, 1)
        factors = twist(k2, -1.0)
        for a in range(8):
            value = out[a] if a == 0 else mul(out[a], factors[a])
            for p in range(2):
                mid[k2 * 8 + a, pl.ds(0, rows), pl.ds(128 * p, 128)] = value[p]
        return carry

    lax.fori_loop(0, 8, backward_one, 0)

    def backward_two(a, carry):
        values = [
            tuple(mid[k2 * 8 + a, pl.ds(0, rows), pl.ds(128 * p, 128)] for p in range(2)) for k2 in range(8)
        ]
        out = dft8(values, 1)
        for aa in range(8):
            store(a + 8 * aa, (out[aa][0] * (1.0 / NY), out[aa][1] * (1.0 / NY)))
        return carry

    lax.fori_loop(0, 8, backward_two, 0)


def exchange_kernel(
    tangent_hbm,
    base_hbm,
    theta_hbm,
    eof_ref,
    mode_ref,
    factor_ref,
    inner_ref,
    phase_ref,
    fourier_ref,
    t_out,
    b_out,
    g_out,
    p_out,
    tangent,
    base,
    theta,
    quarter_out,
    quarter_in,
    work,
    mid,
    t_send,
    b_send,
    rows32,
    factors,
    profile,
    load_sem,
    own_sem,
    q_sem,
    t_sem,
    b_sem,
    bg_sem,
    g_sem,
    p_sem,
):
    g = lax.axis_index("grp")
    s = lax.axis_index("slab")
    zh, x, y = s // 16, (s // 4) % 4, s % 4
    core = g % 2

    def at_slab(dz, dx, dy):
        return (g, ((zh + dz) % 4) * 16 + ((x + dx) % 4) * 4 + (y + dy) % 4)

    def partner(i):
        return at_slab(i % 4, (i // 4) % 4, i // 16)

    def in_grp(i):
        mate = g + 1 - 2 * (g % 2) if i % 2 else g
        return (mate + 2) % 4 if i // 2 else mate

    core_mate = in_grp(1)
    far_mate = in_grp(2)

    loads = [
        pltpu.make_async_copy(theta_hbm, theta, load_sem.at[0]),
        pltpu.make_async_copy(tangent_hbm.at[0], tangent, load_sem.at[1]),
        pltpu.make_async_copy(base_hbm, base, load_sem.at[2]),
    ]
    for copy in loads:
        copy.start()

    barrier = pltpu.get_barrier_semaphore()

    def greet(i, carry):
        pl.semaphore_signal(barrier, inc=1, device_id=partner(i), device_id_type=MESH)
        return carry

    lax.fori_loop(1, SLAB, greet, 0)
    for i in (1, 2, 3):
        pl.semaphore_signal(barrier, inc=1, device_id=(in_grp(i), s), device_id_type=MESH)

    def put(src, dst, sems, target):
        return pltpu.make_async_remote_copy(
            src_ref=src, dst_ref=dst, send_sem=sems.at[0], recv_sem=sems.at[1], device_id=target, device_id_type=MESH
        )

    for k in range(NBLK):
        for p in range(2):
            rows32[pl.ds(4 * k + 2 * p, 2), :] = factor_ref[k, p].astype(F32)
    factors[...] = rows32[pl.ds(pl.multiple_of(core * 32, 32), 32), :].astype(BF16)
    profile[...] = jnp.zeros_like(profile)
    profile[:, pl.ds(0, ROWS)] = eof_ref[pl.ds(mode_ref[0], 1), :]

    for copy in loads:
        copy.wait()

    def load_tangent(c, a1, a2):
        depth = pl.ds(pl.multiple_of(c * CH, CH), CH)
        cells = pl.ds(pl.multiple_of((8 * a1 + a2) * 128, 128), 128)
        turn = cos_sin(theta[depth, cells].astype(F32))
        return mul((tangent[0, depth, cells].astype(F32), tangent[1, depth, cells].astype(F32)), turn)

    def store_tangent(c, a, value):
        for p in range(2):
            t_send[c, a, p] = value[p].astype(BF16)

    g_own = g_out.at[core, zh, x, y]
    g_moves = []
    p_moves = []
    for i in (1, 2, 3):
        g_moves.append(put(factors, g_own, g_sem.at[0], at_slab(i, 0, 0)))
        p_moves.append(put(profile, p_out.at[zh, x, y], p_sem.at[0], at_slab(i, 0, 0)))
    gx, px = g_out.at[core, :, x, y], p_out.at[:, x, y]
    gy, py = g_out.at[core, :, :, y], p_out.at[:, :, y]
    g_moves += [put(gx, gx, g_sem.at[1], at_slab(0, i, 0)) for i in (1, 2, 3)]
    p_moves += [put(px, px, p_sem.at[1], at_slab(0, i, 0)) for i in (1, 2, 3)]
    g_moves += [put(gy, gy, g_sem.at[2], at_slab(0, 0, i)) for i in (1, 2, 3)]
    p_moves += [put(py, py, p_sem.at[2], at_slab(0, 0, i)) for i in (1, 2, 3)]
    g_half = put(g_out.at[core], g_out.at[core], g_sem.at[3], (core_mate, s))

    def gather_start(stage):
        for move in g_moves[3 * stage : 3 * stage + 3] + p_moves[3 * stage : 3 * stage + 3]:
            move.start()

    def gather_wait(stage):
        for ref, sem in ((g_out.at[core], g_sem), (p_out, p_sem)):
            part = ref.at[pl.ds(0, 3), 0, 0]
            if stage == 1:
                part = ref.at[:, pl.ds(0, 3), 0]
            if stage == 2:
                part = ref.at[:, :, pl.ds(0, 3)]
            put(part, part, sem.at[stage], at_slab(1, 0, 0)).wait()

    def quarter_move(i):
        return put(quarter_out.at[in_grp(i)], quarter_in.at[g], q_sem, (in_grp(i), s))

    def t_move(c, i):
        target = partner(i)
        return put(t_send.at[c, target[1]], t_out.at[c, s], t_sem.at[c], target)

    def b_move(i):
        target = partner(i)
        return put(b_send.at[target[1]], b_out.at[g, s], b_sem, target)

    def start_all(move):
        def step(i, carry):
            move(i).start()
            return carry

        lax.fori_loop(1, SLAB, step, 0)

    def own_t(c):
        return pltpu.make_async_copy(t_send.at[c, s], t_out.at[c, s], own_sem.at[c])

    own_b = pltpu.make_async_copy(b_send.at[s], b_out.at[g, s], own_sem.at[2])
    own_g = pltpu.make_async_copy(factors, g_own, own_sem.at[3])
    own_p = pltpu.make_async_copy(profile, p_out.at[zh, x, y], own_sem.at[4])
    own_q = pltpu.make_async_copy(quarter_out.at[g], quarter_in.at[g], own_sem.at[5])

    def chunk(c, carry):
        cross_range(
            CH,
            functools.partial(load_tangent, c),
            functools.partial(store_tangent, c),
            inner_ref,
            phase_ref,
            fourier_ref,
            work,
            mid,
        )

        @pl.when(c == 0)
        def _():
            def screen(a, carry):
                cells = pl.ds(pl.multiple_of(a * 128, 128), 128)
                there = pl.ds(pl.multiple_of(g * 2048 + a * 128, 128), 128)
                turn = cos_sin(theta[:, there].astype(F32))
                value = mul((base[0, :, cells].astype(F32), base[1, :, cells].astype(F32)), turn)
                for part in range(4):
                    depth = slice(8 * part, 8 * part + 8)
                    quarter_out[part, a] = jnp.concatenate([value[0][depth], value[1][depth]], axis=0).astype(BF16)
                return carry

            lax.fori_loop(0, 16, screen, 0)
            pl.semaphore_wait(barrier, SLAB - 1 + 3)
            for i in (1, 2, 3):
                quarter_move(i).start()
            own_q.start()
            gather_start(0)
            own_g.start()
            own_p.start()
            start_all(functools.partial(t_move, 0))
            own_t(0).start()

        return carry

    lax.fori_loop(0, 2, chunk, 0)

    own_q.wait()
    three = quarter_out.at[pl.ds(0, 3)]
    put(three, quarter_in.at[pl.ds(0, 3)], q_sem, (core_mate, s)).wait()

    def load_base(a1, a2):
        tile = quarter_in[a1 // 2, 8 * (a1 % 2) + a2].astype(F32)
        return (tile[:8], tile[8:])

    def store_base(a, value):
        b_send[a] = jnp.concatenate(value, axis=0).astype(BF16)

    cross_range(8, load_base, store_base, inner_ref, phase_ref, fourier_ref, work, mid)
    start_all(b_move)
    own_b.start()
    own_g.wait()
    own_p.wait()
    gather_wait(0)
    gather_start(1)
    start_all(functools.partial(t_move, 1))
    own_t(1).start()
    gather_wait(1)
    gather_start(2)

    own_b.wait()
    most = pl.ds(0, SLAB - 1)
    put(b_send.at[most], b_out.at[0, most], b_sem, (core_mate, s)).wait()
    mine = b_out.at[g]
    to_core = put(mine, mine, bg_sem.at[0], (core_mate, s))
    to_far = put(mine, mine, bg_sem.at[1], (far_mate, s))
    to_far.start()
    to_core.start()
    gather_wait(2)
    g_half.start()
    to_far.wait()
    theirs = b_out.at[far_mate]
    onward = put(theirs, theirs, bg_sem.at[2], (core_mate, s))
    onward.start()
    to_core.wait()
    g_half.wait()
    onward.wait()
    for c in range(2):
        own_t(c).wait()
        put(t_send.at[c, most], t_out.at[c, most], t_sem.at[c], (core_mate, s)).wait()


def solve_kernel(t_ref, b_ref, g_ref, p_ref, t_next, b_next, values, spread32, blocks, matrix, rhs, edge):
    zeros = jnp.zeros((2, 8, 256), F32)
    values[:, pl.ds(0, 8), :] = zeros
    values[:, pl.ds(NZ + 8, 8), :] = zeros
    diagonal = lax.broadcasted_iota(jnp.int32, (ROWS, 128), 0) == lax.broadcasted_iota(jnp.int32, (ROWS, 128), 1)

    def combine(s, carry):
        profile = jnp.sum(jnp.where(diagonal, p_ref[s], 0.0), axis=1, keepdims=True)
        for c in range(2):
            t_real = t_ref[c, s, 0].astype(F32)
            t_imag = t_ref[c, s, 1].astype(F32)
            for h in range(2):
                tile = b_ref[2 * c + h, s].astype(F32)
                b_real, b_imag = tile[:8], tile[8:]
                part = slice(8 * h, 8 * h + 8)
                at = CH * c + 8 * h
                scale = profile[at : at + 8]
                here = pl.ds(pl.multiple_of(s * ROWS + at + 8, 8), 8)
                values[0, here, pl.ds(0, 128)] = t_real[part] - scale * b_imag
                values[1, here, pl.ds(0, 128)] = t_imag[part] + scale * b_real
                values[0, here, pl.ds(128, 128)] = b_real
                values[1, here, pl.ds(128, 128)] = b_imag
        return carry

    lax.fori_loop(0, SLAB, combine, 0)

    def widen(s, carry):
        for h in range(2):
            spread32[pl.ds(pl.multiple_of(h * 2048 + s * 32, 32), 32), :] = g_ref[h, s].astype(F32)
        return carry

    lax.fori_loop(0, SLAB, widen, 0)

    def arrange(k, carry):
        start = (k // 8) * 2048 + (k % 8) * 4
        for p in range(2):
            for r in range(2):
                rows = spread32[pl.ds(start + 2 * p + r, 64, stride=32), :]
                blocks[k, p, pl.ds(r, 64, stride=2), :] = rows
        real = blocks[k, 0]
        imag = blocks[k, 1]
        upper = jnp.concatenate([real, -imag], axis=1)
        lower = jnp.concatenate([imag, real], axis=1)
        matrix[k, pl.ds(0, 128), :] = upper.astype(BF16)
        matrix[k, pl.ds(128, 128), :] = lower.astype(BF16)
        return carry

    lax.fori_loop(0, NBLK, arrange, 0)

    def right_side(k, carry):
        shifted = []
        for p in range(2):
            wide = values[p, pl.ds(pl.multiple_of(k * BLK, BLK), BLK + 16), :]
            centre = wide[8 : BLK + 8]
            shifted.append((centre, wide[7 : BLK + 7] + wide[9 : BLK + 9] - 2.0 * centre))
        (c_real, d_real), (c_imag, d_imag) = shifted
        r_real = c_real + ALPHA_REAL * d_real - ALPHA_IMAG * d_imag
        r_imag = c_imag + ALPHA_REAL * d_imag + ALPHA_IMAG * d_real
        rhs[k, 0] = r_real
        rhs[k, 1] = r_imag
        both = jnp.concatenate([r_real, r_imag], axis=0).astype(BF16)
        first = [blocks[k, p, pl.ds(0, 1), :] for p in range(2)]
        last = [blocks[k, p, pl.ds(BLK - 1, 1), :] for p in range(2)]
        lhs = []
        for real, imag in (first, last):
            lhs.append(jnp.concatenate([real, -imag], axis=1))
            lhs.append(jnp.concatenate([imag, real], axis=1))
        lhs = jnp.concatenate(lhs + lhs, axis=0).astype(BF16)
        edge[k] = jnp.dot(lhs, both, preferred_element_type=F32)
        return carry

    lax.fori_loop(0, NBLK, right_side, 0)

    couple = (COUPLE_REAL, COUPLE_IMAG)

    def entry(k, row, col):
        return tuple(blocks[k, p, pl.ds(row, 1), pl.ds(col, 1)] for p in range(2))

    def row_of(k, i):
        return tuple(edge[k, pl.ds(i + p, 1), :] for p in range(2))

    carried = []
    starts = []
    held = None
    for k in range(NBLK):
        first, last = row_of(k, 0), row_of(k, 2)
        if held is not None:
            scaled = mul(held, couple)
            carried.append(scaled)
            first = sub(first, mul(scaled, entry(k, 0, 0)))
            last = sub(last, mul(scaled, entry(k, BLK - 1, 0)))
        starts.append(first)
        held = last
    held = None
    for k in range(NBLK - 1, -1, -1):
        value = starts[k]
        if held is not None:
            scaled = mul(held, couple)
            for p in range(2):
                rhs[k, p, pl.ds(BLK - 1, 1), :] -= scaled[p]
            value = sub(value, mul(scaled, entry(k, 0, BLK - 1)))
        held = value
    for k in range(1, NBLK):
        for p in range(2):
            rhs[k, p, pl.ds(0, 1), :] -= carried[k - 1][p]

    def finish(k, carry):
        both = rhs[k].reshape(256, 256).astype(BF16)
        result = jnp.dot(matrix[k], both, preferred_element_type=F32).astype(BF16)
        here = pl.ds(pl.multiple_of(k * BLK, BLK), BLK)
        for p in range(2):
            t_next[0, p, here, :] = result[128 * p : 128 * p + 128, :128]
            b_next[p, here, :] = result[128 * p : 128 * p + 128, 128:]
        return carry

    lax.fori_loop(0, NBLK, finish, 0)


def on_device(tangent, base, theta, eof_table, mode_of_field, block_factors):
    phases, fourier, inner = tables()
    in_vmem = pl.BlockSpec(memory_space=VMEM)
    in_smem = pl.BlockSpec(memory_space=pltpu.SMEM)
    anywhere = pl.BlockSpec(memory_space=ANY)
    dma = pltpu.SemaphoreType.DMA
    t_all, b_all, g_all, p_all = pl.pallas_call(
        exchange_kernel,
        out_shape=(
            jax.ShapeDtypeStruct((2, SLAB, 2, CH, 128), BF16),
            jax.ShapeDtypeStruct((GRP, SLAB, 16, 128), BF16),
            jax.ShapeDtypeStruct((2, 4, 4, 4, 32, 128), BF16),
            jax.ShapeDtypeStruct((4, 4, 4, 1, 128), F32),
        ),
        in_specs=[anywhere, anywhere, anywhere, in_vmem, in_smem, in_vmem, in_smem, in_vmem, in_vmem],
        out_specs=(anywhere, anywhere, anywhere, anywhere),
        scratch_shapes=[
            VMEM((2, ROWS, NY), BF16),
            VMEM((2, ROWS, NY // 4), BF16),
            VMEM((ROWS, NY), BF16),
            VMEM((4, 16, 16, 128), BF16),
            VMEM((4, 16, 16, 128), BF16),
            VMEM((R1, 2, CH, 128), F32),
            VMEM((R1, CH, 256), F32),
            VMEM((2, SLAB, 2, CH, 128), BF16),
            VMEM((SLAB, 16, 128), BF16),
            VMEM((64, 128), F32),
            VMEM((32, 128), BF16),
            VMEM((1, 128), F32),
            dma((3,)),
            dma((6,)),
            dma((2,)),
            dma((2, 2)),
            dma((2,)),
            dma((3, 2)),
            dma((4, 2)),
            dma((3, 2)),
        ],
        compiler_params=pltpu.CompilerParams(
            collective_id=0, has_side_effects=True, vmem_limit_bytes=48 * 2**20
        ),
        name="exchange",
    )(
        tangent,
        base,
        theta,
        eof_table,
        mode_of_field,
        block_factors,
        jnp.asarray(inner),
        jnp.asarray(phases),
        jnp.asarray(fourier),
    )
    return pl.pallas_call(
        solve_kernel,
        out_shape=(
            jax.ShapeDtypeStruct((1, 2, NZ, 128), BF16),
            jax.ShapeDtypeStruct((2, NZ, 128), BF16),
        ),
        in_specs=[in_vmem] * 4,
        out_specs=(in_vmem, in_vmem),
        scratch_shapes=[
            VMEM((2, NZ + 16, 256), F32),
            VMEM((4096, 128), F32),
            VMEM((NBLK, 2, BLK, 128), F32),
            VMEM((NBLK, 256, 256), BF16),
            VMEM((NBLK, 2, BLK, 256), F32),
            VMEM((NBLK, 8, 256), F32),
        ],
        compiler_params=pltpu.CompilerParams(vmem_limit_bytes=48 * 2**20),
        name="solve",
    )(t_all, b_all, g_all.reshape(2, SLAB, 32, 128), p_all.reshape(SLAB, 1, 128))


def solution(mesh):
    in_specs = (
        P("grp", None, "slab", None),
        P(None, "slab", "grp"),
        P("slab", None),
        P(None, "slab"),
        P("grp"),
        P(None, None, "slab", None),
    )
    out_specs = (P("grp", None, None, "slab"), P(None, None, "slab"))
    return jax.shard_map(on_device, mesh=mesh, in_specs=in_specs, out_specs=out_specs, check_vma=False)
```

```python
import functools
import math

import jax
import jax.numpy as jnp
import ml_dtypes
import numpy as np
from jax import lax
from jax.experimental import pallas as pl
from jax.experimental.pallas import tpu as pltpu
from jax.sharding import PartitionSpec as P

MESH = pl.DeviceIdType.MESH
NZ = 2048
NY = 8192
R1 = 64
R2 = 128
NBLK = 16
BLK = 128
SLAB = 64
GRP = 4
ROWS = 32
CH = 16
ALPHA_REAL = 0.15
ALPHA_IMAG = 0.1
COUPLE_REAL = 0.35
COUPLE_IMAG = -0.25
VMEM = pltpu.VMEM
ANY = pl.ANY
F32 = jnp.float32
BF16 = jnp.bfloat16


def trig_coefficients():
    nodes = np.cos(np.pi * (np.arange(64) + 0.5) / 64)
    square = (nodes + 1.0) * 0.5 * math.pi**2
    root = np.sqrt(square)
    cheb = np.polynomial.chebyshev
    sine = cheb.cheb2poly(cheb.chebfit(nodes, np.sin(root) / root, 7))
    cosine = cheb.cheb2poly(cheb.chebfit(nodes, np.cos(root), 8))

    def in_square(coefs):
        total = np.zeros(1)
        shift = np.array([-1.0, 2.0 / math.pi**2])
        power = np.ones(1)
        for coef in coefs:
            total = np.polynomial.polynomial.polyadd(total, coef * power)
            power = np.polynomial.polynomial.polymul(power, shift)
        return [float(v) for v in total]

    return in_square(sine), in_square(cosine)


SIN_COEFS, COS_COEFS = trig_coefficients()


def tables():
    k1 = np.arange(R1)
    b = np.arange(R2)
    angle = -2.0 * np.pi * ((k1[:, None] * b[None, :]) % NY) / NY
    wave = k1[:, None] + R1 * b[None, :]
    signed = np.where(wave < NY // 2, wave, wave - NY)
    kernel_angle = -np.pi * ((signed * signed) % (2 * NY)) / NY
    phases = np.stack([np.cos(angle), np.sin(angle), np.cos(kernel_angle), np.sin(kernel_angle)])
    phases = phases.astype(np.float32).reshape(4, R1, 1, R2)
    turn = 2.0 * np.pi * ((b[:, None] * b[None, :]) % R2) / R2
    c = np.cos(turn).astype(ml_dtypes.bfloat16).astype(np.float32)
    s = np.sin(turn).astype(ml_dtypes.bfloat16).astype(np.float32)
    forward = np.block([[c, -s], [s, c]])
    backward = np.block([[c, s], [-s, c]])
    fourier = np.stack([forward, backward]).astype(ml_dtypes.bfloat16)
    eight = np.arange(8)
    inner = -2.0 * np.pi * (eight[:, None] * eight[None, :]) / 64.0
    inner = np.concatenate([np.cos(inner), np.sin(inner)], axis=1).astype(np.float32)
    return phases, fourier, inner


def add(p, q):
    return (p[0] + q[0], p[1] + q[1])


def sub(p, q):
    return (p[0] - q[0], p[1] - q[1])


def mul(p, q):
    return (p[0] * q[0] - p[1] * q[1], p[0] * q[1] + p[1] * q[0])


def quarter(p, sign):
    return (-p[1], p[0]) if sign > 0 else (p[1], -p[0])


def dft8(x, sign):
    half = math.sqrt(0.5)

    def four(a, b, c, d):
        e0, e1 = add(a, c), sub(a, c)
        o0, o1 = add(b, d), quarter(sub(b, d), sign)
        return add(e0, o0), add(e1, o1), sub(e0, o0), sub(e1, o1)

    e = four(x[0], x[2], x[4], x[6])
    o = four(x[1], x[3], x[5], x[7])
    u1 = quarter(o[1], sign)
    u3 = quarter(o[3], sign)
    o1 = ((o[1][0] + u1[0]) * half, (o[1][1] + u1[1]) * half)
    o2 = quarter(o[2], sign)
    o3 = ((u3[0] - o[3][0]) * half, (u3[1] - o[3][1]) * half)
    o = (o[0], o1, o2, o3)
    return [add(e[i], o[i]) for i in range(4)] + [sub(e[i], o[i]) for i in range(4)]


def cos_sin(theta):
    u = theta * theta
    s = SIN_COEFS[-1]
    for coef in SIN_COEFS[-2::-1]:
        s = s * u + coef
    c = COS_COEFS[-1]
    for coef in COS_COEFS[-2::-1]:
        c = c * u + coef
    return c, s * theta


def cross_range(rows, load, store, inner_ref, phase_ref, fourier_ref, work, mid, between=None):
    def twist(index, sign):
        return [None] + [(inner_ref[index, k], sign * inner_ref[index, 8 + k]) for k in range(1, 8)]

    def forward_one(a2, carry):
        out = dft8([load(a1, a2) for a1 in range(8)], -1)
        factors = twist(a2, 1.0)
        for k in range(8):
            value = out[k] if k == 0 else mul(out[k], factors[k])
            for p in range(2):
                work[a2 * 8 + k, p, pl.ds(0, rows), :] = value[p]
        return carry

    lax.fori_loop(0, 8, forward_one, 0)

    def forward_two(k, carry):
        values = [tuple(work[a2 * 8 + k, p, pl.ds(0, rows), :] for p in range(2)) for a2 in range(8)]
        out = dft8(values, -1)
        for kk in range(8):
            k1 = k + 8 * kk
            value = mul(out[kk], (phase_ref[0, k1], phase_ref[1, k1]))
            for p in range(2):
                mid[k1, pl.ds(0, rows), pl.ds(128 * p, 128)] = value[p]
        return carry

    lax.fori_loop(0, 8, forward_two, 0)
    if between is not None:
        between()

    def inner(i, carry):
        part = pl.ds(i * 16, 16)
        y = mid[part, pl.ds(0, rows), :].reshape(16 * rows, 256).astype(BF16)
        y = jnp.dot(y, fourier_ref[0], preferred_element_type=F32).reshape(16, rows, 256)
        y = mul((y[:, :, :128], y[:, :, 128:]), (phase_ref[2, part], phase_ref[3, part]))
        y = jnp.concatenate(y, axis=2).reshape(16 * rows, 256).astype(BF16)
        y = jnp.dot(y, fourier_ref[1], preferred_element_type=F32).reshape(16, rows, 256)
        y = mul((y[:, :, :128], y[:, :, 128:]), (phase_ref[0, part], -phase_ref[1, part]))
        for p in range(2):
            work[part, p, pl.ds(0, rows), :] = y[p]
        return carry

    lax.fori_loop(0, 4, inner, 0)

    def backward_one(k2, carry):
        values = [tuple(work[8 * q + k2, p, pl.ds(0, rows), :] for p in range(2)) for q in range(8)]
        out = dft8(values, 1)
        factors = twist(k2, -1.0)
        for a in range(8):
            value = out[a] if a == 0 else mul(out[a], factors[a])
            for p in range(2):
                mid[k2 * 8 + a, pl.ds(0, rows), pl.ds(128 * p, 128)] = value[p]
        return carry

    lax.fori_loop(0, 8, backward_one, 0)

    def backward_two(a, carry):
        values = [
            tuple(mid[k2 * 8 + a, pl.ds(0, rows), pl.ds(128 * p, 128)] for p in range(2)) for k2 in range(8)
        ]
        out = dft8(values, 1)
        for aa in range(8):
            store(a + 8 * aa, (out[aa][0] * (1.0 / NY), out[aa][1] * (1.0 / NY)))
        return carry

    lax.fori_loop(0, 8, backward_two, 0)


def clear_ends(values):
    zeros = jnp.zeros((2, 8, 128), F32)
    values[:, pl.ds(0, 8), :] = zeros
    values[:, pl.ds(NZ + 8, 8), :] = zeros


def right_side(values, edge_lhs, rhs, edge):
    def step(k, carry):
        pairs = []
        for p in range(2):
            centre = values[p, pl.ds(pl.multiple_of(k * BLK + 8, 8), BLK), :]
            above = values[p, pl.ds(k * BLK + 7, BLK), :]
            below = values[p, pl.ds(k * BLK + 9, BLK), :]
            pairs.append((centre, above + below - 2.0 * centre))
        (c_real, d_real), (c_imag, d_imag) = pairs
        r_real = c_real + ALPHA_REAL * d_real - ALPHA_IMAG * d_imag
        r_imag = c_imag + ALPHA_REAL * d_imag + ALPHA_IMAG * d_real
        rhs[k, pl.ds(0, BLK), :] = r_real
        rhs[k, pl.ds(BLK, BLK), :] = r_imag
        both = jnp.concatenate([r_real.astype(BF16), r_imag.astype(BF16)], axis=0)
        edge[k] = jnp.dot(edge_lhs[k], both, preferred_element_type=F32)
        return carry

    lax.fori_loop(0, NBLK, step, 0, unroll=2)


def recur(edge, corner, rhs):
    couple = (COUPLE_REAL, COUPLE_IMAG)

    def entry(k, i):
        return tuple(corner[k, pl.ds(2 * i + p, 1), :] for p in range(2))

    def row_of(k, i):
        return tuple(edge[k, pl.ds(i + p, 1), :] for p in range(2))

    starts = []
    held = None
    for k in range(NBLK):
        first, last = row_of(k, 0), row_of(k, 2)
        if held is not None:
            scaled = mul(held, couple)
            for p in range(2):
                rhs[k, pl.ds(BLK * p, 1), :] -= scaled[p]
            first = sub(first, mul(scaled, entry(k, 0)))
            last = sub(last, mul(scaled, entry(k, 1)))
        starts.append(first)
        held = last
    held = None
    for k in range(NBLK - 1, -1, -1):
        value = starts[k]
        if held is not None:
            scaled = mul(held, couple)
            for p in range(2):
                rhs[k, pl.ds(BLK * p + BLK - 1, 1), :] -= scaled[p]
            value = sub(value, mul(scaled, entry(k, 2)))
        held = value


def finish(matrix, rhs, store, begin, count):
    def step(i, carry):
        k = begin + i
        result = jnp.dot(matrix[k], rhs[k].astype(BF16), preferred_element_type=F32).astype(BF16)
        here = pl.ds(pl.multiple_of(k * BLK, BLK), BLK)
        for p in range(2):
            store(p, here, result[128 * p : 128 * p + 128])
        return carry

    lax.fori_loop(0, count, step, 0, unroll=2)


def exchange_kernel(
    tangent_hbm,
    base_hbm,
    theta_hbm,
    eof_hbm,
    mode_hbm,
    factor_hbm,
    inner_hbm,
    phase_hbm,
    fourier_hbm,
    t_next,
    b_next,
    t_late,
    values,
    matrix,
    edge_lhs,
    corner,
    done,
    tangent,
    base,
    theta,
    eof,
    mode,
    factor_in,
    inner_ref,
    phase_ref,
    fourier_ref,
    quarter_out,
    quarter_in,
    work,
    mid,
    t_send,
    b_send,
    rows32,
    factors,
    profile,
    t_early,
    b_all,
    g_all,
    p_all,
    p_wide,
    spread32,
    blocks,
    b_values,
    rhs,
    edge,
    load_sem,
    own_sem,
    q_sem,
    t_sem,
    b_sem,
    bg_sem,
    g_sem,
    p_sem,
    round_sem,
    done_sem,
):
    g = lax.axis_index("grp")
    s = lax.axis_index("slab")
    zh, x, y = s // 16, (s // 4) % 4, s % 4
    core = g % 2

    def at_slab(dz, dx, dy):
        return (g, ((zh + dz) % 4) * 16 + ((x + dx) % 4) * 4 + (y + dy) % 4)

    def partner(i):
        return at_slab(i % 4, (i // 4) % 4, i // 16)

    def in_grp(i):
        mate = g + 1 - 2 * (g % 2) if i % 2 else g
        return (mate + 2) % 4 if i // 2 else mate

    core_mate = in_grp(1)
    far_mate = in_grp(2)
    lines = [[at_slab(i, 0, 0) for i in (1, 2, 3)], [at_slab(0, i, 0) for i in (1, 2, 3)], [at_slab(0, 0, i) for i in (1, 2, 3)]]
    grp_line = [(in_grp(i), s) for i in (1, 2, 3)]

    barrier = pltpu.get_barrier_semaphore()
    for target in lines[0] + lines[1] + lines[2] + grp_line:
        pl.semaphore_signal(barrier, inc=1, device_id=target, device_id_type=MESH)

    pairs = [
        (theta_hbm, theta),
        (base_hbm, base),
        (factor_hbm, factor_in),
        (eof_hbm, eof),
        (mode_hbm, mode),
        (tangent_hbm.at[0], tangent),
        (inner_hbm, inner_ref),
        (phase_hbm, phase_ref),
        (fourier_hbm, fourier_ref),
    ]
    loads = [pltpu.make_async_copy(src, dst, load_sem.at[i]) for i, (src, dst) in enumerate(pairs)]
    for copy in loads:
        copy.start()

    def put(src, dst, sems, target):
        return pltpu.make_async_remote_copy(
            src_ref=src, dst_ref=dst, send_sem=sems.at[0], recv_sem=sems.at[1], device_id=target, device_id_type=MESH
        )

    def signal_round(i):
        for target in lines[i + 1]:
            pl.semaphore_signal(round_sem.at[i], inc=1, device_id=target, device_id_type=MESH)

    for copy in loads[:5]:
        copy.wait()

    def screen(a, carry):
        cells = pl.ds(pl.multiple_of(a * 128, 128), 128)
        there = pl.ds(pl.multiple_of(g * 2048 + a * 128, 128), 128)
        turn = cos_sin(theta[:, there].astype(F32))
        value = mul((base[0, :, cells].astype(F32), base[1, :, cells].astype(F32)), turn)
        for part in range(4):
            depth = slice(8 * part, 8 * part + 8)
            quarter_out[part, a] = jnp.concatenate([value[0][depth], value[1][depth]], axis=0).astype(BF16)
        return carry

    lax.fori_loop(0, 16, screen, 0)

    for k in range(NBLK):
        for p in range(2):
            rows32[pl.ds(4 * k + 2 * p, 2), :] = factor_in[k, p].astype(F32)
    factors[...] = rows32[pl.ds(pl.multiple_of(core * 32, 32), 32), :].astype(BF16)
    chosen = lax.broadcasted_iota(jnp.int32, eof.shape, 1) == mode[0]
    column = jnp.sum(jnp.where(chosen, eof[...], 0.0), axis=1, keepdims=True)
    diagonal = lax.broadcasted_iota(jnp.int32, (ROWS, 128), 0) == lax.broadcasted_iota(jnp.int32, (ROWS, 128), 1)
    profile[...] = jnp.sum(jnp.where(diagonal, column, 0.0), axis=0, keepdims=True)

    for copy in loads[5:]:
        copy.wait()

    def load_tangent(c, a1, a2):
        depth = pl.ds(c * CH, CH)
        cells = pl.ds(pl.multiple_of((8 * a1 + a2) * 128, 128), 128)
        turn = cos_sin(theta[depth, cells].astype(F32))
        return mul((tangent[0, depth, cells].astype(F32), tangent[1, depth, cells].astype(F32)), turn)

    def store_tangent(c, a, value):
        for p in range(2):
            t_send[c, a, p] = value[p].astype(BF16)

    g_own, p_own = g_all.at[core, zh, x, y], p_all.at[zh, x, y]
    gx, px = g_all.at[core, :, x, y], p_all.at[:, x, y]
    gy, py = g_all.at[core, :, :, y], p_all.at[:, :, y]
    stages = [((factors, g_own), (profile, p_own)), ((gx, gx), (px, px)), ((gy, gy), (py, py))]
    g_half = put(g_all.at[core], g_all.at[core], g_sem.at[3], (core_mate, s))

    def gather_start(stage):
        for target in lines[stage]:
            for (src, dst), sem in zip(stages[stage], (g_sem, p_sem)):
                put(src, dst, sem.at[stage], target).start()

    def gather_wait(stage):
        for ref, sem in ((g_all.at[core], g_sem), (p_all, p_sem)):
            if stage == 0:
                part = ref.at[pl.ds(0, 3), 0, 0]
            elif stage == 1:
                part = ref.at[:, pl.ds(0, 3), 0]
            else:
                part = ref.at[:, :, pl.ds(0, 3)]
            put(part, part, sem.at[stage], lines[stage][0]).wait()

    t_land = [t_early, t_late]

    def t_move(c, i):
        target = partner(i)
        return put(t_send.at[c, target[1]], t_land[c].at[s], t_sem.at[c], target)

    def b_move(i):
        target = partner(i)
        return put(b_send.at[target[1]], b_all.at[g, s], b_sem, target)

    def start_all(move):
        def step(i, carry):
            move(i).start()
            return carry

        lax.fori_loop(1, SLAB, step, 0)

    def own(src, dst, i):
        return pltpu.make_async_copy(src, dst, own_sem.at[i])

    own_t = [own(t_send.at[c, s], t_land[c].at[s], c) for c in range(2)]
    own_b = own(b_send.at[s], b_all.at[g, s], 2)
    own_g = own(factors, g_own, 3)
    own_p = own(profile, p_own, 4)
    own_q = own(quarter_out.at[g], quarter_in.at[g], 5)

    tabs = (inner_ref, phase_ref, fourier_ref, work, mid)
    most = pl.ds(0, SLAB - 1)

    pl.semaphore_wait(barrier, 12)
    signal_round(0)
    for i in (1, 2, 3):
        put(quarter_out.at[in_grp(i)], quarter_in.at[g], q_sem, (in_grp(i), s)).start()
    own_q.start()
    gather_start(0)
    own_g.start()
    own_p.start()

    def second_round():
        pl.semaphore_wait(round_sem.at[0], 3)
        signal_round(1)

    cross_range(
        CH, functools.partial(load_tangent, 0), functools.partial(store_tangent, 0), *tabs, between=second_round
    )
    pl.semaphore_wait(round_sem.at[1], 3)
    start_all(functools.partial(t_move, 0))
    own_t[0].start()
    own_g.wait()
    own_p.wait()
    gather_wait(0)
    gather_start(1)

    own_q.wait()
    put(quarter_out.at[pl.ds(0, 3)], quarter_in.at[pl.ds(0, 3)], q_sem, (core_mate, s)).wait()

    def load_base(a1, a2):
        tile = quarter_in[a1 // 2, 8 * (a1 % 2) + a2].astype(F32)
        return (tile[:8], tile[8:])

    def store_base(a, value):
        b_send[a] = jnp.concatenate(value, axis=0).astype(BF16)

    cross_range(8, load_base, store_base, *tabs)
    start_all(b_move)
    own_b.start()
    cross_range(CH, functools.partial(load_tangent, 1), functools.partial(store_tangent, 1), *tabs)
    gather_wait(1)
    gather_start(2)
    early = put(t_send.at[0, most], t_early.at[most], t_sem.at[0], (core_mate, s))
    early.wait_send()
    start_all(functools.partial(t_move, 1))
    own_t[1].start()

    clear_ends(values)
    clear_ends(b_values)
    gather_wait(2)
    g_half.start()

    own_b.wait()
    put(b_send.at[most], b_all.at[0, most], b_sem, (core_mate, s)).wait()
    mine = b_all.at[g]
    to_core = put(mine, mine, bg_sem.at[0], (core_mate, s))
    to_far = put(mine, mine, bg_sem.at[1], (far_mate, s))
    to_far.start()
    to_core.start()

    def widen_profile(i, carry):
        column = jnp.sum(jnp.where(diagonal, p_all[i // 16, (i // 4) % 4, i % 4], 0.0), axis=1, keepdims=True)
        p_wide[pl.ds(pl.multiple_of(i * ROWS, ROWS), ROWS), :] = jnp.broadcast_to(column, (ROWS, 128))
        return carry

    lax.fori_loop(0, SLAB, widen_profile, 0)
    g_half.wait()

    def widen(i, carry):
        for h in range(2):
            rows = pl.ds(pl.multiple_of(h * 2048 + i * 32, 32), 32)
            spread32[rows, :] = g_all[h, i // 16, (i // 4) % 4, i % 4].astype(F32)
        return carry

    lax.fori_loop(0, SLAB, widen, 0)

    def arrange(k, carry):
        start = (k // 8) * 2048 + (k % 8) * 4
        for p in range(2):
            for r in range(2):
                blocks[p, pl.ds(r, 64, stride=2), :] = spread32[pl.ds(start + 2 * p + r, 64, stride=32), :]
        real = blocks[0]
        imag = blocks[1]
        upper = jnp.concatenate([real, -imag], axis=1)
        lower = jnp.concatenate([imag, real], axis=1)
        matrix[k, pl.ds(0, 128), :] = upper.astype(BF16)
        matrix[k, pl.ds(128, 128), :] = lower.astype(BF16)
        ends = []
        for row in (0, BLK - 1):
            ends += [upper[row : row + 1], lower[row : row + 1]]
        edge_lhs[k] = jnp.concatenate(ends + ends, axis=0).astype(BF16)
        points = []
        for row, col in ((0, 0), (BLK - 1, 0), (0, BLK - 1), (0, BLK - 1)):
            for p in range(2):
                points.append(jnp.broadcast_to(blocks[p, pl.ds(row, 1), pl.ds(col, 1)], (1, 128)))
        corner[k] = jnp.concatenate(points, axis=0)
        return carry

    lax.fori_loop(0, NBLK, arrange, 0)

    to_far.wait()
    theirs = b_all.at[far_mate]
    onward = put(theirs, theirs, bg_sem.at[2], (core_mate, s))
    onward.start()
    own_t[0].wait()
    early.wait_recv()
    to_core.wait()
    onward.wait()

    def combine(i, carry):
        for c in range(2):
            if c == 0:
                t_real = t_early[i, 0].astype(F32)
                t_imag = t_early[i, 1].astype(F32)
            for h in range(2):
                tile = b_all[2 * c + h, i].astype(F32)
                b_real, b_imag = tile[:8], tile[8:]
                at = CH * c + 8 * h
                scale = p_wide[pl.ds(pl.multiple_of(i * ROWS + at, 8), 8), :]
                here = pl.ds(pl.multiple_of(i * ROWS + at + 8, 8), 8)
                real = -scale * b_imag
                imag = scale * b_real
                if c == 0:
                    real += t_real[8 * h : 8 * h + 8]
                    imag += t_imag[8 * h : 8 * h + 8]
                values[0, here, :] = real
                values[1, here, :] = imag
                b_values[0, here, :] = b_real
                b_values[1, here, :] = b_imag
        return carry

    lax.fori_loop(0, SLAB, combine, 0, unroll=2)

    def store_done(f, p, here, result):
        done[f, p, here, :] = result

    outs = (t_next.at[0], b_next)

    def hand_out(f):
        def part(h):
            rows = pl.ds(h * (NZ // 2), NZ // 2)
            return pltpu.make_async_copy(done.at[f, :, rows], outs[f].at[:, rows], done_sem.at[2 * f + h])

        halves = [part(h) for h in range(2)]
        for h in range(2):
            finish(matrix, rhs, functools.partial(store_done, f), h * (NBLK // 2), NBLK // 2)
            halves[h].start()
        return halves

    right_side(b_values, edge_lhs, rhs, edge)
    recur(edge, corner, rhs)
    base_out = hand_out(1)

    own_t[1].wait()
    put(t_send.at[1, most], t_late.at[most], t_sem.at[1], (core_mate, s)).wait()

    def add_late(i, carry):
        for p in range(2):
            here = pl.ds(pl.multiple_of(i * ROWS + CH + 8, 8), CH)
            values[p, here, :] += t_late[i, p].astype(F32)
        return carry

    lax.fori_loop(0, SLAB, add_late, 0, unroll=4)
    right_side(values, edge_lhs, rhs, edge)
    recur(edge, corner, rhs)
    tangent_out = hand_out(0)
    for copy in base_out + tangent_out:
        copy.wait()


def copy_kernel(t_in, b_in, t_out, b_out, sem):
    copies = []
    for p in range(2):
        copies.append(pltpu.make_async_copy(t_in.at[0, p], t_out.at[0, p], sem.at[p]))
        copies.append(pltpu.make_async_copy(b_in.at[p], b_out.at[p], sem.at[2 + p]))
    for copy in copies:
        copy.start()
    for copy in copies:
        copy.wait()


def on_device(tangent, base, theta, eof_table, mode_of_field, block_factors):
    phases, fourier, inner = tables()
    in_hbm = pl.BlockSpec(memory_space=pltpu.HBM)
    anywhere = pl.BlockSpec(memory_space=ANY)
    smem = pltpu.SMEM
    dma = pltpu.SemaphoreType.DMA
    shape = jax.ShapeDtypeStruct
    results = (shape((1, 2, NZ, 128), BF16), shape((2, NZ, 128), BF16))
    handed = pl.pallas_call(
        exchange_kernel,
        out_shape=results,
        in_specs=[in_hbm] * 9,
        out_specs=(anywhere, anywhere),
        scratch_shapes=[
            VMEM((SLAB, 2, CH, 128), BF16),
            VMEM((2, NZ + 16, 128), F32),
            VMEM((NBLK, 256, 256), BF16),
            VMEM((NBLK, 8, 256), BF16),
            VMEM((NBLK, 8, 128), F32),
            VMEM((2, 2, NZ, 128), BF16),
            VMEM((2, ROWS, NY), BF16),
            VMEM((2, ROWS, NY // 4), BF16),
            VMEM((ROWS, NY), BF16),
            VMEM((ROWS, 112), F32),
            smem((1,), jnp.int32),
            VMEM((NBLK, 2, 2, 128), BF16),
            smem((8, 16), F32),
            VMEM((4, R1, 1, R2), F32),
            VMEM((2, 256, 256), BF16),
            VMEM((4, 16, 16, 128), BF16),
            VMEM((4, 16, 16, 128), BF16),
            VMEM((R1, 2, CH, 128), F32),
            VMEM((R1, CH, 256), F32),
            VMEM((2, SLAB, 2, CH, 128), BF16),
            VMEM((SLAB, 16, 128), BF16),
            VMEM((64, 128), F32),
            VMEM((32, 128), BF16),
            VMEM((1, 128), F32),
            VMEM((SLAB, 2, CH, 128), BF16),
            VMEM((GRP, SLAB, 16, 128), BF16),
            VMEM((2, 4, 4, 4, 32, 128), BF16),
            VMEM((4, 4, 4, 1, 128), F32),
            VMEM((NZ, 128), F32),
            VMEM((4096, 128), F32),
            VMEM((2, BLK, 128), F32),
            VMEM((2, NZ + 16, 128), F32),
            VMEM((NBLK, 256, 128), F32),
            VMEM((NBLK, 8, 128), F32),
            dma((9,)),
            dma((6,)),
            dma((2,)),
            dma((2, 2)),
            dma((2,)),
            dma((3, 2)),
            dma((4, 2)),
            dma((3, 2)),
            pltpu.SemaphoreType.REGULAR((2,)),
            dma((4,)),
        ],
        compiler_params=pltpu.CompilerParams(
            collective_id=0, has_side_effects=True, vmem_limit_bytes=56 * 2**20
        ),
        name="exchange",
    )(
        tangent,
        base,
        theta,
        eof_table.T,
        mode_of_field,
        block_factors,
        jnp.asarray(inner),
        jnp.asarray(phases),
        jnp.asarray(fourier),
    )
    return pl.pallas_call(
        copy_kernel,
        out_shape=results,
        in_specs=[anywhere] * 2,
        out_specs=(anywhere, anywhere),
        scratch_shapes=[dma((4,))],
        compiler_params=pltpu.CompilerParams(vmem_limit_bytes=56 * 2**20),
        name="hand_over",
    )(*handed)


def solution(mesh):
    in_specs = (
        P("grp", None, "slab", None),
        P(None, "slab", "grp"),
        P("slab", None),
        P(None, "slab"),
        P("grp"),
        P(None, None, "slab", None),
    )
    out_specs = (P("grp", None, None, "slab"), P(None, None, "slab"))
    return jax.shard_map(on_device, mesh=mesh, in_specs=in_specs, out_specs=out_specs, check_vma=False)
```

```python
import functools
import math

import jax
import jax.numpy as jnp
import ml_dtypes
import numpy as np
from jax import lax
from jax.experimental import pallas as pl
from jax.experimental.pallas import tpu as pltpu
from jax.sharding import PartitionSpec as P

MESH = pl.DeviceIdType.MESH
NZ = 2048
NY = 8192
R1 = 64
R2 = 128
NBLK = 16
BLK = 128
SLAB = 64
GRP = 4
ROWS = 32
CH = 16
ALPHA_REAL = 0.15
ALPHA_IMAG = 0.1
COUPLE_REAL = 0.35
COUPLE_IMAG = -0.25
VMEM = pltpu.VMEM
ANY = pl.ANY
F32 = jnp.float32
BF16 = jnp.bfloat16


def trig_coefficients():
    nodes = np.cos(np.pi * (np.arange(64) + 0.5) / 64)
    square = (nodes + 1.0) * 0.5 * math.pi**2
    root = np.sqrt(square)
    cheb = np.polynomial.chebyshev
    sine = cheb.cheb2poly(cheb.chebfit(nodes, np.sin(root) / root, 7))
    cosine = cheb.cheb2poly(cheb.chebfit(nodes, np.cos(root), 8))

    def in_square(coefs):
        total = np.zeros(1)
        shift = np.array([-1.0, 2.0 / math.pi**2])
        power = np.ones(1)
        for coef in coefs:
            total = np.polynomial.polynomial.polyadd(total, coef * power)
            power = np.polynomial.polynomial.polymul(power, shift)
        return [float(v) for v in total]

    return in_square(sine), in_square(cosine)


SIN_COEFS, COS_COEFS = trig_coefficients()


def tables():
    k1 = np.arange(R1)
    b = np.arange(R2)
    angle = -2.0 * np.pi * ((k1[:, None] * b[None, :]) % NY) / NY
    wave = k1[:, None] + R1 * b[None, :]
    signed = np.where(wave < NY // 2, wave, wave - NY)
    kernel_angle = -np.pi * ((signed * signed) % (2 * NY)) / NY
    phases = np.stack([np.cos(angle), np.sin(angle), np.cos(kernel_angle), np.sin(kernel_angle)])
    phases = phases.astype(np.float32).reshape(4, R1, 1, R2)
    turn = 2.0 * np.pi * ((b[:, None] * b[None, :]) % R2) / R2
    c = np.cos(turn).astype(ml_dtypes.bfloat16).astype(np.float32)
    s = np.sin(turn).astype(ml_dtypes.bfloat16).astype(np.float32)
    forward = np.block([[c, -s], [s, c]])
    backward = np.block([[c, s], [-s, c]])
    fourier = np.stack([forward, backward]).astype(ml_dtypes.bfloat16)
    eight = np.arange(8)
    inner = -2.0 * np.pi * (eight[:, None] * eight[None, :]) / 64.0
    inner = np.concatenate([np.cos(inner), np.sin(inner)], axis=1).astype(np.float32)
    return phases, fourier, inner


def add(p, q):
    return (p[0] + q[0], p[1] + q[1])


def sub(p, q):
    return (p[0] - q[0], p[1] - q[1])


def mul(p, q):
    return (p[0] * q[0] - p[1] * q[1], p[0] * q[1] + p[1] * q[0])


def quarter(p, sign):
    return (-p[1], p[0]) if sign > 0 else (p[1], -p[0])


def dft8(x, sign):
    half = math.sqrt(0.5)

    def four(a, b, c, d):
        e0, e1 = add(a, c), sub(a, c)
        o0, o1 = add(b, d), quarter(sub(b, d), sign)
        return add(e0, o0), add(e1, o1), sub(e0, o0), sub(e1, o1)

    e = four(x[0], x[2], x[4], x[6])
    o = four(x[1], x[3], x[5], x[7])
    u1 = quarter(o[1], sign)
    u3 = quarter(o[3], sign)
    o1 = ((o[1][0] + u1[0]) * half, (o[1][1] + u1[1]) * half)
    o2 = quarter(o[2], sign)
    o3 = ((u3[0] - o[3][0]) * half, (u3[1] - o[3][1]) * half)
    o = (o[0], o1, o2, o3)
    return [add(e[i], o[i]) for i in range(4)] + [sub(e[i], o[i]) for i in range(4)]


def cos_sin(theta):
    u = theta * theta
    s = SIN_COEFS[-1]
    for coef in SIN_COEFS[-2::-1]:
        s = s * u + coef
    c = COS_COEFS[-1]
    for coef in COS_COEFS[-2::-1]:
        c = c * u + coef
    return c, s * theta


def cross_range(rows, load, store, inner_ref, phase_ref, fourier_ref, work, mid, between=None):
    def twist(index, sign):
        return [None] + [(inner_ref[index, k], sign * inner_ref[index, 8 + k]) for k in range(1, 8)]

    def forward_one(a2, carry):
        out = dft8([load(a1, a2) for a1 in range(8)], -1)
        factors = twist(a2, 1.0)
        for k in range(8):
            value = out[k] if k == 0 else mul(out[k], factors[k])
            for p in range(2):
                work[a2 * 8 + k, p, pl.ds(0, rows), :] = value[p]
        return carry

    lax.fori_loop(0, 8, forward_one, 0)

    def forward_two(k, carry):
        values = [tuple(work[a2 * 8 + k, p, pl.ds(0, rows), :] for p in range(2)) for a2 in range(8)]
        out = dft8(values, -1)
        for kk in range(8):
            k1 = k + 8 * kk
            value = mul(out[kk], (phase_ref[0, k1], phase_ref[1, k1]))
            for p in range(2):
                mid[k1, pl.ds(0, rows), pl.ds(128 * p, 128)] = value[p]
        return carry

    lax.fori_loop(0, 8, forward_two, 0)
    if between is not None:
        between()

    def inner(i, carry):
        part = pl.ds(i * 16, 16)
        y = mid[part, pl.ds(0, rows), :].reshape(16 * rows, 256).astype(BF16)
        y = jnp.dot(y, fourier_ref[0], preferred_element_type=F32).reshape(16, rows, 256)
        y = mul((y[:, :, :128], y[:, :, 128:]), (phase_ref[2, part], phase_ref[3, part]))
        y = jnp.concatenate(y, axis=2).reshape(16 * rows, 256).astype(BF16)
        y = jnp.dot(y, fourier_ref[1], preferred_element_type=F32).reshape(16, rows, 256)
        y = mul((y[:, :, :128], y[:, :, 128:]), (phase_ref[0, part], -phase_ref[1, part]))
        for p in range(2):
            work[part, p, pl.ds(0, rows), :] = y[p]
        return carry

    lax.fori_loop(0, 4, inner, 0)

    def backward_one(k2, carry):
        values = [tuple(work[8 * q + k2, p, pl.ds(0, rows), :] for p in range(2)) for q in range(8)]
        out = dft8(values, 1)
        factors = twist(k2, -1.0)
        for a in range(8):
            value = out[a] if a == 0 else mul(out[a], factors[a])
            for p in range(2):
                mid[k2 * 8 + a, pl.ds(0, rows), pl.ds(128 * p, 128)] = value[p]
        return carry

    lax.fori_loop(0, 8, backward_one, 0)

    def backward_two(a, carry):
        values = [
            tuple(mid[k2 * 8 + a, pl.ds(0, rows), pl.ds(128 * p, 128)] for p in range(2)) for k2 in range(8)
        ]
        out = dft8(values, 1)
        for aa in range(8):
            store(a + 8 * aa, (out[aa][0] * (1.0 / NY), out[aa][1] * (1.0 / NY)))
        return carry

    lax.fori_loop(0, 8, backward_two, 0)


def clear_ends(values):
    zeros = jnp.zeros((2, 8, 128), F32)
    values[:, pl.ds(0, 8), :] = zeros
    values[:, pl.ds(NZ + 8, 8), :] = zeros


def right_side(values, edge_lhs, rhs, edge):
    def step(k, carry):
        pairs = []
        for p in range(2):
            centre = values[p, pl.ds(pl.multiple_of(k * BLK + 8, 8), BLK), :]
            above = values[p, pl.ds(k * BLK + 7, BLK), :]
            below = values[p, pl.ds(k * BLK + 9, BLK), :]
            pairs.append((centre, above + below - 2.0 * centre))
        (c_real, d_real), (c_imag, d_imag) = pairs
        r_real = c_real + ALPHA_REAL * d_real - ALPHA_IMAG * d_imag
        r_imag = c_imag + ALPHA_REAL * d_imag + ALPHA_IMAG * d_real
        rhs[k, pl.ds(0, BLK), :] = r_real
        rhs[k, pl.ds(BLK, BLK), :] = r_imag
        both = jnp.concatenate([r_real.astype(BF16), r_imag.astype(BF16)], axis=0)
        edge[k] = jnp.dot(edge_lhs[k], both, preferred_element_type=F32)
        return carry

    lax.fori_loop(0, NBLK, step, 0, unroll=2)


def recur(edge, corner, rhs):
    couple = (COUPLE_REAL, COUPLE_IMAG)

    def entry(k, i):
        return tuple(corner[k, pl.ds(2 * i + p, 1), :] for p in range(2))

    def row_of(k, i):
        return tuple(edge[k, pl.ds(i + p, 1), :] for p in range(2))

    starts = []
    held = None
    for k in range(NBLK):
        first, last = row_of(k, 0), row_of(k, 2)
        if held is not None:
            scaled = mul(held, couple)
            for p in range(2):
                rhs[k, pl.ds(BLK * p, 1), :] -= scaled[p]
            first = sub(first, mul(scaled, entry(k, 0)))
            last = sub(last, mul(scaled, entry(k, 1)))
        starts.append(first)
        held = last
    held = None
    for k in range(NBLK - 1, -1, -1):
        value = starts[k]
        if held is not None:
            scaled = mul(held, couple)
            for p in range(2):
                rhs[k, pl.ds(BLK * p + BLK - 1, 1), :] -= scaled[p]
            value = sub(value, mul(scaled, entry(k, 2)))
        held = value


def finish(matrix, rhs, store, begin, count):
    def step(i, carry):
        k = begin + i
        result = jnp.dot(matrix[k], rhs[k].astype(BF16), preferred_element_type=F32).astype(BF16)
        here = pl.ds(pl.multiple_of(k * BLK, BLK), BLK)
        for p in range(2):
            store(p, here, result[128 * p : 128 * p + 128])
        return carry

    lax.fori_loop(0, count, step, 0, unroll=2)


def exchange_kernel(
    tangent_hbm,
    base_hbm,
    theta_hbm,
    eof_hbm,
    mode_hbm,
    factor_hbm,
    inner_hbm,
    phase_hbm,
    fourier_hbm,
    t_next,
    b_next,
    t_late,
    values,
    matrix,
    edge_lhs,
    corner,
    done,
    tangent,
    base,
    theta,
    eof,
    mode,
    factor_in,
    inner_ref,
    phase_ref,
    fourier_ref,
    quarter_out,
    quarter_in,
    work,
    mid,
    t_send,
    b_send,
    rows32,
    factors,
    profile,
    t_early,
    b_all,
    g_all,
    p_all,
    p_wide,
    spread32,
    blocks,
    b_values,
    rhs,
    edge,
    load_sem,
    own_sem,
    q_sem,
    t_sem,
    b_sem,
    fw_sem,
    cx_sem,
    g_sem,
    p_sem,
    round_sem,
    done_sem,
):
    g = lax.axis_index("grp")
    s = lax.axis_index("slab")
    zh, x, y = s // 16, (s // 4) % 4, s % 4
    core = g % 2

    def at_slab(dz, dx, dy):
        return (g, ((zh + dz) % 4) * 16 + ((x + dx) % 4) * 4 + (y + dy) % 4)

    def partner(i):
        return at_slab(i % 4, (i // 4) % 4, i // 16)

    def in_grp(i):
        mate = g + 1 - 2 * (g % 2) if i % 2 else g
        return (mate + 2) % 4 if i // 2 else mate

    core_mate = in_grp(1)
    far_mate = in_grp(2)
    lines = [[at_slab(i, 0, 0) for i in (1, 2, 3)], [at_slab(0, i, 0) for i in (1, 2, 3)], [at_slab(0, 0, i) for i in (1, 2, 3)]]
    grp_line = [(in_grp(i), s) for i in (1, 2, 3)]

    barrier = pltpu.get_barrier_semaphore()
    for target in lines[0] + lines[1] + lines[2] + grp_line:
        pl.semaphore_signal(barrier, inc=1, device_id=target, device_id_type=MESH)

    pairs = [
        (theta_hbm, theta),
        (base_hbm, base),
        (factor_hbm, factor_in),
        (eof_hbm, eof),
        (mode_hbm, mode),
        (tangent_hbm.at[0], tangent),
        (inner_hbm, inner_ref),
        (phase_hbm, phase_ref),
        (fourier_hbm, fourier_ref),
    ]
    loads = [pltpu.make_async_copy(src, dst, load_sem.at[i]) for i, (src, dst) in enumerate(pairs)]
    for copy in loads:
        copy.start()

    def put(src, dst, sems, target):
        return pltpu.make_async_remote_copy(
            src_ref=src, dst_ref=dst, send_sem=sems.at[0], recv_sem=sems.at[1], device_id=target, device_id_type=MESH
        )

    def signal_round(i):
        for target in lines[i + 1]:
            pl.semaphore_signal(round_sem.at[i], inc=1, device_id=target, device_id_type=MESH)

    for copy in loads[:5]:
        copy.wait()

    def screen(a, carry):
        cells = pl.ds(pl.multiple_of(a * 128, 128), 128)
        there = pl.ds(pl.multiple_of(g * 2048 + a * 128, 128), 128)
        turn = cos_sin(theta[:, there].astype(F32))
        value = mul((base[0, :, cells].astype(F32), base[1, :, cells].astype(F32)), turn)
        for c in range(2):
            for p in range(2):
                quarter_out[c, a, p] = value[p][CH * c : CH * c + CH].astype(BF16)
        return carry

    lax.fori_loop(0, 16, screen, 0)

    for k in range(NBLK):
        for p in range(2):
            rows32[pl.ds(4 * k + 2 * p, 2), :] = factor_in[k, p].astype(F32)
    factors[...] = rows32[pl.ds(pl.multiple_of(core * 32, 32), 32), :].astype(BF16)
    chosen = lax.broadcasted_iota(jnp.int32, eof.shape, 1) == mode[0]
    column = jnp.sum(jnp.where(chosen, eof[...], 0.0), axis=1, keepdims=True)
    diagonal = lax.broadcasted_iota(jnp.int32, (ROWS, 128), 0) == lax.broadcasted_iota(jnp.int32, (ROWS, 128), 1)
    profile[...] = jnp.sum(jnp.where(diagonal, column, 0.0), axis=0, keepdims=True)

    for copy in loads[5:]:
        copy.wait()

    def load_tangent(c, a1, a2):
        depth = pl.ds(c * CH, CH)
        cells = pl.ds(pl.multiple_of((8 * a1 + a2) * 128, 128), 128)
        turn = cos_sin(theta[depth, cells].astype(F32))
        return mul((tangent[0, depth, cells].astype(F32), tangent[1, depth, cells].astype(F32)), turn)

    def store_tangent(c, a, value):
        for p in range(2):
            t_send[c, a, p] = value[p].astype(BF16)

    g_own, p_own = g_all.at[core, zh, x, y], p_all.at[zh, x, y]
    gx, px = g_all.at[core, :, x, y], p_all.at[:, x, y]
    gy, py = g_all.at[core, :, :, y], p_all.at[:, :, y]
    stages = [((factors, g_own), (profile, p_own)), ((gx, gx), (px, px)), ((gy, gy), (py, py))]
    g_half = put(g_all.at[core], g_all.at[core], g_sem.at[3], (core_mate, s))

    def gather_start(stage):
        for target in lines[stage]:
            for (src, dst), sem in zip(stages[stage], (g_sem, p_sem)):
                put(src, dst, sem.at[stage], target).start()

    def gather_wait(stage):
        for ref, sem in ((g_all.at[core], g_sem), (p_all, p_sem)):
            if stage == 0:
                part = ref.at[pl.ds(0, 3), 0, 0]
            elif stage == 1:
                part = ref.at[:, pl.ds(0, 3), 0]
            else:
                part = ref.at[:, :, pl.ds(0, 3)]
            put(part, part, sem.at[stage], lines[stage][0]).wait()

    t_land = [t_early, t_late]

    def t_move(c, i):
        target = partner(i)
        return put(t_send.at[c, target[1]], t_land[c].at[s], t_sem.at[c], target)

    up = g // 2
    near_step = 3 - 2 * up
    near_from = (zh + 2 * up + 3) % 4
    other_from = (near_from + 2) % 4
    across_from = (zh + 2) % 4

    def plane_move(i):
        target = at_slab(0, i % 4, i // 4)
        return put(b_send.at[target[1]], b_all.at[core, s], b_sem.at[0], target)

    def near_move(i):
        cells = at_slab(near_step, i % 4, i // 4)[1]
        return put(b_send.at[cells], b_all.at[core, s], b_sem.at[1], (far_mate, cells))

    def across_move(i):
        cells = at_slab(2, i % 4, i // 4)[1]
        return put(b_send.at[cells], b_all.at[core, s], b_sem.at[2], (far_mate, cells))

    def layer(index):
        return b_all.at[core, pl.ds(index * 16, 16)]

    def layer_move(index, sems, target):
        return put(layer(index), layer(index), sems, (target, s))

    def start_all(move, begin=1, end=SLAB):
        def step(i, carry):
            move(i).start()
            return carry

        lax.fori_loop(begin, end, step, 0)

    def own(src, dst, i):
        return pltpu.make_async_copy(src, dst, own_sem.at[i])

    own_t = [own(t_send.at[c, s], t_land[c].at[s], c) for c in range(2)]
    own_b = own(b_send.at[s], b_all.at[core, s], 2)
    own_g = own(factors, g_own, 3)
    own_p = own(profile, p_own, 4)
    own_q = own(quarter_out.at[core], quarter_in.at[g], 5)

    tabs = (inner_ref, phase_ref, fourier_ref, work, mid)
    most = pl.ds(0, SLAB - 1)

    pl.semaphore_wait(barrier, 12)
    signal_round(0)
    for i in (1, 2, 3):
        put(quarter_out.at[in_grp(i) % 2], quarter_in.at[g], q_sem, (in_grp(i), s)).start()
    own_q.start()
    gather_start(0)
    own_g.start()
    own_p.start()

    def second_round():
        pl.semaphore_wait(round_sem.at[0], 3)
        signal_round(1)

    cross_range(
        CH, functools.partial(load_tangent, 0), functools.partial(store_tangent, 0), *tabs, between=second_round
    )
    pl.semaphore_wait(round_sem.at[1], 3)
    pl.semaphore_signal(round_sem.at[2], inc=1, device_id=(far_mate, s), device_id_type=MESH)
    start_all(functools.partial(t_move, 0))
    own_t[0].start()
    own_g.wait()
    own_p.wait()
    gather_wait(0)
    gather_start(1)

    cross_range(CH, functools.partial(load_tangent, 1), functools.partial(store_tangent, 1), *tabs)
    gather_wait(1)
    gather_start(2)
    own_q.wait()
    put(quarter_in.at[pl.ds(0, 3)], quarter_in.at[pl.ds(0, 3)], q_sem, (core_mate, s)).wait()

    def load_base(a1, a2):
        return tuple(quarter_in[a1 // 2, 8 * (a1 % 2) + a2, p].astype(F32) for p in range(2))

    def store_base(a, value):
        for p in range(2):
            b_send[a, p] = value[p].astype(BF16)

    cross_range(CH, load_base, store_base, *tabs)
    pl.semaphore_wait(round_sem.at[2], 1)

    @pl.when(up + core == 1)
    def _():
        start_all(across_move, 0, 16)

    start_all(near_move, 0, 16)
    start_all(plane_move, 1, 16)
    own_b.start()
    start_all(functools.partial(t_move, 1))
    own_t[1].start()

    clear_ends(values)
    clear_ends(b_values)
    gather_wait(2)
    g_half.start()

    def widen_profile(i, carry):
        column = jnp.sum(jnp.where(diagonal, p_all[i // 16, (i // 4) % 4, i % 4], 0.0), axis=1, keepdims=True)
        p_wide[pl.ds(pl.multiple_of(i * ROWS, ROWS), ROWS), :] = jnp.broadcast_to(column, (ROWS, 128))
        return carry

    lax.fori_loop(0, SLAB, widen_profile, 0)
    g_half.wait()

    def widen(i, carry):
        for h in range(2):
            rows = pl.ds(pl.multiple_of(h * 2048 + i * 32, 32), 32)
            spread32[rows, :] = g_all[h, i // 16, (i // 4) % 4, i % 4].astype(F32)
        return carry

    lax.fori_loop(0, SLAB, widen, 0)

    def arrange(k, carry):
        start = (k // 8) * 2048 + (k % 8) * 4
        for p in range(2):
            for r in range(2):
                blocks[p, pl.ds(r, 64, stride=2), :] = spread32[pl.ds(start + 2 * p + r, 64, stride=32), :]
        real = blocks[0]
        imag = blocks[1]
        upper = jnp.concatenate([real, -imag], axis=1)
        lower = jnp.concatenate([imag, real], axis=1)
        matrix[k, pl.ds(0, 128), :] = upper.astype(BF16)
        matrix[k, pl.ds(128, 128), :] = lower.astype(BF16)
        ends = []
        for row in (0, BLK - 1):
            ends += [upper[row : row + 1], lower[row : row + 1]]
        edge_lhs[k] = jnp.concatenate(ends + ends, axis=0).astype(BF16)
        points = []
        for row, col in ((0, 0), (BLK - 1, 0), (0, BLK - 1), (0, BLK - 1)):
            for p in range(2):
                points.append(jnp.broadcast_to(blocks[p, pl.ds(row, 1), pl.ds(col, 1)], (1, 128)))
        corner[k] = jnp.concatenate(points, axis=0)
        return carry

    lax.fori_loop(0, NBLK, arrange, 0)

    crossing = [layer_move(i, cx_sem.at[k], core_mate) for k, i in enumerate((zh, near_from, across_from, other_from))]
    near_on = layer_move(near_from, fw_sem.at[0], far_mate)
    across_on = layer_move(across_from, fw_sem.at[1], far_mate)
    sixteen = pl.ds(0, 16)
    near_all = put(b_send.at[sixteen], b_all.at[0, sixteen], b_sem.at[1], (far_mate, s))
    near_all.wait()
    near_on.start()
    crossing[1].start()
    across_all = put(b_send.at[sixteen], b_all.at[0, sixteen], b_sem.at[2], (far_mate, s))

    @pl.when(up == core)
    def _():
        across_all.wait_recv()
        across_on.start()
        crossing[2].start()

    own_b.wait()
    fifteen = pl.ds(0, 15)
    put(b_send.at[fifteen], b_all.at[0, fifteen], b_sem.at[0], (core_mate, s)).wait()
    crossing[0].start()
    near_on.wait()
    crossing[3].start()

    @pl.when(up == core)
    def _():
        across_on.wait_send()

    @pl.when(up + core == 1)
    def _():
        across_all.wait_send()
        across_on.wait_recv()
        crossing[2].start()

    own_t[0].wait()
    early = put(t_send.at[0, most], t_early.at[most], t_sem.at[0], (core_mate, s))
    early.wait()
    for move in crossing:
        move.wait()

    def combine(i, carry):
        for c in range(2):
            scale = p_wide[pl.ds(pl.multiple_of(i * ROWS + CH * c, CH), CH), :]
            here = pl.ds(pl.multiple_of(i * ROWS + CH * c + 8, 8), CH)
            b_real = b_all[c, i, 0].astype(F32)
            b_imag = b_all[c, i, 1].astype(F32)
            real = -scale * b_imag
            imag = scale * b_real
            if c == 0:
                real += t_early[i, 0].astype(F32)
                imag += t_early[i, 1].astype(F32)
            values[0, here, :] = real
            values[1, here, :] = imag
            b_values[0, here, :] = b_real
            b_values[1, here, :] = b_imag
        return carry

    lax.fori_loop(0, SLAB, combine, 0, unroll=2)

    def store_done(f, p, here, result):
        done[f, p, here, :] = result

    outs = (t_next.at[0], b_next)

    def hand_out(f):
        def part(h):
            rows = pl.ds(h * (NZ // 2), NZ // 2)
            return pltpu.make_async_copy(done.at[f, :, rows], outs[f].at[:, rows], done_sem.at[2 * f + h])

        halves = [part(h) for h in range(2)]
        for h in range(2):
            finish(matrix, rhs, functools.partial(store_done, f), h * (NBLK // 2), NBLK // 2)
            halves[h].start()
        return halves

    right_side(b_values, edge_lhs, rhs, edge)
    recur(edge, corner, rhs)
    base_out = hand_out(1)

    own_t[1].wait()
    put(t_send.at[1, most], t_late.at[most], t_sem.at[1], (core_mate, s)).wait()

    def add_late(i, carry):
        for p in range(2):
            here = pl.ds(pl.multiple_of(i * ROWS + CH + 8, 8), CH)
            values[p, here, :] += t_late[i, p].astype(F32)
        return carry

    lax.fori_loop(0, SLAB, add_late, 0, unroll=4)
    right_side(values, edge_lhs, rhs, edge)
    recur(edge, corner, rhs)
    tangent_out = hand_out(0)
    for copy in base_out + tangent_out:
        copy.wait()


def copy_kernel(t_in, b_in, t_out, b_out, held, sem):
    arrivals = []
    leaves = []
    for f, (src, dst) in enumerate(((t_in.at[0], t_out.at[0]), (b_in, b_out))):
        for p in range(2):
            for h in range(2):
                rows = pl.ds(h * (NZ // 2), NZ // 2)
                i = 4 * f + 2 * p + h
                arrivals.append(pltpu.make_async_copy(src.at[p, rows], held.at[i], sem.at[0, i]))
                leaves.append(pltpu.make_async_copy(held.at[i], dst.at[p, rows], sem.at[1, i]))
    for copy in arrivals:
        copy.start()
    for arrival, leave in zip(arrivals, leaves):
        arrival.wait()
        leave.start()
    for leave in leaves:
        leave.wait()


def on_device(tangent, base, theta, eof_table, mode_of_field, block_factors):
    phases, fourier, inner = tables()
    in_hbm = pl.BlockSpec(memory_space=pltpu.HBM)
    anywhere = pl.BlockSpec(memory_space=ANY)
    smem = pltpu.SMEM
    dma = pltpu.SemaphoreType.DMA
    shape = jax.ShapeDtypeStruct
    results = (shape((1, 2, NZ, 128), BF16), shape((2, NZ, 128), BF16))
    handed = pl.pallas_call(
        exchange_kernel,
        out_shape=results,
        in_specs=[in_hbm] * 9,
        out_specs=(anywhere, anywhere),
        scratch_shapes=[
            VMEM((SLAB, 2, CH, 128), BF16),
            VMEM((2, NZ + 16, 128), F32),
            VMEM((NBLK, 256, 256), BF16),
            VMEM((NBLK, 8, 256), BF16),
            VMEM((NBLK, 8, 128), F32),
            VMEM((2, 2, NZ, 128), BF16),
            VMEM((2, ROWS, NY), BF16),
            VMEM((2, ROWS, NY // 4), BF16),
            VMEM((ROWS, NY), BF16),
            VMEM((ROWS, 112), F32),
            smem((1,), jnp.int32),
            VMEM((NBLK, 2, 2, 128), BF16),
            smem((8, 16), F32),
            VMEM((4, R1, 1, R2), F32),
            VMEM((2, 256, 256), BF16),
            VMEM((2, 16, 2, CH, 128), BF16),
            VMEM((4, 16, 2, CH, 128), BF16),
            VMEM((R1, 2, CH, 128), F32),
            VMEM((R1, CH, 256), F32),
            VMEM((2, SLAB, 2, CH, 128), BF16),
            VMEM((SLAB, 2, CH, 128), BF16),
            VMEM((64, 128), F32),
            VMEM((32, 128), BF16),
            VMEM((1, 128), F32),
            VMEM((SLAB, 2, CH, 128), BF16),
            VMEM((2, SLAB, 2, CH, 128), BF16),
            VMEM((2, 4, 4, 4, 32, 128), BF16),
            VMEM((4, 4, 4, 1, 128), F32),
            VMEM((NZ, 128), F32),
            VMEM((4096, 128), F32),
            VMEM((2, BLK, 128), F32),
            VMEM((2, NZ + 16, 128), F32),
            VMEM((NBLK, 256, 128), F32),
            VMEM((NBLK, 8, 128), F32),
            dma((9,)),
            dma((6,)),
            dma((2,)),
            dma((2, 2)),
            dma((3, 2)),
            dma((2, 2)),
            dma((4, 2)),
            dma((4, 2)),
            dma((3, 2)),
            pltpu.SemaphoreType.REGULAR((3,)),
            dma((4,)),
        ],
        compiler_params=pltpu.CompilerParams(
            collective_id=0, has_side_effects=True, vmem_limit_bytes=56 * 2**20
        ),
        name="exchange",
    )(
        tangent,
        base,
        theta,
        eof_table.T,
        mode_of_field,
        block_factors,
        jnp.asarray(inner),
        jnp.asarray(phases),
        jnp.asarray(fourier),
    )
    return pl.pallas_call(
        copy_kernel,
        out_shape=results,
        in_specs=[anywhere] * 2,
        out_specs=(anywhere, anywhere),
        scratch_shapes=[VMEM((8, NZ // 2, 128), BF16), dma((2, 8))],
        compiler_params=pltpu.CompilerParams(vmem_limit_bytes=56 * 2**20),
        name="hand_over",
    )(*handed)


def solution(mesh):
    in_specs = (
        P("grp", None, "slab", None),
        P(None, "slab", "grp"),
        P("slab", None),
        P(None, "slab"),
        P("grp"),
        P(None, None, "slab", None),
    )
    out_specs = (P("grp", None, None, "slab"), P(None, None, "slab"))
    return jax.shard_map(on_device, mesh=mesh, in_specs=in_specs, out_specs=out_specs, check_vma=False)
```

```python
import functools
import math

import jax
import jax.numpy as jnp
import ml_dtypes
import numpy as np
from jax import lax
from jax.experimental import pallas as pl
from jax.experimental.pallas import tpu as pltpu
from jax.sharding import PartitionSpec as P

MESH = pl.DeviceIdType.MESH
NZ = 2048
NY = 8192
R1 = 64
R2 = 128
NBLK = 16
BLK = 128
SLAB = 64
GRP = 4
ROWS = 32
CH = 16
ALPHA_REAL = 0.15
ALPHA_IMAG = 0.1
COUPLE_REAL = 0.35
COUPLE_IMAG = -0.25
VMEM = pltpu.VMEM
ANY = pl.ANY
F32 = jnp.float32
BF16 = jnp.bfloat16


def trig_coefficients():
    nodes = np.cos(np.pi * (np.arange(64) + 0.5) / 64)
    square = (nodes + 1.0) * 0.5 * math.pi**2
    root = np.sqrt(square)
    cheb = np.polynomial.chebyshev
    sine = cheb.cheb2poly(cheb.chebfit(nodes, np.sin(root) / root, 7))
    cosine = cheb.cheb2poly(cheb.chebfit(nodes, np.cos(root), 8))

    def in_square(coefs):
        total = np.zeros(1)
        shift = np.array([-1.0, 2.0 / math.pi**2])
        power = np.ones(1)
        for coef in coefs:
            total = np.polynomial.polynomial.polyadd(total, coef * power)
            power = np.polynomial.polynomial.polymul(power, shift)
        return [float(v) for v in total]

    return in_square(sine), in_square(cosine)


SIN_COEFS, COS_COEFS = trig_coefficients()


def tables():
    k1 = np.arange(R1)
    b = np.arange(R2)
    angle = -2.0 * np.pi * ((k1[:, None] * b[None, :]) % NY) / NY
    wave = k1[:, None] + R1 * b[None, :]
    signed = np.where(wave < NY // 2, wave, wave - NY)
    kernel_angle = -np.pi * ((signed * signed) % (2 * NY)) / NY
    phases = np.stack([np.cos(angle), np.sin(angle), np.cos(kernel_angle), np.sin(kernel_angle)])
    phases = phases.astype(np.float32).reshape(4, R1, 1, R2)
    turn = 2.0 * np.pi * ((b[:, None] * b[None, :]) % R2) / R2
    c = np.cos(turn).astype(ml_dtypes.bfloat16).astype(np.float32)
    s = np.sin(turn).astype(ml_dtypes.bfloat16).astype(np.float32)
    forward = np.block([[c, -s], [s, c]])
    backward = np.block([[c, s], [-s, c]])
    fourier = np.stack([forward, backward]).astype(ml_dtypes.bfloat16)
    eight = np.arange(8)
    inner = -2.0 * np.pi * (eight[:, None] * eight[None, :]) / 64.0
    inner = np.concatenate([np.cos(inner), np.sin(inner)], axis=1).astype(np.float32)
    return phases, fourier, inner


def add(p, q):
    return (p[0] + q[0], p[1] + q[1])


def sub(p, q):
    return (p[0] - q[0], p[1] - q[1])


def mul(p, q):
    return (p[0] * q[0] - p[1] * q[1], p[0] * q[1] + p[1] * q[0])


def quarter(p, sign):
    return (-p[1], p[0]) if sign > 0 else (p[1], -p[0])


def dft8(x, sign):
    half = math.sqrt(0.5)

    def four(a, b, c, d):
        e0, e1 = add(a, c), sub(a, c)
        o0, o1 = add(b, d), quarter(sub(b, d), sign)
        return add(e0, o0), add(e1, o1), sub(e0, o0), sub(e1, o1)

    e = four(x[0], x[2], x[4], x[6])
    o = four(x[1], x[3], x[5], x[7])
    u1 = quarter(o[1], sign)
    u3 = quarter(o[3], sign)
    o1 = ((o[1][0] + u1[0]) * half, (o[1][1] + u1[1]) * half)
    o2 = quarter(o[2], sign)
    o3 = ((u3[0] - o[3][0]) * half, (u3[1] - o[3][1]) * half)
    o = (o[0], o1, o2, o3)
    return [add(e[i], o[i]) for i in range(4)] + [sub(e[i], o[i]) for i in range(4)]


def cos_sin(theta):
    u = theta * theta
    s = SIN_COEFS[-1]
    for coef in SIN_COEFS[-2::-1]:
        s = s * u + coef
    c = COS_COEFS[-1]
    for coef in COS_COEFS[-2::-1]:
        c = c * u + coef
    return c, s * theta


def cross_range(rows, load, store, inner_ref, phase_ref, fourier_ref, work, mid, between=None):
    def twist(index, sign):
        return [None] + [(inner_ref[index, k], sign * inner_ref[index, 8 + k]) for k in range(1, 8)]

    def forward_one(a2, carry):
        out = dft8([load(a1, a2) for a1 in range(8)], -1)
        factors = twist(a2, 1.0)
        for k in range(8):
            value = out[k] if k == 0 else mul(out[k], factors[k])
            for p in range(2):
                work[a2 * 8 + k, p, pl.ds(0, rows), :] = value[p]
        return carry

    lax.fori_loop(0, 8, forward_one, 0)

    def forward_two(k, carry):
        values = [tuple(work[a2 * 8 + k, p, pl.ds(0, rows), :] for p in range(2)) for a2 in range(8)]
        out = dft8(values, -1)
        for kk in range(8):
            k1 = k + 8 * kk
            value = mul(out[kk], (phase_ref[0, k1], phase_ref[1, k1]))
            for p in range(2):
                mid[k1, pl.ds(0, rows), pl.ds(128 * p, 128)] = value[p]
        return carry

    lax.fori_loop(0, 8, forward_two, 0)
    if between is not None:
        between()

    def inner(i, carry):
        part = pl.ds(i * 16, 16)
        y = mid[part, pl.ds(0, rows), :].reshape(16 * rows, 256).astype(BF16)
        y = jnp.dot(y, fourier_ref[0], preferred_element_type=F32).reshape(16, rows, 256)
        y = mul((y[:, :, :128], y[:, :, 128:]), (phase_ref[2, part], phase_ref[3, part]))
        y = jnp.concatenate(y, axis=2).reshape(16 * rows, 256).astype(BF16)
        y = jnp.dot(y, fourier_ref[1], preferred_element_type=F32).reshape(16, rows, 256)
        y = mul((y[:, :, :128], y[:, :, 128:]), (phase_ref[0, part], -phase_ref[1, part]))
        for p in range(2):
            work[part, p, pl.ds(0, rows), :] = y[p]
        return carry

    lax.fori_loop(0, 4, inner, 0)

    def backward_one(k2, carry):
        values = [tuple(work[8 * q + k2, p, pl.ds(0, rows), :] for p in range(2)) for q in range(8)]
        out = dft8(values, 1)
        factors = twist(k2, -1.0)
        for a in range(8):
            value = out[a] if a == 0 else mul(out[a], factors[a])
            for p in range(2):
                mid[k2 * 8 + a, pl.ds(0, rows), pl.ds(128 * p, 128)] = value[p]
        return carry

    lax.fori_loop(0, 8, backward_one, 0)

    def backward_two(a, carry):
        values = [
            tuple(mid[k2 * 8 + a, pl.ds(0, rows), pl.ds(128 * p, 128)] for p in range(2)) for k2 in range(8)
        ]
        out = dft8(values, 1)
        for aa in range(8):
            store(a + 8 * aa, (out[aa][0] * (1.0 / NY), out[aa][1] * (1.0 / NY)))
        return carry

    lax.fori_loop(0, 8, backward_two, 0)


def clear_ends(values):
    zeros = jnp.zeros((2, 8, 128), F32)
    values[:, pl.ds(0, 8), :] = zeros
    values[:, pl.ds(NZ + 8, 8), :] = zeros


def right_side(values, edge_lhs, rhs, edge):
    def step(k, carry):
        pairs = []
        for p in range(2):
            centre = values[p, pl.ds(pl.multiple_of(k * BLK + 8, 8), BLK), :]
            above = values[p, pl.ds(k * BLK + 7, BLK), :]
            below = values[p, pl.ds(k * BLK + 9, BLK), :]
            pairs.append((centre, above + below - 2.0 * centre))
        (c_real, d_real), (c_imag, d_imag) = pairs
        r_real = c_real + ALPHA_REAL * d_real - ALPHA_IMAG * d_imag
        r_imag = c_imag + ALPHA_REAL * d_imag + ALPHA_IMAG * d_real
        rhs[k, pl.ds(0, BLK), :] = r_real
        rhs[k, pl.ds(BLK, BLK), :] = r_imag
        both = jnp.concatenate([r_real.astype(BF16), r_imag.astype(BF16)], axis=0)
        edge[k] = jnp.dot(edge_lhs[k], both, preferred_element_type=F32)
        return carry

    lax.fori_loop(0, NBLK, step, 0, unroll=2)


def recur(edge, corner, rhs):
    couple = (COUPLE_REAL, COUPLE_IMAG)

    def entry(k, i):
        return tuple(corner[k, pl.ds(2 * i + p, 1), :] for p in range(2))

    def row_of(k, i):
        return tuple(edge[k, pl.ds(i + p, 1), :] for p in range(2))

    starts = []
    held = None
    for k in range(NBLK):
        first, last = row_of(k, 0), row_of(k, 2)
        if held is not None:
            scaled = mul(held, couple)
            for p in range(2):
                rhs[k, pl.ds(BLK * p, 1), :] -= scaled[p]
            first = sub(first, mul(scaled, entry(k, 0)))
            last = sub(last, mul(scaled, entry(k, 1)))
        starts.append(first)
        held = last
    held = None
    for k in range(NBLK - 1, -1, -1):
        value = starts[k]
        if held is not None:
            scaled = mul(held, couple)
            for p in range(2):
                rhs[k, pl.ds(BLK * p + BLK - 1, 1), :] -= scaled[p]
            value = sub(value, mul(scaled, entry(k, 2)))
        held = value


def finish(matrix, rhs, store, begin, count):
    def step(i, carry):
        k = begin + i
        result = jnp.dot(matrix[k], rhs[k].astype(BF16), preferred_element_type=F32).astype(BF16)
        here = pl.ds(pl.multiple_of(k * BLK, BLK), BLK)
        for p in range(2):
            store(p, here, result[128 * p : 128 * p + 128])
        return carry

    lax.fori_loop(0, count, step, 0, unroll=2)


def exchange_kernel(
    tangent_hbm,
    base_hbm,
    theta_hbm,
    eof_hbm,
    mode_hbm,
    factor_hbm,
    inner_hbm,
    phase_hbm,
    fourier_hbm,
    t_next,
    b_next,
    t_late,
    values,
    matrix,
    edge_lhs,
    corner,
    done,
    tangent,
    base,
    theta,
    eof,
    mode,
    factor_in,
    inner_ref,
    phase_ref,
    fourier_ref,
    quarter_out,
    quarter_in,
    work,
    mid,
    t_send,
    b_send,
    rows32,
    factors,
    profile,
    t_early,
    b_all,
    g_all,
    p_all,
    p_wide,
    spread32,
    blocks,
    b_values,
    rhs,
    edge,
    load_sem,
    own_sem,
    q_sem,
    t_sem,
    b_sem,
    far_sem,
    bg_sem,
    g_sem,
    p_sem,
    round_sem,
    done_sem,
):
    g = lax.axis_index("grp")
    s = lax.axis_index("slab")
    zh, x, y = s // 16, (s // 4) % 4, s % 4
    core = g % 2

    def at_slab(dz, dx, dy):
        return (g, ((zh + dz) % 4) * 16 + ((x + dx) % 4) * 4 + (y + dy) % 4)

    def partner(i):
        return at_slab(i % 4, (i // 4) % 4, i // 16)

    def in_grp(i):
        mate = g + 1 - 2 * (g % 2) if i % 2 else g
        return (mate + 2) % 4 if i // 2 else mate

    core_mate = in_grp(1)
    far_mate = in_grp(2)
    lines = [[at_slab(i, 0, 0) for i in (1, 2, 3)], [at_slab(0, i, 0) for i in (1, 2, 3)], [at_slab(0, 0, i) for i in (1, 2, 3)]]
    grp_line = [(in_grp(i), s) for i in (1, 2, 3)]

    barrier = pltpu.get_barrier_semaphore()
    for target in lines[0] + lines[1] + lines[2] + grp_line:
        pl.semaphore_signal(barrier, inc=1, device_id=target, device_id_type=MESH)

    pairs = [
        (theta_hbm, theta),
        (base_hbm, base),
        (factor_hbm, factor_in),
        (eof_hbm, eof),
        (mode_hbm, mode),
        (tangent_hbm.at[0], tangent),
        (inner_hbm, inner_ref),
        (phase_hbm, phase_ref),
        (fourier_hbm, fourier_ref),
    ]
    loads = [pltpu.make_async_copy(src, dst, load_sem.at[i]) for i, (src, dst) in enumerate(pairs)]
    for copy in loads:
        copy.start()

    def put(src, dst, sems, target):
        return pltpu.make_async_remote_copy(
            src_ref=src, dst_ref=dst, send_sem=sems.at[0], recv_sem=sems.at[1], device_id=target, device_id_type=MESH
        )

    def signal_round(i):
        for target in lines[i + 1]:
            pl.semaphore_signal(round_sem.at[i], inc=1, device_id=target, device_id_type=MESH)

    for copy in loads[:5]:
        copy.wait()

    def screen(a, carry):
        cells = pl.ds(pl.multiple_of(a * 128, 128), 128)
        there = pl.ds(pl.multiple_of(g * 2048 + a * 128, 128), 128)
        turn = cos_sin(theta[:, there].astype(F32))
        value = mul((base[0, :, cells].astype(F32), base[1, :, cells].astype(F32)), turn)
        for part in range(4):
            depth = slice(8 * part, 8 * part + 8)
            quarter_out[part, a] = jnp.concatenate([value[0][depth], value[1][depth]], axis=0).astype(BF16)
        return carry

    lax.fori_loop(0, 16, screen, 0)

    for k in range(NBLK):
        for p in range(2):
            rows32[pl.ds(4 * k + 2 * p, 2), :] = factor_in[k, p].astype(F32)
    factors[...] = rows32[pl.ds(pl.multiple_of(core * 32, 32), 32), :].astype(BF16)
    chosen = lax.broadcasted_iota(jnp.int32, eof.shape, 1) == mode[0]
    column = jnp.sum(jnp.where(chosen, eof[...], 0.0), axis=1, keepdims=True)
    diagonal = lax.broadcasted_iota(jnp.int32, (ROWS, 128), 0) == lax.broadcasted_iota(jnp.int32, (ROWS, 128), 1)
    profile[...] = jnp.sum(jnp.where(diagonal, column, 0.0), axis=0, keepdims=True)

    for copy in loads[5:]:
        copy.wait()

    def load_tangent(c, a1, a2):
        depth = pl.ds(c * CH, CH)
        cells = pl.ds(pl.multiple_of((8 * a1 + a2) * 128, 128), 128)
        turn = cos_sin(theta[depth, cells].astype(F32))
        return mul((tangent[0, depth, cells].astype(F32), tangent[1, depth, cells].astype(F32)), turn)

    def store_tangent(c, a, value):
        for p in range(2):
            t_send[c, a, p] = value[p].astype(BF16)

    g_own, p_own = g_all.at[core, zh, x, y], p_all.at[zh, x, y]
    gx, px = g_all.at[core, :, x, y], p_all.at[:, x, y]
    gy, py = g_all.at[core, :, :, y], p_all.at[:, :, y]
    stages = [((factors, g_own), (profile, p_own)), ((gx, gx), (px, px)), ((gy, gy), (py, py))]
    g_half = put(g_all.at[core], g_all.at[core], g_sem.at[3], (core_mate, s))

    def gather_start(stage):
        for target in lines[stage]:
            for (src, dst), sem in zip(stages[stage], (g_sem, p_sem)):
                put(src, dst, sem.at[stage], target).start()

    def gather_wait(stage):
        for ref, sem in ((g_all.at[core], g_sem), (p_all, p_sem)):
            if stage == 0:
                part = ref.at[pl.ds(0, 3), 0, 0]
            elif stage == 1:
                part = ref.at[:, pl.ds(0, 3), 0]
            else:
                part = ref.at[:, :, pl.ds(0, 3)]
            put(part, part, sem.at[stage], lines[stage][0]).wait()

    t_land = [t_early, t_late]

    def t_move(c, i):
        target = partner(i)
        return put(t_send.at[c, target[1]], t_land[c].at[s], t_sem.at[c], target)

    def b_move(i):
        target = partner(i)
        return put(b_send.at[target[1]], b_all.at[g, s], b_sem, target)

    def far_move(i):
        cells = partner(i)[1]
        return put(b_send.at[cells], b_all.at[g, s], far_sem, (far_mate, cells))

    def start_all(move):
        def step(i, carry):
            move(i).start()
            return carry

        lax.fori_loop(1, SLAB, step, 0)

    def own(src, dst, i):
        return pltpu.make_async_copy(src, dst, own_sem.at[i])

    own_t = [own(t_send.at[c, s], t_land[c].at[s], c) for c in range(2)]
    own_b = own(b_send.at[s], b_all.at[g, s], 2)
    own_g = own(factors, g_own, 3)
    own_p = own(profile, p_own, 4)
    own_q = own(quarter_out.at[g], quarter_in.at[g], 5)

    tabs = (inner_ref, phase_ref, fourier_ref, work, mid)
    most = pl.ds(0, SLAB - 1)

    pl.semaphore_wait(barrier, 12)
    signal_round(0)
    for i in (1, 2, 3):
        put(quarter_out.at[in_grp(i)], quarter_in.at[g], q_sem, (in_grp(i), s)).start()
    own_q.start()
    gather_start(0)
    own_g.start()
    own_p.start()

    def second_round():
        pl.semaphore_wait(round_sem.at[0], 3)
        signal_round(1)

    cross_range(
        CH, functools.partial(load_tangent, 0), functools.partial(store_tangent, 0), *tabs, between=second_round
    )
    pl.semaphore_wait(round_sem.at[1], 3)
    pl.semaphore_signal(round_sem.at[2], inc=1, device_id=(far_mate, s), device_id_type=MESH)
    start_all(functools.partial(t_move, 0))
    own_t[0].start()
    own_g.wait()
    own_p.wait()
    gather_wait(0)
    gather_start(1)

    own_q.wait()
    put(quarter_out.at[pl.ds(0, 3)], quarter_in.at[pl.ds(0, 3)], q_sem, (core_mate, s)).wait()

    def load_base(a1, a2):
        tile = quarter_in[a1 // 2, 8 * (a1 % 2) + a2].astype(F32)
        return (tile[:8], tile[8:])

    def store_base(a, value):
        b_send[a] = jnp.concatenate(value, axis=0).astype(BF16)

    cross_range(8, load_base, store_base, *tabs)
    pl.semaphore_wait(round_sem.at[2], 1)

    def both_ways(i, carry):
        far_move(i).start()
        b_move(i).start()
        return carry

    far_move(0).start()
    lax.fori_loop(1, SLAB, both_ways, 0)
    own_b.start()
    cross_range(CH, functools.partial(load_tangent, 1), functools.partial(store_tangent, 1), *tabs)
    gather_wait(1)
    gather_start(2)
    early = put(t_send.at[0, most], t_early.at[most], t_sem.at[0], (core_mate, s))
    early.wait_send()
    start_all(functools.partial(t_move, 1))
    own_t[1].start()

    clear_ends(values)
    clear_ends(b_values)
    gather_wait(2)
    g_half.start()

    def widen_profile(i, carry):
        column = jnp.sum(jnp.where(diagonal, p_all[i // 16, (i // 4) % 4, i % 4], 0.0), axis=1, keepdims=True)
        p_wide[pl.ds(pl.multiple_of(i * ROWS, ROWS), ROWS), :] = jnp.broadcast_to(column, (ROWS, 128))
        return carry

    lax.fori_loop(0, SLAB, widen_profile, 0)
    g_half.wait()

    def widen(i, carry):
        for h in range(2):
            rows = pl.ds(pl.multiple_of(h * 2048 + i * 32, 32), 32)
            spread32[rows, :] = g_all[h, i // 16, (i // 4) % 4, i % 4].astype(F32)
        return carry

    lax.fori_loop(0, SLAB, widen, 0)

    def arrange(k, carry):
        start = (k // 8) * 2048 + (k % 8) * 4
        for p in range(2):
            for r in range(2):
                blocks[p, pl.ds(r, 64, stride=2), :] = spread32[pl.ds(start + 2 * p + r, 64, stride=32), :]
        real = blocks[0]
        imag = blocks[1]
        upper = jnp.concatenate([real, -imag], axis=1)
        lower = jnp.concatenate([imag, real], axis=1)
        matrix[k, pl.ds(0, 128), :] = upper.astype(BF16)
        matrix[k, pl.ds(128, 128), :] = lower.astype(BF16)
        ends = []
        for row in (0, BLK - 1):
            ends += [upper[row : row + 1], lower[row : row + 1]]
        edge_lhs[k] = jnp.concatenate(ends + ends, axis=0).astype(BF16)
        points = []
        for row, col in ((0, 0), (BLK - 1, 0), (0, BLK - 1), (0, BLK - 1)):
            for p in range(2):
                points.append(jnp.broadcast_to(blocks[p, pl.ds(row, 1), pl.ds(col, 1)], (1, 128)))
        corner[k] = jnp.concatenate(points, axis=0)
        return carry

    lax.fori_loop(0, NBLK, arrange, 0)

    own_b.wait()
    mine, theirs = b_all.at[g], b_all.at[far_mate]
    put(b_send.at[most], b_all.at[0, most], b_sem, (core_mate, s)).wait()
    to_core = put(mine, mine, bg_sem.at[0], (core_mate, s))
    to_core.start()
    put(b_send, theirs, far_sem, (far_mate, s)).wait()
    onward = put(theirs, theirs, bg_sem.at[1], (core_mate, s))
    onward.start()
    own_t[0].wait()
    early.wait_recv()
    to_core.wait()
    onward.wait()

    def combine(i, carry):
        for c in range(2):
            if c == 0:
                t_real = t_early[i, 0].astype(F32)
                t_imag = t_early[i, 1].astype(F32)
            for h in range(2):
                tile = b_all[2 * c + h, i].astype(F32)
                b_real, b_imag = tile[:8], tile[8:]
                at = CH * c + 8 * h
                scale = p_wide[pl.ds(pl.multiple_of(i * ROWS + at, 8), 8), :]
                here = pl.ds(pl.multiple_of(i * ROWS + at + 8, 8), 8)
                real = -scale * b_imag
                imag = scale * b_real
                if c == 0:
                    real += t_real[8 * h : 8 * h + 8]
                    imag += t_imag[8 * h : 8 * h + 8]
                values[0, here, :] = real
                values[1, here, :] = imag
                b_values[0, here, :] = b_real
                b_values[1, here, :] = b_imag
        return carry

    lax.fori_loop(0, SLAB, combine, 0, unroll=2)

    def store_done(f, p, here, result):
        done[f, p, here, :] = result

    outs = (t_next.at[0], b_next)

    def hand_out(f):
        def part(h):
            rows = pl.ds(h * (NZ // 2), NZ // 2)
            return pltpu.make_async_copy(done.at[f, :, rows], outs[f].at[:, rows], done_sem.at[2 * f + h])

        halves = [part(h) for h in range(2)]
        for h in range(2):
            finish(matrix, rhs, functools.partial(store_done, f), h * (NBLK // 2), NBLK // 2)
            halves[h].start()
        return halves

    right_side(b_values, edge_lhs, rhs, edge)
    recur(edge, corner, rhs)
    base_out = hand_out(1)

    own_t[1].wait()
    put(t_send.at[1, most], t_late.at[most], t_sem.at[1], (core_mate, s)).wait()

    def add_late(i, carry):
        for p in range(2):
            here = pl.ds(pl.multiple_of(i * ROWS + CH + 8, 8), CH)
            values[p, here, :] += t_late[i, p].astype(F32)
        return carry

    lax.fori_loop(0, SLAB, add_late, 0, unroll=4)
    right_side(values, edge_lhs, rhs, edge)
    recur(edge, corner, rhs)
    tangent_out = hand_out(0)
    for copy in base_out + tangent_out:
        copy.wait()


def copy_kernel(t_in, b_in, t_out, b_out, held, sem):
    arrivals = []
    leaves = []
    for f, (src, dst) in enumerate(((t_in.at[0], t_out.at[0]), (b_in, b_out))):
        for p in range(2):
            for h in range(2):
                rows = pl.ds(h * (NZ // 2), NZ // 2)
                i = 4 * f + 2 * p + h
                arrivals.append(pltpu.make_async_copy(src.at[p, rows], held.at[i], sem.at[0, i]))
                leaves.append(pltpu.make_async_copy(held.at[i], dst.at[p, rows], sem.at[1, i]))
    for copy in arrivals:
        copy.start()
    for arrival, leave in zip(arrivals, leaves):
        arrival.wait()
        leave.start()
    for leave in leaves:
        leave.wait()


def on_device(tangent, base, theta, eof_table, mode_of_field, block_factors):
    phases, fourier, inner = tables()
    in_hbm = pl.BlockSpec(memory_space=pltpu.HBM)
    anywhere = pl.BlockSpec(memory_space=ANY)
    smem = pltpu.SMEM
    dma = pltpu.SemaphoreType.DMA
    shape = jax.ShapeDtypeStruct
    results = (shape((1, 2, NZ, 128), BF16), shape((2, NZ, 128), BF16))
    handed = pl.pallas_call(
        exchange_kernel,
        out_shape=results,
        in_specs=[in_hbm] * 9,
        out_specs=(anywhere, anywhere),
        scratch_shapes=[
            VMEM((SLAB, 2, CH, 128), BF16),
            VMEM((2, NZ + 16, 128), F32),
            VMEM((NBLK, 256, 256), BF16),
            VMEM((NBLK, 8, 256), BF16),
            VMEM((NBLK, 8, 128), F32),
            VMEM((2, 2, NZ, 128), BF16),
            VMEM((2, ROWS, NY), BF16),
            VMEM((2, ROWS, NY // 4), BF16),
            VMEM((ROWS, NY), BF16),
            VMEM((ROWS, 112), F32),
            smem((1,), jnp.int32),
            VMEM((NBLK, 2, 2, 128), BF16),
            smem((8, 16), F32),
            VMEM((4, R1, 1, R2), F32),
            VMEM((2, 256, 256), BF16),
            VMEM((4, 16, 16, 128), BF16),
            VMEM((4, 16, 16, 128), BF16),
            VMEM((R1, 2, CH, 128), F32),
            VMEM((R1, CH, 256), F32),
            VMEM((2, SLAB, 2, CH, 128), BF16),
            VMEM((SLAB, 16, 128), BF16),
            VMEM((64, 128), F32),
            VMEM((32, 128), BF16),
            VMEM((1, 128), F32),
            VMEM((SLAB, 2, CH, 128), BF16),
            VMEM((GRP, SLAB, 16, 128), BF16),
            VMEM((2, 4, 4, 4, 32, 128), BF16),
            VMEM((4, 4, 4, 1, 128), F32),
            VMEM((NZ, 128), F32),
            VMEM((4096, 128), F32),
            VMEM((2, BLK, 128), F32),
            VMEM((2, NZ + 16, 128), F32),
            VMEM((NBLK, 256, 128), F32),
            VMEM((NBLK, 8, 128), F32),
            dma((9,)),
            dma((6,)),
            dma((2,)),
            dma((2, 2)),
            dma((2,)),
            dma((2,)),
            dma((2, 2)),
            dma((4, 2)),
            dma((3, 2)),
            pltpu.SemaphoreType.REGULAR((3,)),
            dma((4,)),
        ],
        compiler_params=pltpu.CompilerParams(
            collective_id=0, has_side_effects=True, vmem_limit_bytes=56 * 2**20
        ),
        name="exchange",
    )(
        tangent,
        base,
        theta,
        eof_table.T,
        mode_of_field,
        block_factors,
        jnp.asarray(inner),
        jnp.asarray(phases),
        jnp.asarray(fourier),
    )
    return pl.pallas_call(
        copy_kernel,
        out_shape=results,
        in_specs=[anywhere] * 2,
        out_specs=(anywhere, anywhere),
        scratch_shapes=[VMEM((8, NZ // 2, 128), BF16), dma((2, 8))],
        compiler_params=pltpu.CompilerParams(vmem_limit_bytes=56 * 2**20),
        name="hand_over",
    )(*handed)


def solution(mesh):
    in_specs = (
        P("grp", None, "slab", None),
        P(None, "slab", "grp"),
        P("slab", None),
        P(None, "slab"),
        P("grp"),
        P(None, None, "slab", None),
    )
    out_specs = (P("grp", None, None, "slab"), P(None, None, "slab"))
    return jax.shard_map(on_device, mesh=mesh, in_specs=in_specs, out_specs=out_specs, check_vma=False)
```

```python
import functools
import math

import jax
import jax.numpy as jnp
import ml_dtypes
import numpy as np
from jax import lax
from jax.experimental import pallas as pl
from jax.experimental.pallas import tpu as pltpu
from jax.sharding import PartitionSpec as P

MESH = pl.DeviceIdType.MESH
NZ = 2048
NY = 8192
R1 = 64
R2 = 128
NBLK = 16
BLK = 128
SLAB = 64
GRP = 4
ROWS = 32
CH = 16
ALPHA_REAL = 0.15
ALPHA_IMAG = 0.1
COUPLE_REAL = 0.35
COUPLE_IMAG = -0.25
VMEM = pltpu.VMEM
ANY = pl.ANY
F32 = jnp.float32
BF16 = jnp.bfloat16


def trig_coefficients():
    nodes = np.cos(np.pi * (np.arange(64) + 0.5) / 64)
    square = (nodes + 1.0) * 0.5 * math.pi**2
    root = np.sqrt(square)
    cheb = np.polynomial.chebyshev
    sine = cheb.cheb2poly(cheb.chebfit(nodes, np.sin(root) / root, 7))
    cosine = cheb.cheb2poly(cheb.chebfit(nodes, np.cos(root), 8))

    def in_square(coefs):
        total = np.zeros(1)
        shift = np.array([-1.0, 2.0 / math.pi**2])
        power = np.ones(1)
        for coef in coefs:
            total = np.polynomial.polynomial.polyadd(total, coef * power)
            power = np.polynomial.polynomial.polymul(power, shift)
        return [float(v) for v in total]

    return in_square(sine), in_square(cosine)


SIN_COEFS, COS_COEFS = trig_coefficients()


def tables():
    k1 = np.arange(R1)
    b = np.arange(R2)
    angle = -2.0 * np.pi * ((k1[:, None] * b[None, :]) % NY) / NY
    wave = k1[:, None] + R1 * b[None, :]
    signed = np.where(wave < NY // 2, wave, wave - NY)
    kernel_angle = -np.pi * ((signed * signed) % (2 * NY)) / NY
    phases = np.stack([np.cos(angle), np.sin(angle), np.cos(kernel_angle), np.sin(kernel_angle)])
    phases = phases.astype(np.float32).reshape(4, R1, 1, R2)
    turn = 2.0 * np.pi * ((b[:, None] * b[None, :]) % R2) / R2
    c = np.cos(turn).astype(ml_dtypes.bfloat16).astype(np.float32)
    s = np.sin(turn).astype(ml_dtypes.bfloat16).astype(np.float32)
    forward = np.block([[c, -s], [s, c]])
    backward = np.block([[c, s], [-s, c]])
    fourier = np.stack([forward, backward]).astype(ml_dtypes.bfloat16)
    eight = np.arange(8)
    inner = -2.0 * np.pi * (eight[:, None] * eight[None, :]) / 64.0
    inner = np.concatenate([np.cos(inner), np.sin(inner)], axis=1).astype(np.float32)
    return phases, fourier, inner


def add(p, q):
    return (p[0] + q[0], p[1] + q[1])


def sub(p, q):
    return (p[0] - q[0], p[1] - q[1])


def mul(p, q):
    return (p[0] * q[0] - p[1] * q[1], p[0] * q[1] + p[1] * q[0])


def quarter(p, sign):
    return (-p[1], p[0]) if sign > 0 else (p[1], -p[0])


def dft8(x, sign):
    half = math.sqrt(0.5)

    def four(a, b, c, d):
        e0, e1 = add(a, c), sub(a, c)
        o0, o1 = add(b, d), quarter(sub(b, d), sign)
        return add(e0, o0), add(e1, o1), sub(e0, o0), sub(e1, o1)

    e = four(x[0], x[2], x[4], x[6])
    o = four(x[1], x[3], x[5], x[7])
    u1 = quarter(o[1], sign)
    u3 = quarter(o[3], sign)
    o1 = ((o[1][0] + u1[0]) * half, (o[1][1] + u1[1]) * half)
    o2 = quarter(o[2], sign)
    o3 = ((u3[0] - o[3][0]) * half, (u3[1] - o[3][1]) * half)
    o = (o[0], o1, o2, o3)
    return [add(e[i], o[i]) for i in range(4)] + [sub(e[i], o[i]) for i in range(4)]


def cos_sin(theta):
    u = theta * theta
    s = SIN_COEFS[-1]
    for coef in SIN_COEFS[-2::-1]:
        s = s * u + coef
    c = COS_COEFS[-1]
    for coef in COS_COEFS[-2::-1]:
        c = c * u + coef
    return c, s * theta


def cross_range(rows, load, store, inner_ref, phase_ref, fourier_ref, work, mid, between=None):
    def twist(index, sign):
        return [None] + [(inner_ref[index, k], sign * inner_ref[index, 8 + k]) for k in range(1, 8)]

    def forward_one(a2, carry):
        out = dft8([load(a1, a2) for a1 in range(8)], -1)
        factors = twist(a2, 1.0)
        for k in range(8):
            value = out[k] if k == 0 else mul(out[k], factors[k])
            for p in range(2):
                work[a2 * 8 + k, p, pl.ds(0, rows), :] = value[p]
        return carry

    lax.fori_loop(0, 8, forward_one, 0)

    def forward_two(k, carry):
        values = [tuple(work[a2 * 8 + k, p, pl.ds(0, rows), :] for p in range(2)) for a2 in range(8)]
        out = dft8(values, -1)
        for kk in range(8):
            k1 = k + 8 * kk
            value = mul(out[kk], (phase_ref[0, k1], phase_ref[1, k1]))
            for p in range(2):
                mid[k1, pl.ds(0, rows), pl.ds(128 * p, 128)] = value[p]
        return carry

    lax.fori_loop(0, 8, forward_two, 0)
    if between is not None:
        between()

    def inner(i, carry):
        part = pl.ds(i * 16, 16)
        y = mid[part, pl.ds(0, rows), :].reshape(16 * rows, 256).astype(BF16)
        y = jnp.dot(y, fourier_ref[0], preferred_element_type=F32).reshape(16, rows, 256)
        y = mul((y[:, :, :128], y[:, :, 128:]), (phase_ref[2, part], phase_ref[3, part]))
        y = jnp.concatenate(y, axis=2).reshape(16 * rows, 256).astype(BF16)
        y = jnp.dot(y, fourier_ref[1], preferred_element_type=F32).reshape(16, rows, 256)
        y = mul((y[:, :, :128], y[:, :, 128:]), (phase_ref[0, part], -phase_ref[1, part]))
        for p in range(2):
            work[part, p, pl.ds(0, rows), :] = y[p]
        return carry

    lax.fori_loop(0, 4, inner, 0)

    def backward_one(k2, carry):
        values = [tuple(work[8 * q + k2, p, pl.ds(0, rows), :] for p in range(2)) for q in range(8)]
        out = dft8(values, 1)
        factors = twist(k2, -1.0)
        for a in range(8):
            value = out[a] if a == 0 else mul(out[a], factors[a])
            for p in range(2):
                mid[k2 * 8 + a, pl.ds(0, rows), pl.ds(128 * p, 128)] = value[p]
        return carry

    lax.fori_loop(0, 8, backward_one, 0)

    def backward_two(a, carry):
        values = [
            tuple(mid[k2 * 8 + a, pl.ds(0, rows), pl.ds(128 * p, 128)] for p in range(2)) for k2 in range(8)
        ]
        out = dft8(values, 1)
        for aa in range(8):
            store(a + 8 * aa, (out[aa][0] * (1.0 / NY), out[aa][1] * (1.0 / NY)))
        return carry

    lax.fori_loop(0, 8, backward_two, 0)


def clear_ends(values):
    zeros = jnp.zeros((2, 8, 128), F32)
    values[:, pl.ds(0, 8), :] = zeros
    values[:, pl.ds(NZ + 8, 8), :] = zeros


def right_side(values, edge_lhs, rhs, edge):
    def step(k, carry):
        pairs = []
        for p in range(2):
            centre = values[p, pl.ds(pl.multiple_of(k * BLK + 8, 8), BLK), :]
            above = values[p, pl.ds(k * BLK + 7, BLK), :]
            below = values[p, pl.ds(k * BLK + 9, BLK), :]
            pairs.append((centre, above + below - 2.0 * centre))
        (c_real, d_real), (c_imag, d_imag) = pairs
        r_real = c_real + ALPHA_REAL * d_real - ALPHA_IMAG * d_imag
        r_imag = c_imag + ALPHA_REAL * d_imag + ALPHA_IMAG * d_real
        rhs[k, pl.ds(0, BLK), :] = r_real
        rhs[k, pl.ds(BLK, BLK), :] = r_imag
        both = jnp.concatenate([r_real.astype(BF16), r_imag.astype(BF16)], axis=0)
        edge[k] = jnp.dot(edge_lhs[k], both, preferred_element_type=F32)
        return carry

    lax.fori_loop(0, NBLK, step, 0, unroll=8)


def recur(edge, corner, rhs):
    couple = (COUPLE_REAL, COUPLE_IMAG)

    def entry(k, i):
        return tuple(corner[k, pl.ds(2 * i + p, 1), :] for p in range(2))

    def row_of(k, i):
        return tuple(edge[k, pl.ds(i + p, 1), :] for p in range(2))

    starts = []
    held = None
    for k in range(NBLK):
        first, last = row_of(k, 0), row_of(k, 2)
        if held is not None:
            scaled = mul(held, couple)
            for p in range(2):
                rhs[k, pl.ds(BLK * p, 1), :] -= scaled[p]
            first = sub(first, mul(scaled, entry(k, 0)))
            last = sub(last, mul(scaled, entry(k, 1)))
        starts.append(first)
        held = last
    held = None
    for k in range(NBLK - 1, -1, -1):
        value = starts[k]
        if held is not None:
            scaled = mul(held, couple)
            for p in range(2):
                rhs[k, pl.ds(BLK * p + BLK - 1, 1), :] -= scaled[p]
            value = sub(value, mul(scaled, entry(k, 2)))
        held = value


def finish(matrix, rhs, store, begin, count):
    def step(i, carry):
        k = begin + i
        result = jnp.dot(matrix[k], rhs[k].astype(BF16), preferred_element_type=F32).astype(BF16)
        here = pl.ds(pl.multiple_of(k * BLK, BLK), BLK)
        for p in range(2):
            store(p, here, result[128 * p : 128 * p + 128])
        return carry

    lax.fori_loop(0, count, step, 0, unroll=8)


def exchange_kernel(
    tangent_hbm,
    base_hbm,
    theta_hbm,
    eof_hbm,
    mode_hbm,
    factor_hbm,
    inner_hbm,
    phase_hbm,
    fourier_hbm,
    t_next,
    b_next,
    t_late,
    values,
    matrix,
    edge_lhs,
    corner,
    done,
    tangent,
    base,
    theta,
    eof,
    mode,
    factor_in,
    inner_ref,
    phase_ref,
    fourier_ref,
    quarter_out,
    quarter_in,
    work,
    mid,
    t_send,
    b_send,
    rows32,
    factors,
    profile,
    t_early,
    b_all,
    g_all,
    p_all,
    p_wide,
    spread32,
    blocks,
    b_values,
    rhs,
    edge,
    load_sem,
    own_sem,
    q_sem,
    t_sem,
    b_sem,
    far_sem,
    bg_sem,
    g_sem,
    p_sem,
    round_sem,
    done_sem,
):
    g = lax.axis_index("grp")
    s = lax.axis_index("slab")
    zh, x, y = s // 16, (s // 4) % 4, s % 4
    core = g % 2

    def at_slab(dz, dx, dy):
        return (g, ((zh + dz) % 4) * 16 + ((x + dx) % 4) * 4 + (y + dy) % 4)

    def partner(i):
        return at_slab(i % 4, (i // 4) % 4, i // 16)

    def in_grp(i):
        mate = g + 1 - 2 * (g % 2) if i % 2 else g
        return (mate + 2) % 4 if i // 2 else mate

    core_mate = in_grp(1)
    far_mate = in_grp(2)
    lines = [[at_slab(i, 0, 0) for i in (1, 2, 3)], [at_slab(0, i, 0) for i in (1, 2, 3)], [at_slab(0, 0, i) for i in (1, 2, 3)]]
    grp_line = [(in_grp(i), s) for i in (1, 2, 3)]

    barrier = pltpu.get_barrier_semaphore()
    for target in lines[0] + lines[1] + lines[2] + grp_line:
        pl.semaphore_signal(barrier, inc=1, device_id=target, device_id_type=MESH)

    pairs = [
        (theta_hbm, theta),
        (base_hbm, base),
        (factor_hbm, factor_in),
        (eof_hbm, eof),
        (mode_hbm, mode),
        (tangent_hbm.at[0], tangent),
        (inner_hbm, inner_ref),
        (phase_hbm, phase_ref),
        (fourier_hbm, fourier_ref),
    ]
    loads = [pltpu.make_async_copy(src, dst, load_sem.at[i]) for i, (src, dst) in enumerate(pairs)]
    for copy in loads:
        copy.start()

    def put(src, dst, sems, target):
        return pltpu.make_async_remote_copy(
            src_ref=src, dst_ref=dst, send_sem=sems.at[0], recv_sem=sems.at[1], device_id=target, device_id_type=MESH
        )

    def signal_round(i):
        for target in lines[i + 1]:
            pl.semaphore_signal(round_sem.at[i], inc=1, device_id=target, device_id_type=MESH)

    for copy in loads[:5]:
        copy.wait()

    def screen(a, carry):
        cells = pl.ds(pl.multiple_of(a * 128, 128), 128)
        there = pl.ds(pl.multiple_of(g * 2048 + a * 128, 128), 128)
        turn = cos_sin(theta[:, there].astype(F32))
        value = mul((base[0, :, cells].astype(F32), base[1, :, cells].astype(F32)), turn)
        for part in range(4):
            depth = slice(8 * part, 8 * part + 8)
            quarter_out[part, a] = jnp.concatenate([value[0][depth], value[1][depth]], axis=0).astype(BF16)
        return carry

    lax.fori_loop(0, 16, screen, 0)

    for k in range(NBLK):
        for p in range(2):
            rows32[pl.ds(4 * k + 2 * p, 2), :] = factor_in[k, p].astype(F32)
    factors[...] = rows32[pl.ds(pl.multiple_of(core * 32, 32), 32), :].astype(BF16)
    chosen = lax.broadcasted_iota(jnp.int32, eof.shape, 1) == mode[0]
    column = jnp.sum(jnp.where(chosen, eof[...], 0.0), axis=1, keepdims=True)
    diagonal = lax.broadcasted_iota(jnp.int32, (ROWS, 128), 0) == lax.broadcasted_iota(jnp.int32, (ROWS, 128), 1)
    profile[...] = jnp.sum(jnp.where(diagonal, column, 0.0), axis=0, keepdims=True)

    for copy in loads[5:]:
        copy.wait()

    def load_tangent(c, a1, a2):
        depth = pl.ds(c * CH, CH)
        cells = pl.ds(pl.multiple_of((8 * a1 + a2) * 128, 128), 128)
        turn = cos_sin(theta[depth, cells].astype(F32))
        return mul((tangent[0, depth, cells].astype(F32), tangent[1, depth, cells].astype(F32)), turn)

    def store_tangent(c, a, value):
        for p in range(2):
            t_send[c, a, p] = value[p].astype(BF16)

    g_own, p_own = g_all.at[core, zh, x, y], p_all.at[zh, x, y]
    gx, px = g_all.at[core, :, x, y], p_all.at[:, x, y]
    gy, py = g_all.at[core, :, :, y], p_all.at[:, :, y]
    stages = [((factors, g_own), (profile, p_own)), ((gx, gx), (px, px)), ((gy, gy), (py, py))]
    g_half = put(g_all.at[core], g_all.at[core], g_sem.at[3], (core_mate, s))

    def gather_start(stage):
        for target in lines[stage]:
            for (src, dst), sem in zip(stages[stage], (g_sem, p_sem)):
                put(src, dst, sem.at[stage], target).start()

    def gather_wait(stage):
        for ref, sem in ((g_all.at[core], g_sem), (p_all, p_sem)):
            if stage == 0:
                part = ref.at[pl.ds(0, 3), 0, 0]
            elif stage == 1:
                part = ref.at[:, pl.ds(0, 3), 0]
            else:
                part = ref.at[:, :, pl.ds(0, 3)]
            put(part, part, sem.at[stage], lines[stage][0]).wait()

    t_land = [t_early, t_late]

    def t_move(c, i):
        target = partner(i)
        return put(t_send.at[c, target[1]], t_land[c].at[s], t_sem.at[c], target)

    def b_move(i):
        target = partner(i)
        return put(b_send.at[target[1]], b_all.at[g, s], b_sem, target)

    def far_move(i):
        cells = partner(i)[1]
        return put(b_send.at[cells], b_all.at[g, s], far_sem, (far_mate, cells))

    def start_all(move):
        def step(i, carry):
            move(i).start()
            return carry

        lax.fori_loop(1, SLAB, step, 0)

    def own(src, dst, i):
        return pltpu.make_async_copy(src, dst, own_sem.at[i])

    own_t = [own(t_send.at[c, s], t_land[c].at[s], c) for c in range(2)]
    own_b = own(b_send.at[s], b_all.at[g, s], 2)
    own_g = own(factors, g_own, 3)
    own_p = own(profile, p_own, 4)
    own_q = own(quarter_out.at[g], quarter_in.at[g], 5)

    tabs = (inner_ref, phase_ref, fourier_ref, work, mid)
    most = pl.ds(0, SLAB - 1)

    pl.semaphore_wait(barrier, 12)
    signal_round(0)
    for i in (1, 2, 3):
        put(quarter_out.at[in_grp(i)], quarter_in.at[g], q_sem, (in_grp(i), s)).start()
    own_q.start()
    gather_start(0)
    own_g.start()
    own_p.start()

    def second_round():
        pl.semaphore_wait(round_sem.at[0], 3)
        signal_round(1)

    cross_range(
        CH, functools.partial(load_tangent, 0), functools.partial(store_tangent, 0), *tabs, between=second_round
    )
    pl.semaphore_wait(round_sem.at[1], 3)
    pl.semaphore_signal(round_sem.at[2], inc=1, device_id=(far_mate, s), device_id_type=MESH)
    start_all(functools.partial(t_move, 0))
    own_t[0].start()
    own_g.wait()
    own_p.wait()
    gather_wait(0)
    gather_start(1)

    own_q.wait()
    put(quarter_out.at[pl.ds(0, 3)], quarter_in.at[pl.ds(0, 3)], q_sem, (core_mate, s)).wait()

    def load_base(a1, a2):
        tile = quarter_in[a1 // 2, 8 * (a1 % 2) + a2].astype(F32)
        return (tile[:8], tile[8:])

    def store_base(a, value):
        b_send[a] = jnp.concatenate(value, axis=0).astype(BF16)

    cross_range(8, load_base, store_base, *tabs)
    pl.semaphore_wait(round_sem.at[2], 1)

    def both_ways(i, carry):
        far_move(i).start()
        b_move(i).start()
        return carry

    far_move(0).start()
    lax.fori_loop(1, SLAB, both_ways, 0)
    own_b.start()
    cross_range(CH, functools.partial(load_tangent, 1), functools.partial(store_tangent, 1), *tabs)
    gather_wait(1)
    gather_start(2)
    early = put(t_send.at[0, most], t_early.at[most], t_sem.at[0], (core_mate, s))
    early.wait_send()
    start_all(functools.partial(t_move, 1))
    own_t[1].start()

    clear_ends(values)
    clear_ends(b_values)
    gather_wait(2)
    g_half.start()

    def widen_profile(i, carry):
        column = jnp.sum(jnp.where(diagonal, p_all[i // 16, (i // 4) % 4, i % 4], 0.0), axis=1, keepdims=True)
        p_wide[pl.ds(pl.multiple_of(i * ROWS, ROWS), ROWS), :] = jnp.broadcast_to(column, (ROWS, 128))
        return carry

    lax.fori_loop(0, SLAB, widen_profile, 0)
    g_half.wait()

    def widen(i, carry):
        for h in range(2):
            rows = pl.ds(pl.multiple_of(h * 2048 + i * 32, 32), 32)
            spread32[rows, :] = g_all[h, i // 16, (i // 4) % 4, i % 4].astype(F32)
        return carry

    lax.fori_loop(0, SLAB, widen, 0)

    def arrange(k, carry):
        start = (k // 8) * 2048 + (k % 8) * 4
        for p in range(2):
            for r in range(2):
                blocks[p, pl.ds(r, 64, stride=2), :] = spread32[pl.ds(start + 2 * p + r, 64, stride=32), :]
        real = blocks[0]
        imag = blocks[1]
        upper = jnp.concatenate([real, -imag], axis=1)
        lower = jnp.concatenate([imag, real], axis=1)
        matrix[k, pl.ds(0, 128), :] = upper.astype(BF16)
        matrix[k, pl.ds(128, 128), :] = lower.astype(BF16)
        ends = []
        for row in (0, BLK - 1):
            ends += [upper[row : row + 1], lower[row : row + 1]]
        edge_lhs[k] = jnp.concatenate(ends + ends, axis=0).astype(BF16)
        points = []
        for row, col in ((0, 0), (BLK - 1, 0), (0, BLK - 1), (0, BLK - 1)):
            for p in range(2):
                points.append(jnp.broadcast_to(blocks[p, pl.ds(row, 1), pl.ds(col, 1)], (1, 128)))
        corner[k] = jnp.concatenate(points, axis=0)
        return carry

    lax.fori_loop(0, NBLK, arrange, 0)

    own_b.wait()
    mine, theirs = b_all.at[g], b_all.at[far_mate]
    put(b_send.at[most], b_all.at[0, most], b_sem, (core_mate, s)).wait()
    to_core = put(mine, mine, bg_sem.at[0], (core_mate, s))
    to_core.start()
    put(b_send, theirs, far_sem, (far_mate, s)).wait()
    onward = put(theirs, theirs, bg_sem.at[1], (core_mate, s))
    onward.start()
    own_t[0].wait()
    early.wait_recv()
    to_core.wait()
    onward.wait()

    def combine(i, carry):
        for c in range(2):
            if c == 0:
                t_real = t_early[i, 0].astype(F32)
                t_imag = t_early[i, 1].astype(F32)
            for h in range(2):
                tile = b_all[2 * c + h, i].astype(F32)
                b_real, b_imag = tile[:8], tile[8:]
                at = CH * c + 8 * h
                scale = p_wide[pl.ds(pl.multiple_of(i * ROWS + at, 8), 8), :]
                here = pl.ds(pl.multiple_of(i * ROWS + at + 8, 8), 8)
                real = -scale * b_imag
                imag = scale * b_real
                if c == 0:
                    real += t_real[8 * h : 8 * h + 8]
                    imag += t_imag[8 * h : 8 * h + 8]
                values[0, here, :] = real
                values[1, here, :] = imag
                b_values[0, here, :] = b_real
                b_values[1, here, :] = b_imag
        return carry

    lax.fori_loop(0, SLAB, combine, 0, unroll=2)

    def store_done(f, p, here, result):
        done[f, p, here, :] = result

    outs = (t_next.at[0], b_next)

    def hand_out(f):
        def part(h):
            rows = pl.ds(h * (NZ // 2), NZ // 2)
            return pltpu.make_async_copy(done.at[f, :, rows], outs[f].at[:, rows], done_sem.at[2 * f + h])

        halves = [part(h) for h in range(2)]
        for h in range(2):
            finish(matrix, rhs, functools.partial(store_done, f), h * (NBLK // 2), NBLK // 2)
            halves[h].start()
        return halves

    right_side(b_values, edge_lhs, rhs, edge)
    recur(edge, corner, rhs)
    base_out = hand_out(1)

    own_t[1].wait()
    put(t_send.at[1, most], t_late.at[most], t_sem.at[1], (core_mate, s)).wait()

    def add_late(i, carry):
        for p in range(2):
            here = pl.ds(pl.multiple_of(i * ROWS + CH + 8, 8), CH)
            values[p, here, :] += t_late[i, p].astype(F32)
        return carry

    lax.fori_loop(0, SLAB, add_late, 0, unroll=4)
    right_side(values, edge_lhs, rhs, edge)
    recur(edge, corner, rhs)
    tangent_out = hand_out(0)
    for copy in base_out + tangent_out:
        copy.wait()


def copy_kernel(t_in, b_in, t_out, b_out, held, sem):
    arrivals = []
    leaves = []
    for f, (src, dst) in enumerate(((t_in.at[0], t_out.at[0]), (b_in, b_out))):
        for p in range(2):
            for h in range(2):
                rows = pl.ds(h * (NZ // 2), NZ // 2)
                i = 4 * f + 2 * p + h
                arrivals.append(pltpu.make_async_copy(src.at[p, rows], held.at[i], sem.at[0, i]))
                leaves.append(pltpu.make_async_copy(held.at[i], dst.at[p, rows], sem.at[1, i]))
    for copy in arrivals:
        copy.start()
    for arrival, leave in zip(arrivals, leaves):
        arrival.wait()
        leave.start()
    for leave in leaves:
        leave.wait()


def on_device(tangent, base, theta, eof_table, mode_of_field, block_factors):
    phases, fourier, inner = tables()
    in_hbm = pl.BlockSpec(memory_space=pltpu.HBM)
    anywhere = pl.BlockSpec(memory_space=ANY)
    smem = pltpu.SMEM
    dma = pltpu.SemaphoreType.DMA
    shape = jax.ShapeDtypeStruct
    results = (shape((1, 2, NZ, 128), BF16), shape((2, NZ, 128), BF16))
    handed = pl.pallas_call(
        exchange_kernel,
        out_shape=results,
        in_specs=[in_hbm] * 9,
        out_specs=(anywhere, anywhere),
        scratch_shapes=[
            VMEM((SLAB, 2, CH, 128), BF16),
            VMEM((2, NZ + 16, 128), F32),
            VMEM((NBLK, 256, 256), BF16),
            VMEM((NBLK, 8, 256), BF16),
            VMEM((NBLK, 8, 128), F32),
            VMEM((2, 2, NZ, 128), BF16),
            VMEM((2, ROWS, NY), BF16),
            VMEM((2, ROWS, NY // 4), BF16),
            VMEM((ROWS, NY), BF16),
            VMEM((ROWS, 112), F32),
            smem((1,), jnp.int32),
            VMEM((NBLK, 2, 2, 128), BF16),
            smem((8, 16), F32),
            VMEM((4, R1, 1, R2), F32),
            VMEM((2, 256, 256), BF16),
            VMEM((4, 16, 16, 128), BF16),
            VMEM((4, 16, 16, 128), BF16),
            VMEM((R1, 2, CH, 128), F32),
            VMEM((R1, CH, 256), F32),
            VMEM((2, SLAB, 2, CH, 128), BF16),
            VMEM((SLAB, 16, 128), BF16),
            VMEM((64, 128), F32),
            VMEM((32, 128), BF16),
            VMEM((1, 128), F32),
            VMEM((SLAB, 2, CH, 128), BF16),
            VMEM((GRP, SLAB, 16, 128), BF16),
            VMEM((2, 4, 4, 4, 32, 128), BF16),
            VMEM((4, 4, 4, 1, 128), F32),
            VMEM((NZ, 128), F32),
            VMEM((4096, 128), F32),
            VMEM((2, BLK, 128), F32),
            VMEM((2, NZ + 16, 128), F32),
            VMEM((NBLK, 256, 128), F32),
            VMEM((NBLK, 8, 128), F32),
            dma((9,)),
            dma((6,)),
            dma((2,)),
            dma((2, 2)),
            dma((2,)),
            dma((2,)),
            dma((2, 2)),
            dma((4, 2)),
            dma((3, 2)),
            pltpu.SemaphoreType.REGULAR((3,)),
            dma((4,)),
        ],
        compiler_params=pltpu.CompilerParams(
            collective_id=0, has_side_effects=True, vmem_limit_bytes=56 * 2**20
        ),
        name="exchange",
    )(
        tangent,
        base,
        theta,
        eof_table.T,
        mode_of_field,
        block_factors,
        jnp.asarray(inner),
        jnp.asarray(phases),
        jnp.asarray(fourier),
    )
    return pl.pallas_call(
        copy_kernel,
        out_shape=results,
        in_specs=[anywhere] * 2,
        out_specs=(anywhere, anywhere),
        scratch_shapes=[VMEM((8, NZ // 2, 128), BF16), dma((2, 8))],
        compiler_params=pltpu.CompilerParams(vmem_limit_bytes=56 * 2**20),
        name="hand_over",
    )(*handed)


def solution(mesh):
    in_specs = (
        P("grp", None, "slab", None),
        P(None, "slab", "grp"),
        P("slab", None),
        P(None, "slab"),
        P("grp"),
        P(None, None, "slab", None),
    )
    out_specs = (P("grp", None, None, "slab"), P(None, None, "slab"))
    return jax.shard_map(on_device, mesh=mesh, in_specs=in_specs, out_specs=out_specs, check_vma=False)
```

```python
import functools
import math

import jax
import jax.numpy as jnp
import ml_dtypes
import numpy as np
from jax import lax
from jax.experimental import pallas as pl
from jax.experimental.pallas import tpu as pltpu
from jax.sharding import PartitionSpec as P

MESH = pl.DeviceIdType.MESH
NZ = 2048
NY = 8192
R1 = 64
R2 = 128
NBLK = 16
BLK = 128
SLAB = 64
GRP = 4
ROWS = 32
CH = 16
ALPHA_REAL = 0.15
ALPHA_IMAG = 0.1
COUPLE_REAL = 0.35
COUPLE_IMAG = -0.25
VMEM = pltpu.VMEM
ANY = pl.ANY
F32 = jnp.float32
BF16 = jnp.bfloat16


def trig_coefficients():
    nodes = np.cos(np.pi * (np.arange(64) + 0.5) / 64)
    square = (nodes + 1.0) * 0.5 * math.pi**2
    root = np.sqrt(square)
    cheb = np.polynomial.chebyshev
    sine = cheb.cheb2poly(cheb.chebfit(nodes, np.sin(root) / root, 7))
    cosine = cheb.cheb2poly(cheb.chebfit(nodes, np.cos(root), 8))

    def in_square(coefs):
        total = np.zeros(1)
        shift = np.array([-1.0, 2.0 / math.pi**2])
        power = np.ones(1)
        for coef in coefs:
            total = np.polynomial.polynomial.polyadd(total, coef * power)
            power = np.polynomial.polynomial.polymul(power, shift)
        return [float(v) for v in total]

    return in_square(sine), in_square(cosine)


SIN_COEFS, COS_COEFS = trig_coefficients()


def tables():
    k1 = np.arange(R1)
    b = np.arange(R2)
    angle = -2.0 * np.pi * ((k1[:, None] * b[None, :]) % NY) / NY
    wave = k1[:, None] + R1 * b[None, :]
    signed = np.where(wave < NY // 2, wave, wave - NY)
    kernel_angle = -np.pi * ((signed * signed) % (2 * NY)) / NY
    phases = np.stack([np.cos(angle), np.sin(angle), np.cos(kernel_angle), np.sin(kernel_angle)])
    phases = phases.astype(np.float32).reshape(4, R1, 1, R2)
    turn = 2.0 * np.pi * ((b[:, None] * b[None, :]) % R2) / R2
    c = np.cos(turn).astype(ml_dtypes.bfloat16).astype(np.float32)
    s = np.sin(turn).astype(ml_dtypes.bfloat16).astype(np.float32)
    forward = np.block([[c, -s], [s, c]])
    backward = np.block([[c, s], [-s, c]])
    fourier = np.stack([forward, backward]).astype(ml_dtypes.bfloat16)
    eight = np.arange(8)
    inner = -2.0 * np.pi * (eight[:, None] * eight[None, :]) / 64.0
    inner = np.concatenate([np.cos(inner), np.sin(inner)], axis=1).astype(np.float32)
    return phases, fourier, inner


def add(p, q):
    return (p[0] + q[0], p[1] + q[1])


def sub(p, q):
    return (p[0] - q[0], p[1] - q[1])


def mul(p, q):
    return (p[0] * q[0] - p[1] * q[1], p[0] * q[1] + p[1] * q[0])


def quarter(p, sign):
    return (-p[1], p[0]) if sign > 0 else (p[1], -p[0])


def dft8(x, sign):
    half = math.sqrt(0.5)

    def four(a, b, c, d):
        e0, e1 = add(a, c), sub(a, c)
        o0, o1 = add(b, d), quarter(sub(b, d), sign)
        return add(e0, o0), add(e1, o1), sub(e0, o0), sub(e1, o1)

    e = four(x[0], x[2], x[4], x[6])
    o = four(x[1], x[3], x[5], x[7])
    u1 = quarter(o[1], sign)
    u3 = quarter(o[3], sign)
    o1 = ((o[1][0] + u1[0]) * half, (o[1][1] + u1[1]) * half)
    o2 = quarter(o[2], sign)
    o3 = ((u3[0] - o[3][0]) * half, (u3[1] - o[3][1]) * half)
    o = (o[0], o1, o2, o3)
    return [add(e[i], o[i]) for i in range(4)] + [sub(e[i], o[i]) for i in range(4)]


def cos_sin(theta):
    u = theta * theta
    s = SIN_COEFS[-1]
    for coef in SIN_COEFS[-2::-1]:
        s = s * u + coef
    c = COS_COEFS[-1]
    for coef in COS_COEFS[-2::-1]:
        c = c * u + coef
    return c, s * theta


def cross_range(rows, load, store, inner_ref, phase_ref, fourier_ref, work, mid, between=None):
    def twist(index, sign):
        return [None] + [(inner_ref[index, k], sign * inner_ref[index, 8 + k]) for k in range(1, 8)]

    def forward_one(a2, carry):
        out = dft8([load(a1, a2) for a1 in range(8)], -1)
        factors = twist(a2, 1.0)
        for k in range(8):
            value = out[k] if k == 0 else mul(out[k], factors[k])
            for p in range(2):
                work[a2 * 8 + k, p, pl.ds(0, rows), :] = value[p]
        return carry

    lax.fori_loop(0, 8, forward_one, 0)

    def forward_two(k, carry):
        values = [tuple(work[a2 * 8 + k, p, pl.ds(0, rows), :] for p in range(2)) for a2 in range(8)]
        out = dft8(values, -1)
        for kk in range(8):
            k1 = k + 8 * kk
            value = mul(out[kk], (phase_ref[0, k1], phase_ref[1, k1]))
            for p in range(2):
                mid[k1, pl.ds(0, rows), pl.ds(128 * p, 128)] = value[p]
        return carry

    lax.fori_loop(0, 8, forward_two, 0)
    if between is not None:
        between()

    def inner(i, carry):
        part = pl.ds(i * 16, 16)
        y = mid[part, pl.ds(0, rows), :].reshape(16 * rows, 256).astype(BF16)
        y = jnp.dot(y, fourier_ref[0], preferred_element_type=F32).reshape(16, rows, 256)
        y = mul((y[:, :, :128], y[:, :, 128:]), (phase_ref[2, part], phase_ref[3, part]))
        y = jnp.concatenate(y, axis=2).reshape(16 * rows, 256).astype(BF16)
        y = jnp.dot(y, fourier_ref[1], preferred_element_type=F32).reshape(16, rows, 256)
        y = mul((y[:, :, :128], y[:, :, 128:]), (phase_ref[0, part], -phase_ref[1, part]))
        for p in range(2):
            work[part, p, pl.ds(0, rows), :] = y[p]
        return carry

    lax.fori_loop(0, 4, inner, 0)

    def backward_one(k2, carry):
        values = [tuple(work[8 * q + k2, p, pl.ds(0, rows), :] for p in range(2)) for q in range(8)]
        out = dft8(values, 1)
        factors = twist(k2, -1.0)
        for a in range(8):
            value = out[a] if a == 0 else mul(out[a], factors[a])
            for p in range(2):
                mid[k2 * 8 + a, pl.ds(0, rows), pl.ds(128 * p, 128)] = value[p]
        return carry

    lax.fori_loop(0, 8, backward_one, 0)

    def backward_two(a, carry):
        values = [
            tuple(mid[k2 * 8 + a, pl.ds(0, rows), pl.ds(128 * p, 128)] for p in range(2)) for k2 in range(8)
        ]
        out = dft8(values, 1)
        for aa in range(8):
            store(a + 8 * aa, (out[aa][0] * (1.0 / NY), out[aa][1] * (1.0 / NY)))
        return carry

    lax.fori_loop(0, 8, backward_two, 0)


def clear_ends(values):
    zeros = jnp.zeros((2, 8, 128), F32)
    values[:, pl.ds(0, 8), :] = zeros
    values[:, pl.ds(NZ + 8, 8), :] = zeros


def right_side(values, edge_lhs, rhs, edge):
    def step(k, carry):
        pairs = []
        for p in range(2):
            centre = values[p, pl.ds(pl.multiple_of(k * BLK + 8, 8), BLK), :]
            above = values[p, pl.ds(k * BLK + 7, BLK), :]
            below = values[p, pl.ds(k * BLK + 9, BLK), :]
            pairs.append((centre, above + below - 2.0 * centre))
        (c_real, d_real), (c_imag, d_imag) = pairs
        r_real = c_real + ALPHA_REAL * d_real - ALPHA_IMAG * d_imag
        r_imag = c_imag + ALPHA_REAL * d_imag + ALPHA_IMAG * d_real
        rhs[k, pl.ds(0, BLK), :] = r_real
        rhs[k, pl.ds(BLK, BLK), :] = r_imag
        both = jnp.concatenate([r_real.astype(BF16), r_imag.astype(BF16)], axis=0)
        edge[k] = jnp.dot(edge_lhs[k], both, preferred_element_type=F32)
        return carry

    lax.fori_loop(0, NBLK, step, 0, unroll=16)


def recur(edge, corner, rhs):
    couple = (COUPLE_REAL, COUPLE_IMAG)

    def entry(k, i):
        return tuple(corner[k, pl.ds(2 * i + p, 1), :] for p in range(2))

    def row_of(k, i):
        return tuple(edge[k, pl.ds(i + p, 1), :] for p in range(2))

    starts = []
    held = None
    for k in range(NBLK):
        first, last = row_of(k, 0), row_of(k, 2)
        if held is not None:
            scaled = mul(held, couple)
            for p in range(2):
                rhs[k, pl.ds(BLK * p, 1), :] -= scaled[p]
            first = sub(first, mul(scaled, entry(k, 0)))
            last = sub(last, mul(scaled, entry(k, 1)))
        starts.append(first)
        held = last
    held = None
    for k in range(NBLK - 1, -1, -1):
        value = starts[k]
        if held is not None:
            scaled = mul(held, couple)
            for p in range(2):
                rhs[k, pl.ds(BLK * p + BLK - 1, 1), :] -= scaled[p]
            value = sub(value, mul(scaled, entry(k, 2)))
        held = value


def finish(matrix, rhs, store, begin, count):
    def step(i, carry):
        k = begin + i
        result = jnp.dot(matrix[k], rhs[k].astype(BF16), preferred_element_type=F32).astype(BF16)
        here = pl.ds(pl.multiple_of(k * BLK, BLK), BLK)
        for p in range(2):
            store(p, here, result[128 * p : 128 * p + 128])
        return carry

    lax.fori_loop(0, count, step, 0, unroll=8)


def exchange_kernel(
    tangent_hbm,
    base_hbm,
    theta_hbm,
    eof_hbm,
    mode_hbm,
    factor_hbm,
    inner_hbm,
    phase_hbm,
    fourier_hbm,
    t_next,
    b_next,
    t_late,
    values,
    matrix,
    edge_lhs,
    corner,
    done,
    tangent,
    base,
    theta,
    eof,
    mode,
    factor_in,
    inner_ref,
    phase_ref,
    fourier_ref,
    quarter_out,
    quarter_in,
    work,
    mid,
    t_send,
    b_send,
    rows32,
    factors,
    profile,
    t_early,
    b_all,
    g_all,
    p_all,
    p_wide,
    spread32,
    blocks,
    b_values,
    rhs,
    edge,
    load_sem,
    own_sem,
    q_sem,
    t_sem,
    b_sem,
    far_sem,
    bg_sem,
    g_sem,
    p_sem,
    round_sem,
    done_sem,
):
    g = lax.axis_index("grp")
    s = lax.axis_index("slab")
    zh, x, y = s // 16, (s // 4) % 4, s % 4
    core = g % 2

    def at_slab(dz, dx, dy):
        return (g, ((zh + dz) % 4) * 16 + ((x + dx) % 4) * 4 + (y + dy) % 4)

    def partner(i):
        return at_slab(i % 4, (i // 4) % 4, i // 16)

    def in_grp(i):
        mate = g + 1 - 2 * (g % 2) if i % 2 else g
        return (mate + 2) % 4 if i // 2 else mate

    core_mate = in_grp(1)
    far_mate = in_grp(2)
    lines = [[at_slab(i, 0, 0) for i in (1, 2, 3)], [at_slab(0, i, 0) for i in (1, 2, 3)], [at_slab(0, 0, i) for i in (1, 2, 3)]]
    grp_line = [(in_grp(i), s) for i in (1, 2, 3)]

    barrier = pltpu.get_barrier_semaphore()
    for target in lines[0] + lines[1] + lines[2] + grp_line:
        pl.semaphore_signal(barrier, inc=1, device_id=target, device_id_type=MESH)

    pairs = [
        (theta_hbm, theta),
        (base_hbm, base),
        (factor_hbm, factor_in),
        (eof_hbm, eof),
        (mode_hbm, mode),
        (tangent_hbm.at[0], tangent),
        (inner_hbm, inner_ref),
        (phase_hbm, phase_ref),
        (fourier_hbm, fourier_ref),
    ]
    loads = [pltpu.make_async_copy(src, dst, load_sem.at[i]) for i, (src, dst) in enumerate(pairs)]
    for copy in loads:
        copy.start()

    def put(src, dst, sems, target):
        return pltpu.make_async_remote_copy(
            src_ref=src, dst_ref=dst, send_sem=sems.at[0], recv_sem=sems.at[1], device_id=target, device_id_type=MESH
        )

    def signal_round(i):
        for target in lines[i + 1]:
            pl.semaphore_signal(round_sem.at[i], inc=1, device_id=target, device_id_type=MESH)

    for copy in loads[:5]:
        copy.wait()

    def screen(a, carry):
        cells = pl.ds(pl.multiple_of(a * 128, 128), 128)
        there = pl.ds(pl.multiple_of(g * 2048 + a * 128, 128), 128)
        turn = cos_sin(theta[:, there].astype(F32))
        value = mul((base[0, :, cells].astype(F32), base[1, :, cells].astype(F32)), turn)
        for part in range(4):
            depth = slice(8 * part, 8 * part + 8)
            quarter_out[part, a] = jnp.concatenate([value[0][depth], value[1][depth]], axis=0).astype(BF16)
        return carry

    lax.fori_loop(0, 16, screen, 0)

    for k in range(NBLK):
        for p in range(2):
            rows32[pl.ds(4 * k + 2 * p, 2), :] = factor_in[k, p].astype(F32)
    factors[...] = rows32[pl.ds(pl.multiple_of(core * 32, 32), 32), :].astype(BF16)
    chosen = lax.broadcasted_iota(jnp.int32, eof.shape, 1) == mode[0]
    column = jnp.sum(jnp.where(chosen, eof[...], 0.0), axis=1, keepdims=True)
    diagonal = lax.broadcasted_iota(jnp.int32, (ROWS, 128), 0) == lax.broadcasted_iota(jnp.int32, (ROWS, 128), 1)
    profile[...] = jnp.sum(jnp.where(diagonal, column, 0.0), axis=0, keepdims=True)

    for copy in loads[5:]:
        copy.wait()

    def load_tangent(c, a1, a2):
        depth = pl.ds(c * CH, CH)
        cells = pl.ds(pl.multiple_of((8 * a1 + a2) * 128, 128), 128)
        turn = cos_sin(theta[depth, cells].astype(F32))
        return mul((tangent[0, depth, cells].astype(F32), tangent[1, depth, cells].astype(F32)), turn)

    def store_tangent(c, a, value):
        for p in range(2):
            t_send[c, a, p] = value[p].astype(BF16)

    g_own, p_own = g_all.at[core, zh, x, y], p_all.at[zh, x, y]
    gx, px = g_all.at[core, :, x, y], p_all.at[:, x, y]
    gy, py = g_all.at[core, :, :, y], p_all.at[:, :, y]
    stages = [((factors, g_own), (profile, p_own)), ((gx, gx), (px, px)), ((gy, gy), (py, py))]
    g_half = put(g_all.at[core], g_all.at[core], g_sem.at[3], (core_mate, s))

    def gather_start(stage):
        for target in lines[stage]:
            for (src, dst), sem in zip(stages[stage], (g_sem, p_sem)):
                put(src, dst, sem.at[stage], target).start()

    def gather_wait(stage):
        for ref, sem in ((g_all.at[core], g_sem), (p_all, p_sem)):
            if stage == 0:
                part = ref.at[pl.ds(0, 3), 0, 0]
            elif stage == 1:
                part = ref.at[:, pl.ds(0, 3), 0]
            else:
                part = ref.at[:, :, pl.ds(0, 3)]
            put(part, part, sem.at[stage], lines[stage][0]).wait()

    t_land = [t_early, t_late]

    def t_move(c, i):
        target = partner(i)
        return put(t_send.at[c, target[1]], t_land[c].at[s], t_sem.at[c], target)

    def b_move(i):
        target = partner(i)
        return put(b_send.at[target[1]], b_all.at[g, s], b_sem, target)

    def far_move(i):
        cells = partner(i)[1]
        return put(b_send.at[cells], b_all.at[g, s], far_sem, (far_mate, cells))

    def start_all(move):
        def step(i, carry):
            move(i).start()
            return carry

        lax.fori_loop(1, SLAB, step, 0)

    def own(src, dst, i):
        return pltpu.make_async_copy(src, dst, own_sem.at[i])

    own_t = [own(t_send.at[c, s], t_land[c].at[s], c) for c in range(2)]
    own_b = own(b_send.at[s], b_all.at[g, s], 2)
    own_g = own(factors, g_own, 3)
    own_p = own(profile, p_own, 4)
    own_q = own(quarter_out.at[g], quarter_in.at[g], 5)

    tabs = (inner_ref, phase_ref, fourier_ref, work, mid)
    most = pl.ds(0, SLAB - 1)

    pl.semaphore_wait(barrier, 12)
    signal_round(0)
    for i in (1, 2, 3):
        put(quarter_out.at[in_grp(i)], quarter_in.at[g], q_sem, (in_grp(i), s)).start()
    own_q.start()
    gather_start(0)
    own_g.start()
    own_p.start()

    def second_round():
        pl.semaphore_wait(round_sem.at[0], 3)
        signal_round(1)

    cross_range(
        CH, functools.partial(load_tangent, 0), functools.partial(store_tangent, 0), *tabs, between=second_round
    )
    pl.semaphore_wait(round_sem.at[1], 3)
    pl.semaphore_signal(round_sem.at[2], inc=1, device_id=(far_mate, s), device_id_type=MESH)
    start_all(functools.partial(t_move, 0))
    own_t[0].start()
    own_g.wait()
    own_p.wait()
    gather_wait(0)
    gather_start(1)

    own_q.wait()
    put(quarter_out.at[pl.ds(0, 3)], quarter_in.at[pl.ds(0, 3)], q_sem, (core_mate, s)).wait()

    def load_base(a1, a2):
        tile = quarter_in[a1 // 2, 8 * (a1 % 2) + a2].astype(F32)
        return (tile[:8], tile[8:])

    def store_base(a, value):
        b_send[a] = jnp.concatenate(value, axis=0).astype(BF16)

    cross_range(8, load_base, store_base, *tabs)
    pl.semaphore_wait(round_sem.at[2], 1)

    def both_ways(i, carry):
        far_move(i).start()
        b_move(i).start()
        return carry

    far_move(0).start()
    lax.fori_loop(1, SLAB, both_ways, 0)
    own_b.start()
    cross_range(CH, functools.partial(load_tangent, 1), functools.partial(store_tangent, 1), *tabs)
    gather_wait(1)
    gather_start(2)
    early = put(t_send.at[0, most], t_early.at[most], t_sem.at[0], (core_mate, s))
    early.wait_send()
    start_all(functools.partial(t_move, 1))
    own_t[1].start()

    clear_ends(values)
    clear_ends(b_values)
    gather_wait(2)
    g_half.start()

    def widen_profile(i, carry):
        column = jnp.sum(jnp.where(diagonal, p_all[i // 16, (i // 4) % 4, i % 4], 0.0), axis=1, keepdims=True)
        p_wide[pl.ds(pl.multiple_of(i * ROWS, ROWS), ROWS), :] = jnp.broadcast_to(column, (ROWS, 128))
        return carry

    lax.fori_loop(0, SLAB, widen_profile, 0)
    g_half.wait()

    def widen(i, carry):
        for h in range(2):
            rows = pl.ds(pl.multiple_of(h * 2048 + i * 32, 32), 32)
            spread32[rows, :] = g_all[h, i // 16, (i // 4) % 4, i % 4].astype(F32)
        return carry

    lax.fori_loop(0, SLAB, widen, 0)

    def arrange(k, carry):
        start = (k // 8) * 2048 + (k % 8) * 4
        for p in range(2):
            for r in range(2):
                blocks[p, pl.ds(r, 64, stride=2), :] = spread32[pl.ds(start + 2 * p + r, 64, stride=32), :]
        real = blocks[0]
        imag = blocks[1]
        upper = jnp.concatenate([real, -imag], axis=1)
        lower = jnp.concatenate([imag, real], axis=1)
        matrix[k, pl.ds(0, 128), :] = upper.astype(BF16)
        matrix[k, pl.ds(128, 128), :] = lower.astype(BF16)
        ends = []
        for row in (0, BLK - 1):
            ends += [upper[row : row + 1], lower[row : row + 1]]
        edge_lhs[k] = jnp.concatenate(ends + ends, axis=0).astype(BF16)
        points = []
        for row, col in ((0, 0), (BLK - 1, 0), (0, BLK - 1), (0, BLK - 1)):
            for p in range(2):
                points.append(jnp.broadcast_to(blocks[p, pl.ds(row, 1), pl.ds(col, 1)], (1, 128)))
        corner[k] = jnp.concatenate(points, axis=0)
        return carry

    lax.fori_loop(0, NBLK, arrange, 0)

    own_b.wait()
    mine, theirs = b_all.at[g], b_all.at[far_mate]
    put(b_send.at[most], b_all.at[0, most], b_sem, (core_mate, s)).wait()
    to_core = put(mine, mine, bg_sem.at[0], (core_mate, s))
    to_core.start()
    put(b_send, theirs, far_sem, (far_mate, s)).wait()
    onward = put(theirs, theirs, bg_sem.at[1], (core_mate, s))
    onward.start()
    own_t[0].wait()
    early.wait_recv()
    to_core.wait()
    onward.wait()

    def combine(i, carry):
        for c in range(2):
            if c == 0:
                t_real = t_early[i, 0].astype(F32)
                t_imag = t_early[i, 1].astype(F32)
            for h in range(2):
                tile = b_all[2 * c + h, i].astype(F32)
                b_real, b_imag = tile[:8], tile[8:]
                at = CH * c + 8 * h
                scale = p_wide[pl.ds(pl.multiple_of(i * ROWS + at, 8), 8), :]
                here = pl.ds(pl.multiple_of(i * ROWS + at + 8, 8), 8)
                real = -scale * b_imag
                imag = scale * b_real
                if c == 0:
                    real += t_real[8 * h : 8 * h + 8]
                    imag += t_imag[8 * h : 8 * h + 8]
                values[0, here, :] = real
                values[1, here, :] = imag
                b_values[0, here, :] = b_real
                b_values[1, here, :] = b_imag
        return carry

    lax.fori_loop(0, SLAB, combine, 0, unroll=8)

    def store_done(f, p, here, result):
        done[f, p, here, :] = result

    outs = (t_next.at[0], b_next)

    def hand_out(f):
        def part(h):
            rows = pl.ds(h * (NZ // 2), NZ // 2)
            return pltpu.make_async_copy(done.at[f, :, rows], outs[f].at[:, rows], done_sem.at[2 * f + h])

        halves = [part(h) for h in range(2)]
        for h in range(2):
            finish(matrix, rhs, functools.partial(store_done, f), h * (NBLK // 2), NBLK // 2)
            halves[h].start()
        return halves

    right_side(b_values, edge_lhs, rhs, edge)
    recur(edge, corner, rhs)
    base_out = hand_out(1)

    own_t[1].wait()
    put(t_send.at[1, most], t_late.at[most], t_sem.at[1], (core_mate, s)).wait()

    def add_late(i, carry):
        for p in range(2):
            here = pl.ds(pl.multiple_of(i * ROWS + CH + 8, 8), CH)
            values[p, here, :] += t_late[i, p].astype(F32)
        return carry

    lax.fori_loop(0, SLAB, add_late, 0, unroll=16)
    right_side(values, edge_lhs, rhs, edge)
    recur(edge, corner, rhs)
    tangent_out = hand_out(0)
    for copy in base_out + tangent_out:
        copy.wait()


def copy_kernel(t_in, b_in, t_out, b_out, held, sem):
    arrivals = []
    leaves = []
    for f, (src, dst) in enumerate(((t_in.at[0], t_out.at[0]), (b_in, b_out))):
        for p in range(2):
            for h in range(2):
                rows = pl.ds(h * (NZ // 2), NZ // 2)
                i = 4 * f + 2 * p + h
                arrivals.append(pltpu.make_async_copy(src.at[p, rows], held.at[i], sem.at[0, i]))
                leaves.append(pltpu.make_async_copy(held.at[i], dst.at[p, rows], sem.at[1, i]))
    for copy in arrivals:
        copy.start()
    for arrival, leave in zip(arrivals, leaves):
        arrival.wait()
        leave.start()
    for leave in leaves:
        leave.wait()


def on_device(tangent, base, theta, eof_table, mode_of_field, block_factors):
    phases, fourier, inner = tables()
    in_hbm = pl.BlockSpec(memory_space=pltpu.HBM)
    anywhere = pl.BlockSpec(memory_space=ANY)
    smem = pltpu.SMEM
    dma = pltpu.SemaphoreType.DMA
    shape = jax.ShapeDtypeStruct
    results = (shape((1, 2, NZ, 128), BF16), shape((2, NZ, 128), BF16))
    handed = pl.pallas_call(
        exchange_kernel,
        out_shape=results,
        in_specs=[in_hbm] * 9,
        out_specs=(anywhere, anywhere),
        scratch_shapes=[
            VMEM((SLAB, 2, CH, 128), BF16),
            VMEM((2, NZ + 16, 128), F32),
            VMEM((NBLK, 256, 256), BF16),
            VMEM((NBLK, 8, 256), BF16),
            VMEM((NBLK, 8, 128), F32),
            VMEM((2, 2, NZ, 128), BF16),
            VMEM((2, ROWS, NY), BF16),
            VMEM((2, ROWS, NY // 4), BF16),
            VMEM((ROWS, NY), BF16),
            VMEM((ROWS, 112), F32),
            smem((1,), jnp.int32),
            VMEM((NBLK, 2, 2, 128), BF16),
            smem((8, 16), F32),
            VMEM((4, R1, 1, R2), F32),
            VMEM((2, 256, 256), BF16),
            VMEM((4, 16, 16, 128), BF16),
            VMEM((4, 16, 16, 128), BF16),
            VMEM((R1, 2, CH, 128), F32),
            VMEM((R1, CH, 256), F32),
            VMEM((2, SLAB, 2, CH, 128), BF16),
            VMEM((SLAB, 16, 128), BF16),
            VMEM((64, 128), F32),
            VMEM((32, 128), BF16),
            VMEM((1, 128), F32),
            VMEM((SLAB, 2, CH, 128), BF16),
            VMEM((GRP, SLAB, 16, 128), BF16),
            VMEM((2, 4, 4, 4, 32, 128), BF16),
            VMEM((4, 4, 4, 1, 128), F32),
            VMEM((NZ, 128), F32),
            VMEM((4096, 128), F32),
            VMEM((2, BLK, 128), F32),
            VMEM((2, NZ + 16, 128), F32),
            VMEM((NBLK, 256, 128), F32),
            VMEM((NBLK, 8, 128), F32),
            dma((9,)),
            dma((6,)),
            dma((2,)),
            dma((2, 2)),
            dma((2,)),
            dma((2,)),
            dma((2, 2)),
            dma((4, 2)),
            dma((3, 2)),
            pltpu.SemaphoreType.REGULAR((3,)),
            dma((4,)),
        ],
        compiler_params=pltpu.CompilerParams(
            collective_id=0, has_side_effects=True, vmem_limit_bytes=56 * 2**20
        ),
        name="exchange",
    )(
        tangent,
        base,
        theta,
        eof_table.T,
        mode_of_field,
        block_factors,
        jnp.asarray(inner),
        jnp.asarray(phases),
        jnp.asarray(fourier),
    )
    return pl.pallas_call(
        copy_kernel,
        out_shape=results,
        in_specs=[anywhere] * 2,
        out_specs=(anywhere, anywhere),
        scratch_shapes=[VMEM((8, NZ // 2, 128), BF16), dma((2, 8))],
        compiler_params=pltpu.CompilerParams(vmem_limit_bytes=56 * 2**20),
        name="hand_over",
    )(*handed)


def solution(mesh):
    in_specs = (
        P("grp", None, "slab", None),
        P(None, "slab", "grp"),
        P("slab", None),
        P(None, "slab"),
        P("grp"),
        P(None, None, "slab", None),
    )
    out_specs = (P("grp", None, None, "slab"), P(None, None, "slab"))
    return jax.shard_map(on_device, mesh=mesh, in_specs=in_specs, out_specs=out_specs, check_vma=False)
```

```python
import functools
import math

import jax
import jax.numpy as jnp
import ml_dtypes
import numpy as np
from jax import lax
from jax.experimental import pallas as pl
from jax.experimental.pallas import tpu as pltpu
from jax.sharding import PartitionSpec as P

MESH = pl.DeviceIdType.MESH
NZ = 2048
NY = 8192
R1 = 64
R2 = 128
NBLK = 16
BLK = 128
SLAB = 64
GRP = 4
ROWS = 32
CH = 16
ALPHA_REAL = 0.15
ALPHA_IMAG = 0.1
COUPLE_REAL = 0.35
COUPLE_IMAG = -0.25
VMEM = pltpu.VMEM
ANY = pl.ANY
F32 = jnp.float32
BF16 = jnp.bfloat16


def trig_coefficients():
    nodes = np.cos(np.pi * (np.arange(64) + 0.5) / 64)
    square = (nodes + 1.0) * 0.5 * math.pi**2
    root = np.sqrt(square)
    cheb = np.polynomial.chebyshev
    sine = cheb.cheb2poly(cheb.chebfit(nodes, np.sin(root) / root, 7))
    cosine = cheb.cheb2poly(cheb.chebfit(nodes, np.cos(root), 8))

    def in_square(coefs):
        total = np.zeros(1)
        shift = np.array([-1.0, 2.0 / math.pi**2])
        power = np.ones(1)
        for coef in coefs:
            total = np.polynomial.polynomial.polyadd(total, coef * power)
            power = np.polynomial.polynomial.polymul(power, shift)
        return [float(v) for v in total]

    return in_square(sine), in_square(cosine)


SIN_COEFS, COS_COEFS = trig_coefficients()


def tables():
    k1 = np.arange(R1)
    b = np.arange(R2)
    angle = -2.0 * np.pi * ((k1[:, None] * b[None, :]) % NY) / NY
    wave = k1[:, None] + R1 * b[None, :]
    signed = np.where(wave < NY // 2, wave, wave - NY)
    kernel_angle = -np.pi * ((signed * signed) % (2 * NY)) / NY
    phases = np.stack([np.cos(angle), np.sin(angle), np.cos(kernel_angle), np.sin(kernel_angle)])
    phases = phases.astype(np.float32).reshape(4, R1, 1, R2)
    turn = 2.0 * np.pi * ((b[:, None] * b[None, :]) % R2) / R2
    c = np.cos(turn).astype(ml_dtypes.bfloat16).astype(np.float32)
    s = np.sin(turn).astype(ml_dtypes.bfloat16).astype(np.float32)
    forward = np.block([[c, -s], [s, c]])
    backward = np.block([[c, s], [-s, c]])
    fourier = np.stack([forward, backward]).astype(ml_dtypes.bfloat16)
    eight = np.arange(8)
    inner = -2.0 * np.pi * (eight[:, None] * eight[None, :]) / 64.0
    inner = np.concatenate([np.cos(inner), np.sin(inner)], axis=1).astype(np.float32)
    return phases, fourier, inner


def add(p, q):
    return (p[0] + q[0], p[1] + q[1])


def sub(p, q):
    return (p[0] - q[0], p[1] - q[1])


def mul(p, q):
    return (p[0] * q[0] - p[1] * q[1], p[0] * q[1] + p[1] * q[0])


def quarter(p, sign):
    return (-p[1], p[0]) if sign > 0 else (p[1], -p[0])


def dft8(x, sign):
    half = math.sqrt(0.5)

    def four(a, b, c, d):
        e0, e1 = add(a, c), sub(a, c)
        o0, o1 = add(b, d), quarter(sub(b, d), sign)
        return add(e0, o0), add(e1, o1), sub(e0, o0), sub(e1, o1)

    e = four(x[0], x[2], x[4], x[6])
    o = four(x[1], x[3], x[5], x[7])
    u1 = quarter(o[1], sign)
    u3 = quarter(o[3], sign)
    o1 = ((o[1][0] + u1[0]) * half, (o[1][1] + u1[1]) * half)
    o2 = quarter(o[2], sign)
    o3 = ((u3[0] - o[3][0]) * half, (u3[1] - o[3][1]) * half)
    o = (o[0], o1, o2, o3)
    return [add(e[i], o[i]) for i in range(4)] + [sub(e[i], o[i]) for i in range(4)]


def cos_sin(theta):
    u = theta * theta
    s = SIN_COEFS[-1]
    for coef in SIN_COEFS[-2::-1]:
        s = s * u + coef
    c = COS_COEFS[-1]
    for coef in COS_COEFS[-2::-1]:
        c = c * u + coef
    return c, s * theta


def cross_range(rows, load, store, inner_ref, phase_ref, fourier_ref, work, mid, between=None):
    def twist(index, sign):
        return [None] + [(inner_ref[index, k], sign * inner_ref[index, 8 + k]) for k in range(1, 8)]

    def forward_one(a2, carry):
        out = dft8([load(a1, a2) for a1 in range(8)], -1)
        factors = twist(a2, 1.0)
        for k in range(8):
            value = out[k] if k == 0 else mul(out[k], factors[k])
            for p in range(2):
                work[a2 * 8 + k, p, pl.ds(0, rows), :] = value[p]
        return carry

    lax.fori_loop(0, 8, forward_one, 0)

    def forward_two(k, carry):
        values = [tuple(work[a2 * 8 + k, p, pl.ds(0, rows), :] for p in range(2)) for a2 in range(8)]
        out = dft8(values, -1)
        for kk in range(8):
            k1 = k + 8 * kk
            value = mul(out[kk], (phase_ref[0, k1], phase_ref[1, k1]))
            for p in range(2):
                mid[k1, pl.ds(0, rows), pl.ds(128 * p, 128)] = value[p]
        return carry

    lax.fori_loop(0, 8, forward_two, 0)
    if between is not None:
        between()

    def inner(i, carry):
        part = pl.ds(i * 16, 16)
        y = mid[part, pl.ds(0, rows), :].reshape(16 * rows, 256).astype(BF16)
        y = jnp.dot(y, fourier_ref[0], preferred_element_type=F32).reshape(16, rows, 256)
        y = mul((y[:, :, :128], y[:, :, 128:]), (phase_ref[2, part], phase_ref[3, part]))
        y = jnp.concatenate(y, axis=2).reshape(16 * rows, 256).astype(BF16)
        y = jnp.dot(y, fourier_ref[1], preferred_element_type=F32).reshape(16, rows, 256)
        y = mul((y[:, :, :128], y[:, :, 128:]), (phase_ref[0, part], -phase_ref[1, part]))
        for p in range(2):
            work[part, p, pl.ds(0, rows), :] = y[p]
        return carry

    lax.fori_loop(0, 4, inner, 0)

    def backward_one(k2, carry):
        values = [tuple(work[8 * q + k2, p, pl.ds(0, rows), :] for p in range(2)) for q in range(8)]
        out = dft8(values, 1)
        factors = twist(k2, -1.0)
        for a in range(8):
            value = out[a] if a == 0 else mul(out[a], factors[a])
            for p in range(2):
                mid[k2 * 8 + a, pl.ds(0, rows), pl.ds(128 * p, 128)] = value[p]
        return carry

    lax.fori_loop(0, 8, backward_one, 0)

    def backward_two(a, carry):
        values = [
            tuple(mid[k2 * 8 + a, pl.ds(0, rows), pl.ds(128 * p, 128)] for p in range(2)) for k2 in range(8)
        ]
        out = dft8(values, 1)
        for aa in range(8):
            store(a + 8 * aa, (out[aa][0] * (1.0 / NY), out[aa][1] * (1.0 / NY)))
        return carry

    lax.fori_loop(0, 8, backward_two, 0)


def clear_ends(values):
    zeros = jnp.zeros((2, 8, 128), F32)
    values[:, pl.ds(0, 8), :] = zeros
    values[:, pl.ds(NZ + 8, 8), :] = zeros


def right_side(values, edge_lhs, rhs, edge):
    def step(k, carry):
        pairs = []
        for p in range(2):
            centre = values[p, pl.ds(pl.multiple_of(k * BLK + 8, 8), BLK), :]
            above = values[p, pl.ds(k * BLK + 7, BLK), :]
            below = values[p, pl.ds(k * BLK + 9, BLK), :]
            pairs.append((centre, above + below - 2.0 * centre))
        (c_real, d_real), (c_imag, d_imag) = pairs
        r_real = c_real + ALPHA_REAL * d_real - ALPHA_IMAG * d_imag
        r_imag = c_imag + ALPHA_REAL * d_imag + ALPHA_IMAG * d_real
        rhs[k, pl.ds(0, BLK), :] = r_real
        rhs[k, pl.ds(BLK, BLK), :] = r_imag
        both = jnp.concatenate([r_real.astype(BF16), r_imag.astype(BF16)], axis=0)
        edge[k] = jnp.dot(edge_lhs[k], both, preferred_element_type=F32)
        return carry

    lax.fori_loop(0, NBLK, step, 0, unroll=16)


def recur(edge, corner, rhs):
    couple = (COUPLE_REAL, COUPLE_IMAG)

    def entry(k, i):
        return tuple(corner[k, pl.ds(2 * i + p, 1), :] for p in range(2))

    def row_of(k, i):
        return tuple(edge[k, pl.ds(i + p, 1), :] for p in range(2))

    starts = []
    held = None
    for k in range(NBLK):
        first, last = row_of(k, 0), row_of(k, 2)
        if held is not None:
            scaled = mul(held, couple)
            for p in range(2):
                rhs[k, pl.ds(BLK * p, 1), :] -= scaled[p]
            first = sub(first, mul(scaled, entry(k, 0)))
            last = sub(last, mul(scaled, entry(k, 1)))
        starts.append(first)
        held = last
    held = None
    for k in range(NBLK - 1, -1, -1):
        value = starts[k]
        if held is not None:
            scaled = mul(held, couple)
            for p in range(2):
                rhs[k, pl.ds(BLK * p + BLK - 1, 1), :] -= scaled[p]
            value = sub(value, mul(scaled, entry(k, 2)))
        held = value


def finish(matrix, rhs, store, begin, count):
    def step(i, carry):
        k = begin + i
        result = jnp.dot(matrix[k], rhs[k].astype(BF16), preferred_element_type=F32).astype(BF16)
        here = pl.ds(pl.multiple_of(k * BLK, BLK), BLK)
        for p in range(2):
            store(p, here, result[128 * p : 128 * p + 128])
        return carry

    lax.fori_loop(0, count, step, 0, unroll=8)


def exchange_kernel(
    tangent_hbm,
    base_hbm,
    theta_hbm,
    eof_hbm,
    mode_hbm,
    factor_hbm,
    inner_hbm,
    phase_hbm,
    fourier_hbm,
    t_next,
    b_next,
    t_late,
    values,
    matrix,
    edge_lhs,
    corner,
    done,
    tangent,
    base,
    theta,
    eof,
    mode,
    factor_in,
    inner_ref,
    phase_ref,
    fourier_ref,
    quarter_out,
    quarter_in,
    work,
    mid,
    t_send,
    b_send,
    rows32,
    factors,
    profile,
    t_early,
    b_all,
    g_all,
    p_all,
    p_wide,
    spread32,
    blocks,
    b_values,
    rhs,
    edge,
    load_sem,
    own_sem,
    q_sem,
    t_sem,
    b_sem,
    far_sem,
    bg_sem,
    g_sem,
    p_sem,
    round_sem,
    done_sem,
):
    g = lax.axis_index("grp")
    s = lax.axis_index("slab")
    zh, x, y = s // 16, (s // 4) % 4, s % 4
    core = g % 2

    def at_slab(dz, dx, dy):
        return (g, ((zh + dz) % 4) * 16 + ((x + dx) % 4) * 4 + (y + dy) % 4)

    def partner(i):
        return at_slab(i % 4, (i // 4) % 4, i // 16)

    def in_grp(i):
        mate = g + 1 - 2 * (g % 2) if i % 2 else g
        return (mate + 2) % 4 if i // 2 else mate

    core_mate = in_grp(1)
    far_mate = in_grp(2)
    lines = [[at_slab(i, 0, 0) for i in (1, 2, 3)], [at_slab(0, i, 0) for i in (1, 2, 3)], [at_slab(0, 0, i) for i in (1, 2, 3)]]
    grp_line = [(in_grp(i), s) for i in (1, 2, 3)]

    barrier = pltpu.get_barrier_semaphore()
    for target in lines[0] + lines[1] + lines[2] + grp_line:
        pl.semaphore_signal(barrier, inc=1, device_id=target, device_id_type=MESH)

    pairs = [
        (theta_hbm, theta),
        (base_hbm, base),
        (factor_hbm, factor_in),
        (eof_hbm, eof),
        (mode_hbm, mode),
        (tangent_hbm.at[0], tangent),
        (inner_hbm, inner_ref),
        (phase_hbm, phase_ref),
        (fourier_hbm, fourier_ref),
    ]
    loads = [pltpu.make_async_copy(src, dst, load_sem.at[i]) for i, (src, dst) in enumerate(pairs)]
    for copy in loads:
        copy.start()

    def put(src, dst, sems, target):
        return pltpu.make_async_remote_copy(
            src_ref=src, dst_ref=dst, send_sem=sems.at[0], recv_sem=sems.at[1], device_id=target, device_id_type=MESH
        )

    def signal_round(i):
        for target in lines[i + 1]:
            pl.semaphore_signal(round_sem.at[i], inc=1, device_id=target, device_id_type=MESH)

    for copy in loads[:5]:
        copy.wait()

    def screen(a, carry):
        cells = pl.ds(pl.multiple_of(a * 128, 128), 128)
        there = pl.ds(pl.multiple_of(g * 2048 + a * 128, 128), 128)
        turn = cos_sin(theta[:, there].astype(F32))
        value = mul((base[0, :, cells].astype(F32), base[1, :, cells].astype(F32)), turn)
        for part in range(4):
            depth = slice(8 * part, 8 * part + 8)
            quarter_out[part, a] = jnp.concatenate([value[0][depth], value[1][depth]], axis=0).astype(BF16)
        return carry

    lax.fori_loop(0, 16, screen, 0)

    for k in range(NBLK):
        for p in range(2):
            rows32[pl.ds(4 * k + 2 * p, 2), :] = factor_in[k, p].astype(F32)
    factors[...] = rows32[pl.ds(pl.multiple_of(core * 32, 32), 32), :].astype(BF16)
    chosen = lax.broadcasted_iota(jnp.int32, eof.shape, 1) == mode[0]
    column = jnp.sum(jnp.where(chosen, eof[...], 0.0), axis=1, keepdims=True)
    diagonal = lax.broadcasted_iota(jnp.int32, (ROWS, 128), 0) == lax.broadcasted_iota(jnp.int32, (ROWS, 128), 1)
    profile[...] = jnp.sum(jnp.where(diagonal, column, 0.0), axis=0, keepdims=True)

    for copy in loads[5:]:
        copy.wait()

    def load_tangent(c, a1, a2):
        depth = pl.ds(c * CH, CH)
        cells = pl.ds(pl.multiple_of((8 * a1 + a2) * 128, 128), 128)
        turn = cos_sin(theta[depth, cells].astype(F32))
        return mul((tangent[0, depth, cells].astype(F32), tangent[1, depth, cells].astype(F32)), turn)

    def store_tangent(c, a, value):
        for p in range(2):
            t_send[c, a, p] = value[p].astype(BF16)

    g_own, p_own = g_all.at[core, zh, x, y], p_all.at[zh, x, y]
    gx, px = g_all.at[core, :, x, y], p_all.at[:, x, y]
    gy, py = g_all.at[core, :, :, y], p_all.at[:, :, y]
    stages = [((factors, g_own), (profile, p_own)), ((gx, gx), (px, px)), ((gy, gy), (py, py))]
    g_half = put(g_all.at[core], g_all.at[core], g_sem.at[3], (core_mate, s))

    def gather_start(stage):
        for target in lines[stage]:
            for (src, dst), sem in zip(stages[stage], (g_sem, p_sem)):
                put(src, dst, sem.at[stage], target).start()

    def gather_wait(stage):
        for ref, sem in ((g_all.at[core], g_sem), (p_all, p_sem)):
            if stage == 0:
                part = ref.at[pl.ds(0, 3), 0, 0]
            elif stage == 1:
                part = ref.at[:, pl.ds(0, 3), 0]
            else:
                part = ref.at[:, :, pl.ds(0, 3)]
            put(part, part, sem.at[stage], lines[stage][0]).wait()

    t_land = [t_early, t_late]

    def t_move(c, i):
        target = partner(i)
        return put(t_send.at[c, target[1]], t_land[c].at[s], t_sem.at[c], target)

    def b_move(i):
        target = partner(i)
        return put(b_send.at[target[1]], b_all.at[g, s], b_sem, target)

    def far_move(i):
        cells = partner(i)[1]
        return put(b_send.at[cells], b_all.at[g, s], far_sem, (far_mate, cells))

    def start_all(move):
        def step(i, carry):
            move(i).start()
            return carry

        lax.fori_loop(1, SLAB, step, 0)

    def own(src, dst, i):
        return pltpu.make_async_copy(src, dst, own_sem.at[i])

    own_t = [own(t_send.at[c, s], t_land[c].at[s], c) for c in range(2)]
    own_b = own(b_send.at[s], b_all.at[g, s], 2)
    own_g = own(factors, g_own, 3)
    own_p = own(profile, p_own, 4)
    own_q = own(quarter_out.at[g], quarter_in.at[g], 5)

    tabs = (inner_ref, phase_ref, fourier_ref, work, mid)
    most = pl.ds(0, SLAB - 1)

    pl.semaphore_wait(barrier, 12)
    signal_round(0)
    for i in (1, 2, 3):
        put(quarter_out.at[in_grp(i)], quarter_in.at[g], q_sem, (in_grp(i), s)).start()
    own_q.start()
    gather_start(0)
    own_g.start()
    own_p.start()

    def second_round():
        pl.semaphore_wait(round_sem.at[0], 3)
        signal_round(1)

    cross_range(
        CH, functools.partial(load_tangent, 0), functools.partial(store_tangent, 0), *tabs, between=second_round
    )
    pl.semaphore_wait(round_sem.at[1], 3)
    pl.semaphore_signal(round_sem.at[2], inc=1, device_id=(far_mate, s), device_id_type=MESH)
    start_all(functools.partial(t_move, 0))
    own_t[0].start()
    own_g.wait()
    own_p.wait()
    gather_wait(0)
    gather_start(1)

    own_q.wait()
    put(quarter_out.at[pl.ds(0, 3)], quarter_in.at[pl.ds(0, 3)], q_sem, (core_mate, s)).wait()

    def load_base(a1, a2):
        tile = quarter_in[a1 // 2, 8 * (a1 % 2) + a2].astype(F32)
        return (tile[:8], tile[8:])

    def store_base(a, value):
        b_send[a] = jnp.concatenate(value, axis=0).astype(BF16)

    cross_range(8, load_base, store_base, *tabs)
    pl.semaphore_wait(round_sem.at[2], 1)

    def both_ways(i, carry):
        far_move(i).start()
        b_move(i).start()
        return carry

    far_move(0).start()
    lax.fori_loop(1, SLAB, both_ways, 0)
    own_b.start()
    cross_range(CH, functools.partial(load_tangent, 1), functools.partial(store_tangent, 1), *tabs)
    gather_wait(1)
    gather_start(2)
    early = put(t_send.at[0, most], t_early.at[most], t_sem.at[0], (core_mate, s))
    early.wait_send()
    start_all(functools.partial(t_move, 1))
    own_t[1].start()

    clear_ends(values)
    clear_ends(b_values)
    gather_wait(2)
    g_half.start()

    def widen_profile(i, carry):
        column = jnp.sum(jnp.where(diagonal, p_all[i // 16, (i // 4) % 4, i % 4], 0.0), axis=1, keepdims=True)
        p_wide[pl.ds(pl.multiple_of(i * ROWS, ROWS), ROWS), :] = jnp.broadcast_to(column, (ROWS, 128))
        return carry

    lax.fori_loop(0, SLAB, widen_profile, 0, unroll=4)
    g_half.wait()

    def widen(i, carry):
        for h in range(2):
            rows = pl.ds(pl.multiple_of(h * 2048 + i * 32, 32), 32)
            spread32[rows, :] = g_all[h, i // 16, (i // 4) % 4, i % 4].astype(F32)
        return carry

    lax.fori_loop(0, SLAB, widen, 0)

    def arrange(k, carry):
        start = (k // 8) * 2048 + (k % 8) * 4
        for p in range(2):
            for r in range(2):
                blocks[p, pl.ds(r, 64, stride=2), :] = spread32[pl.ds(start + 2 * p + r, 64, stride=32), :]
        real = blocks[0]
        imag = blocks[1]
        upper = jnp.concatenate([real, -imag], axis=1)
        lower = jnp.concatenate([imag, real], axis=1)
        matrix[k, pl.ds(0, 128), :] = upper.astype(BF16)
        matrix[k, pl.ds(128, 128), :] = lower.astype(BF16)
        ends = []
        for row in (0, BLK - 1):
            ends += [upper[row : row + 1], lower[row : row + 1]]
        edge_lhs[k] = jnp.concatenate(ends + ends, axis=0).astype(BF16)
        points = []
        for row, col in ((0, 0), (BLK - 1, 0), (0, BLK - 1), (0, BLK - 1)):
            for p in range(2):
                points.append(jnp.broadcast_to(blocks[p, pl.ds(row, 1), pl.ds(col, 1)], (1, 128)))
        corner[k] = jnp.concatenate(points, axis=0)
        return carry

    lax.fori_loop(0, NBLK, arrange, 0)

    own_b.wait()
    mine, theirs = b_all.at[g], b_all.at[far_mate]
    put(b_send.at[most], b_all.at[0, most], b_sem, (core_mate, s)).wait()
    to_core = put(mine, mine, bg_sem.at[0], (core_mate, s))
    to_core.start()
    put(b_send, theirs, far_sem, (far_mate, s)).wait()
    onward = put(theirs, theirs, bg_sem.at[1], (core_mate, s))
    onward.start()
    own_t[0].wait()
    early.wait_recv()
    to_core.wait()
    onward.wait()

    def combine(i, carry):
        for c in range(2):
            if c == 0:
                t_real = t_early[i, 0].astype(F32)
                t_imag = t_early[i, 1].astype(F32)
            for h in range(2):
                tile = b_all[2 * c + h, i].astype(F32)
                b_real, b_imag = tile[:8], tile[8:]
                at = CH * c + 8 * h
                scale = p_wide[pl.ds(pl.multiple_of(i * ROWS + at, 8), 8), :]
                here = pl.ds(pl.multiple_of(i * ROWS + at + 8, 8), 8)
                real = -scale * b_imag
                imag = scale * b_real
                if c == 0:
                    real += t_real[8 * h : 8 * h + 8]
                    imag += t_imag[8 * h : 8 * h + 8]
                values[0, here, :] = real
                values[1, here, :] = imag
                b_values[0, here, :] = b_real
                b_values[1, here, :] = b_imag
        return carry

    lax.fori_loop(0, SLAB, combine, 0, unroll=8)

    def store_done(f, p, here, result):
        done[f, p, here, :] = result

    outs = (t_next.at[0], b_next)

    def hand_out(f):
        def part(h):
            rows = pl.ds(h * (NZ // 2), NZ // 2)
            return pltpu.make_async_copy(done.at[f, :, rows], outs[f].at[:, rows], done_sem.at[2 * f + h])

        halves = [part(h) for h in range(2)]
        for h in range(2):
            finish(matrix, rhs, functools.partial(store_done, f), h * (NBLK // 2), NBLK // 2)
            halves[h].start()
        return halves

    right_side(b_values, edge_lhs, rhs, edge)
    recur(edge, corner, rhs)
    base_out = hand_out(1)

    own_t[1].wait()
    put(t_send.at[1, most], t_late.at[most], t_sem.at[1], (core_mate, s)).wait()

    def add_late(i, carry):
        for p in range(2):
            here = pl.ds(pl.multiple_of(i * ROWS + CH + 8, 8), CH)
            values[p, here, :] += t_late[i, p].astype(F32)
        return carry

    lax.fori_loop(0, SLAB, add_late, 0, unroll=16)
    right_side(values, edge_lhs, rhs, edge)
    recur(edge, corner, rhs)
    tangent_out = hand_out(0)
    for copy in base_out + tangent_out:
        copy.wait()


def copy_kernel(t_in, b_in, t_out, b_out, held, sem):
    arrivals = []
    leaves = []
    for f, (src, dst) in enumerate(((t_in.at[0], t_out.at[0]), (b_in, b_out))):
        for p in range(2):
            for h in range(2):
                rows = pl.ds(h * (NZ // 2), NZ // 2)
                i = 4 * f + 2 * p + h
                arrivals.append(pltpu.make_async_copy(src.at[p, rows], held.at[i], sem.at[0, i]))
                leaves.append(pltpu.make_async_copy(held.at[i], dst.at[p, rows], sem.at[1, i]))
    for copy in arrivals:
        copy.start()
    for arrival, leave in zip(arrivals, leaves):
        arrival.wait()
        leave.start()
    for leave in leaves:
        leave.wait()


def on_device(tangent, base, theta, eof_table, mode_of_field, block_factors):
    phases, fourier, inner = tables()
    in_hbm = pl.BlockSpec(memory_space=pltpu.HBM)
    anywhere = pl.BlockSpec(memory_space=ANY)
    smem = pltpu.SMEM
    dma = pltpu.SemaphoreType.DMA
    shape = jax.ShapeDtypeStruct
    results = (shape((1, 2, NZ, 128), BF16), shape((2, NZ, 128), BF16))
    handed = pl.pallas_call(
        exchange_kernel,
        out_shape=results,
        in_specs=[in_hbm] * 9,
        out_specs=(anywhere, anywhere),
        scratch_shapes=[
            VMEM((SLAB, 2, CH, 128), BF16),
            VMEM((2, NZ + 16, 128), F32),
            VMEM((NBLK, 256, 256), BF16),
            VMEM((NBLK, 8, 256), BF16),
            VMEM((NBLK, 8, 128), F32),
            VMEM((2, 2, NZ, 128), BF16),
            VMEM((2, ROWS, NY), BF16),
            VMEM((2, ROWS, NY // 4), BF16),
            VMEM((ROWS, NY), BF16),
            VMEM((ROWS, 112), F32),
            smem((1,), jnp.int32),
            VMEM((NBLK, 2, 2, 128), BF16),
            smem((8, 16), F32),
            VMEM((4, R1, 1, R2), F32),
            VMEM((2, 256, 256), BF16),
            VMEM((4, 16, 16, 128), BF16),
            VMEM((4, 16, 16, 128), BF16),
            VMEM((R1, 2, CH, 128), F32),
            VMEM((R1, CH, 256), F32),
            VMEM((2, SLAB, 2, CH, 128), BF16),
            VMEM((SLAB, 16, 128), BF16),
            VMEM((72, 128), F32),
            VMEM((32, 128), BF16),
            VMEM((1, 128), F32),
            VMEM((SLAB, 2, CH, 128), BF16),
            VMEM((GRP, SLAB, 16, 128), BF16),
            VMEM((2, 4, 4, 4, 32, 128), BF16),
            VMEM((4, 4, 4, 1, 128), F32),
            VMEM((NZ, 128), F32),
            VMEM((4352, 128), F32),
            VMEM((3, BLK, 128), F32),
            VMEM((2, NZ + 16, 128), F32),
            VMEM((NBLK + 1, 256, 128), F32),
            VMEM((NBLK + 1, 8, 128), F32),
            dma((9,)),
            dma((6,)),
            dma((2,)),
            dma((2, 2)),
            dma((2,)),
            dma((2,)),
            dma((2, 2)),
            dma((4, 2)),
            dma((3, 2)),
            pltpu.SemaphoreType.REGULAR((3,)),
            dma((4,)),
        ],
        compiler_params=pltpu.CompilerParams(
            collective_id=0, has_side_effects=True, vmem_limit_bytes=56 * 2**20
        ),
        name="exchange",
    )(
        tangent,
        base,
        theta,
        eof_table.T,
        mode_of_field,
        block_factors,
        jnp.asarray(inner),
        jnp.asarray(phases),
        jnp.asarray(fourier),
    )
    return pl.pallas_call(
        copy_kernel,
        out_shape=results,
        in_specs=[anywhere] * 2,
        out_specs=(anywhere, anywhere),
        scratch_shapes=[VMEM((8, NZ // 2, 128), BF16), dma((2, 8))],
        compiler_params=pltpu.CompilerParams(vmem_limit_bytes=56 * 2**20),
        name="hand_over",
    )(*handed)


def solution(mesh):
    in_specs = (
        P("grp", None, "slab", None),
        P(None, "slab", "grp"),
        P("slab", None),
        P(None, "slab"),
        P("grp"),
        P(None, None, "slab", None),
    )
    out_specs = (P("grp", None, None, "slab"), P(None, None, "slab"))
    return jax.shard_map(on_device, mesh=mesh, in_specs=in_specs, out_specs=out_specs, check_vma=False)
```
